32 devices in a mesh: dp: 2 (over core), expert: 16 (over z, y, x).
Axes of the slice: x: 2, y: 2, z: 4, core: 2. Of those that a mesh axis runs over, the one named last changes fastest.
Arguments:
- tokens: bfloat16 [8192, 2048], P(('dp', 'expert')), may hold values from -6 to 6
- segments: int32 [32, 256], P(('dp', 'expert')), may hold values from 0 to 7, never falling along the last dimension, each value on 1 to 128 neighbouring positions
- expert_ids: int32 [8192, 8], P(('dp', 'expert')), may hold values from 0 to 15, all different within a row
- norm_gains: float32 [4, 2048], P(None, ('dp', 'expert')), may hold values from 0.1 to 1.9
- w_query: float32 [2048, 2048], P(('dp', 'expert')), may hold values from -0.125 to 0.125
- w_key: float32 [2048, 2048], P(('dp', 'expert')), may hold values from -0.125 to 0.125
- w_value: float32 [2048, 2048], P(('dp', 'expert')), may hold values from -0.125 to 0.125
- w_out: float32 [2048, 2048], P(('dp', 'expert')), may hold values from -1 to 1
- w_router: float32 [2048, 16], P(('dp', 'expert')), may hold values from -0.0625 to 0.0625
- expert_gate: bfloat16 [16, 2048, 1024], P('expert'), may hold values from -0.125 to 0.125
- expert_up: bfloat16 [16, 2048, 1024], P('expert'), may hold values from -0.125 to 0.125
- expert_down: bfloat16 [16, 1024, 2048], P('expert'), may hold values from -3 to 3
- cotangent: bfloat16 [8192, 2048], P(('dp', 'expert')), may hold values from -6 to 6
Outputs:
- mixed: bfloat16 [8192, 2048], P(('dp', 'expert'))
- grad_tokens: bfloat16 [8192, 2048], P(('dp', 'expert'))
- grad_norm_gains: float32 [4, 2048], P(None, ('dp', 'expert'))
- grad_w_query: float32 [2048, 2048], P(('dp', 'expert'))
- grad_w_key: float32 [2048, 2048], P(('dp', 'expert'))
- grad_w_value: float32 [2048, 2048], P(('dp', 'expert'))
- grad_w_out: float32 [2048, 2048], P(('dp', 'expert'))
- grad_w_router: float32 [2048, 16], P(('dp', 'expert'))
- grad_expert_gate: float32 [2, 16, 2048, 1024], P('dp', 'expert')
- grad_expert_up: float32 [2, 16, 2048, 1024], P('dp', 'expert')
- grad_expert_down: float32 [2, 16, 1024, 2048], P('dp', 'expert')
The draws below stay inside these ranges and needn't reach their ends.
Inputs may be any that keep to these rules, and one draw needn't show every extreme that they name: `expert_ids`: each row names 8 different experts. `segments`: document numbers never fall along a sequence.
All inputs are finite; a program needn't handle non-finite values.
Results may differ from the reference program's by a relative error of at most 0.018.
The reference program's roundings to bfloat16 on the way count: a program that leaves them out, or rounds other values in their place, can miss the bound.
Values may be sent and summed in bfloat16 or wider, within the bound.
No kernel may reach another device: no remote copies, remote signals or barrier semaphores. Data moves between devices by JAX's collectives and lax.ppermute only.
A program may use at most 256 MiB of HBM per device.

```python
import math
import jax
import jax.numpy as jnp
import numpy as np
from jax import lax

D = 2048
H = 16
HD = 128
FF = 1024
TOPK = 8
TOK_DEV = 256
EXPERTS = 16
CAP = 128
NSEQ = 32
TOKENS = 8192
N_DP = 2
N_EXPERT = 16


def block_levels(own_key, shape, cuts, low, top_value):
    def one(axis_at, parts):
        heights = jax.random.uniform(jax.random.fold_in(jax.random.fold_in(own_key, 6), axis_at), (parts,), jnp.float32, low / len(cuts), top_value / len(cuts))
        return jnp.repeat(jnp.exp(heights), shape[axis_at] // parts).reshape((-1,) + (1,) * (len(shape) - axis_at - 1))

    level = one(*cuts[0])
    for cut in cuts[1:]:
        level = level * one(*cut)
    return level


def choose_distinct(rng, rows, count, top, lift):
    sequence = jax.random.permutation(jax.random.fold_in(rng, 1), count)
    favour = sequence
    for power in range(3):
        favour = favour * favour // count
    favour = favour * lift // count
    lots = jax.random.randint(jax.random.fold_in(rng, 2), (rows, count), 0, 4096) + favour
    fixed_rows = jax.random.permutation(jax.random.fold_in(rng, 3), rows)[jnp.arange(count) % rows]
    lots = jnp.where(jnp.arange(rows)[:, None] == fixed_rows[None, :], 1 << 14, lots)
    priority = lots * count + jnp.arange(count)
    return lax.top_k(priority.astype(jnp.int32), top)[1].astype(jnp.int32)


def length_profile(amount, total, reach, skew):
    loads = [(1 << 20) // math.isqrt(grade ** skew) + 1 for grade in range(2, amount + 1)]
    spare, given = total - reach - (amount - 1), [1] * (amount - 1)
    while spare > 0:
        free = [i for i in range(amount - 1) if given[i] < reach]
        mass, remaining = sum([loads[i] for i in free]), spare
        for i in free:
            more = min(reach - given[i], max(1, remaining * loads[i] // mass), spare)
            given[i] = given[i] + more
            spare = spare - more
    return np.array([reach] + given)


def ragged(stream_key, count, total, most, slope):
    if count == 2:
        one = jax.random.randint(stream_key, (), max(1, total - most), min(most, total - 1) + 1)
        return jnp.stack([one, total - one])
    lengths = jnp.asarray(length_profile(count, total, most, slope), jnp.int32)
    twos = (count - 1) // 2
    donor, taker = lengths[1:1 + 2 * twos:2], lengths[2:2 + 2 * twos:2]
    margin = jnp.minimum(donor - 1, most - taker)
    shifted = jax.random.randint(jax.random.fold_in(stream_key, 1), (twos,), 0, 1 << 20) % (margin + 1)
    lengths = lengths.at[1:1 + 2 * twos:2].set(donor - shifted).at[2:2 + 2 * twos:2].set(taker + shifted)
    return lengths[jax.random.permutation(jax.random.fold_in(stream_key, 2), count)]


def normal_values(stream_key, extent, scale, most, cuts=(), held_as=jnp.bfloat16):
    drawn = jax.random.normal(stream_key, extent, jnp.float32) * scale
    if len(cuts) > 0:
        drawn = block_levels(stream_key, extent, cuts, -0.22, 0.18) * drawn
    return jnp.clip(drawn, min=-most, max=most).astype(held_as)


def setup_inputs(seed: int = 0) -> dict:
    streams_of = jax.random.split(jax.random.key(seed), 14)
    return {
        "tokens": normal_values(streams_of[0], (TOKENS, D), 1.0, 6.0, ((0, 32),)),
        "segments": jax.vmap(lambda own: jnp.searchsorted(jnp.cumsum(ragged(own, max(4, TOK_DEV // 32), TOK_DEV, TOK_DEV // 2, 2)), jnp.arange(TOK_DEV), side="right"))(jax.random.split(streams_of[1], NSEQ)).reshape((NSEQ, TOK_DEV)).astype(jnp.int32),
        "expert_ids": choose_distinct(streams_of[2], TOKENS, EXPERTS, TOPK, 4096),
        "norm_gains": jnp.clip(1.0 + 0.18 * jax.random.normal(streams_of[3], (4, D), jnp.float32), 0.1, 1.9),
        "w_query": normal_values(streams_of[4], (D, D), D ** -0.5, 0.125, ((0, 32),), jnp.float32),
        "w_key": normal_values(streams_of[5], (D, D), D ** -0.5, 0.125, ((0, 32),), jnp.float32),
        "w_value": normal_values(streams_of[6], (D, D), D ** -0.5, 0.125, ((0, 32),), jnp.float32),
        "w_out": normal_values(streams_of[7], (D, D), (max(1, D // 64)) ** -0.5, 1.0, ((0, 32),), jnp.float32),
        "w_router": normal_values(streams_of[8], (D, EXPERTS), (4 * D) ** -0.5, 0.0625, ((0, 32),), jnp.float32),
        "expert_gate": normal_values(streams_of[9], (EXPERTS, D, FF), D ** -0.5, 0.125, ((0, 16),)),
        "expert_up": normal_values(streams_of[10], (EXPERTS, D, FF), D ** -0.5, 0.125, ((0, 16),)),
        "expert_down": normal_values(streams_of[11], (EXPERTS, FF, D), (max(1, FF // 256)) ** -0.5, 3.0, ((0, 16),)),
        "cotangent": normal_values(streams_of[12], (TOKENS, D), 1.0, 6.0, ((0, 32),)),
    }


@jax.custom_vjp
def low(v):
    return lax.optimization_barrier(v.astype(jnp.bfloat16)).astype(jnp.float32)

@jax.custom_vjp
def low_back(v):
    return v

def low_keep(v):
    return (low(v), None)

def low_pass(kept, grad):
    return (grad,)

def back_keep(v):
    return (v, None)

def back_low(kept, grad):
    return (low(grad),)
low.defvjp(low_keep, low_pass)
low_back.defvjp(back_keep, back_low)
EPS = 1e-05
THETA = 10000.0
MASKED = -1e+30

def product(left, right):
    return jnp.dot(left, right, precision=lax.Precision.HIGHEST)

def rms_norm(value, gain):
    return value * lax.rsqrt(lax.optimization_barrier(jnp.mean(value * value, axis=-1, keepdims=True)) + EPS) * gain

def rope_tables(length, head):
    half = head // 2
    freq = THETA ** (-(jnp.arange(half, dtype=jnp.float32) * 2.0) / head)
    angle = jnp.arange(length, dtype=jnp.float32)[:, None] * freq[None, :]
    angle = jnp.concatenate([angle, angle], axis=-1)
    return (jnp.cos(angle)[:, None, :], jnp.sin(angle)[:, None, :])

def rotate(value, cosine, sine):
    half = value.shape[-1] // 2
    turned = jnp.concatenate([-value[..., half:], value[..., :half]], axis=-1)
    return value * cosine + turned * sine

def slot_table(block_ids):
    labels = jnp.arange(EXPERTS, dtype=jnp.int32)
    onehot = (block_ids[:, :, None] == labels[None, None, :]).astype(jnp.int32).reshape(-1, EXPERTS)
    before = (jnp.cumsum(onehot, axis=0).astype(jnp.int32) - onehot).astype(jnp.int32)
    position = lax.optimization_barrier(jnp.sum(before * onehot, axis=1)).astype(jnp.int32).reshape(block_ids.shape)
    return jnp.where(position < CAP, block_ids * CAP + position, -1).astype(jnp.int32)

def source_table(slot_index):
    slots = EXPERTS * CAP
    where_to = jnp.where(slot_index >= 0, slot_index, slots).reshape(-1).astype(jnp.int32)
    owner = jnp.broadcast_to(jnp.arange(TOK_DEV, dtype=jnp.int32)[:, None], slot_index.shape).reshape(-1)
    table = jnp.full((slots + 1,), TOK_DEV, jnp.int32).at[where_to].set(owner)
    return table[:slots]

def attend(packed):
    query, key_rows, value_rows, doc_ids = packed
    places = jnp.arange(TOK_DEV, dtype=jnp.int32)
    scores = jnp.einsum('gqhd,gkhd->ghqk', query, key_rows, precision=lax.Precision.HIGHEST) * HD ** (-0.5)
    scores = low_back(scores)
    visible = (doc_ids[:, :, None] == doc_ids[:, None, :]) & (places[:, None] >= places[None, :])[None]
    scores = jnp.where(visible[:, None], scores, MASKED)
    weights = low(jax.nn.softmax(scores, axis=-1))
    return jnp.einsum('ghqk,gkhd->gqhd', weights, value_rows, precision=lax.Precision.HIGHEST)

def expert_block(packed):
    rows_in, gate_w, up_w, down_w = packed
    pre_gate = low_back(product(rows_in, gate_w))
    pre_up = low_back(product(rows_in, up_w))
    activated = low(jax.nn.silu(pre_gate) * pre_up)
    return low(low_back(product(activated, down_w)))

def gather_rows(rows_in, index_in):
    return rows_in[index_in]

def reference(tokens, segments, expert_ids, norm_gains, w_query, w_key, w_value, w_out, w_router, expert_gate, expert_up, expert_down, cotangent):
    blocks = TOKENS // TOK_DEV
    slot_index = jax.vmap(slot_table)(expert_ids.reshape(blocks, TOK_DEV, TOPK))
    sources = jax.vmap(source_table)(slot_index)
    target = jnp.where(slot_index >= 0, slot_index, EXPERTS * CAP).astype(jnp.int32)
    group = math.gcd(blocks, max(1, 4096 // TOK_DEV))
    cosine, sine = rope_tables(TOK_DEV, HD)

    def forward(inputs, gains, wq, wk, wv, wo, wr, gate_all, up_all, down_all):
        gains = low(gains)
        wq, wk, wv, wo, wr = (low(wq), low(wk), low(wv), low(wo), low(wr))
        normed_in = low(rms_norm(inputs, gains[0]))
        query = low_back(product(normed_in, wq))
        key_rows = low_back(product(normed_in, wk))
        value_rows = low(low_back(product(normed_in, wv)))
        query = rms_norm(query, gains[1]).reshape(blocks, TOK_DEV, H, HD)
        key_rows = rms_norm(key_rows, gains[2]).reshape(blocks, TOK_DEV, H, HD)
        query = low(rotate(query, cosine, sine))
        key_rows = low(rotate(key_rows, cosine, sine))
        shaped = (blocks // group, group, TOK_DEV, H, HD)
        attended = lax.map(jax.checkpoint(attend), (query.reshape(shaped), key_rows.reshape(shaped), value_rows.reshape(shaped), segments.reshape(blocks // group, group, TOK_DEV)))
        attended = low(low_back(attended.reshape(TOKENS, D)))
        residual = inputs + low_back(product(attended, wo))
        normed_mid = low(rms_norm(residual, gains[3]))
        logits = low_back(product(normed_mid, wr))
        probs = jax.nn.softmax(logits, axis=-1)
        gate_vals = low(jnp.take_along_axis(probs, expert_ids, axis=1)).reshape(blocks, TOK_DEV, TOPK)
        padded = jnp.concatenate([normed_mid.reshape(blocks, TOK_DEV, D), jnp.zeros((blocks, 1, D), jnp.float32)], axis=1)
        sent = low_back(jax.vmap(gather_rows)(padded, sources))
        grouped = sent.reshape(N_DP, N_EXPERT, EXPERTS, CAP, D).transpose(0, 2, 1, 3, 4).reshape(N_DP * EXPERTS, N_EXPERT * CAP, D)
        results = lax.map(jax.checkpoint(expert_block), (grouped, gate_all.reshape(N_DP * EXPERTS, D, FF), up_all.reshape(N_DP * EXPERTS, D, FF), down_all.reshape(N_DP * EXPERTS, FF, D)))
        returned = results.reshape(N_DP, EXPERTS, N_EXPERT, CAP, D).transpose(0, 2, 1, 3, 4).reshape(blocks, EXPERTS * CAP, D)
        returned = jnp.concatenate([returned, jnp.zeros((blocks, 1, D), jnp.float32)], axis=1)
        moe = jnp.zeros((blocks, TOK_DEV, D), jnp.float32)
        for column in range(TOPK):
            picked = jax.vmap(gather_rows)(returned, target[:, :, column])
            moe = moe + gate_vals[:, :, column, None] * picked
        moe = low_back(moe.reshape(TOKENS, D))
        return residual + moe
    primal = (tokens.astype(jnp.float32), norm_gains, w_query, w_key, w_value, w_out, w_router, jnp.broadcast_to(expert_gate.astype(jnp.float32)[None], (N_DP, EXPERTS, D, FF)), jnp.broadcast_to(expert_up.astype(jnp.float32)[None], (N_DP, EXPERTS, D, FF)), jnp.broadcast_to(expert_down.astype(jnp.float32)[None], (N_DP, EXPERTS, FF, D)))
    mixed, pull = jax.vjp(forward, *primal)
    grads = pull(cotangent.astype(jnp.float32))
    return (mixed.astype(jnp.bfloat16), grads[0].astype(jnp.bfloat16), grads[1], grads[2], grads[3], grads[4], grads[5], grads[6], grads[7], grads[8], grads[9])
```

```python
import jax
import jax.numpy as jnp
from jax import lax
from jax.experimental import pallas as pl
from jax.experimental.pallas import tpu as pltpu
from jax.sharding import PartitionSpec as P

HD = 128


EPS = 1e-05
THETA = 10000.0
MASKED = -1e30
LANES = 128


def norm_rows(value, gain):
    inverse = lax.rsqrt(jnp.mean(value * value, axis=-1, keepdims=True) + EPS)
    normed = value * inverse
    return (normed * gain, normed, inverse)


def norm_back(grad_in, gain, normed, inverse):
    grad_normed = grad_in * gain
    grad_gain = jnp.sum(grad_in * normed, axis=0)
    inner = jnp.mean(grad_normed * normed, axis=-1, keepdims=True)
    return (inverse * (grad_normed - normed * inner), grad_gain)


def rope_tables(length, head):
    half = head // 2
    freq = THETA ** (-(jnp.arange(half, dtype=jnp.float32) * 2.0) / head)
    angle = jnp.arange(length, dtype=jnp.float32)[:, None] * freq[None, :]
    angle = jnp.concatenate([angle, angle], axis=-1)
    return (jnp.cos(angle)[:, None, :], jnp.sin(angle)[:, None, :])


def rotate(value, cosine, sine):
    half = value.shape[-1] // 2
    turned = jnp.concatenate([-value[..., half:], value[..., :half]], axis=-1)
    return value * cosine + turned * sine


def rotate_back(grad_in, cosine, sine):
    half = grad_in.shape[-1] // 2
    part = grad_in * sine
    turned = jnp.concatenate([part[..., half:], -part[..., :half]], axis=-1)
    return grad_in * cosine + turned


def contract_rows(left, right):
    return lax.dot_general(
        left, right, (((0,), (0,)), ((), ())), preferred_element_type=jnp.float32
    )


def contract_cols(left, right):
    return lax.dot_general(
        left, right, (((1,), (1,)), ((), ())), preferred_element_type=jnp.float32
    )


def product(left, right):
    return jnp.dot(left, right, preferred_element_type=jnp.float32)


def tie(*values):
    return lax.optimization_barrier(values)


class Spread:
    def __init__(self, here, own):
        self.here, self.queue, self.done = here, [own], 0

    def step(self):
        here, own = self.here, self.queue[0]
        self.done += 1
        if self.done >= here.nz:
            return []
        if here.nz != 4:
            moves = [(a, (a + self.done) % here.nz) for a in range(here.nz)]
            return [here.along_line(own, moves)]
        if self.done == 1:
            return [
                here.along_line(own, [(0, 1), (1, 0), (2, 3), (3, 2)]),
                here.along_line(own, [(1, 2), (2, 1)]),
            ]
        if self.done == 2:
            return [
                here.along_line(self.middle, [(1, 0), (2, 3)]),
                here.along_line(self.queue[1], [(1, 2), (2, 1)]),
            ]
        return [here.along_line(self.across, [(1, 0), (2, 3)])]

    def land(self, arrays):
        here = self.here
        if not arrays:
            return
        if here.nz != 4:
            self.queue += arrays
            return
        inner = (here.z == 1) | (here.z == 2)
        if self.done == 1:
            one, self.middle = arrays
            self.queue.append(one)
        elif self.done == 2:
            edge, self.across = arrays
            self.queue.append(jnp.where(inner, self.middle, edge))
        else:
            self.queue.append(jnp.where(inner, self.across, arrays[0]))

    def finish(self):
        while len(self.queue) < self.here.nz:
            self.land(self.step())
        return self.queue


class Collect:
    def __init__(self, here):
        self.here, self.came, self.moves = here, [], []

    def add(self, k, part):
        here = self.here
        if k == 0:
            self.total = part
            for value in self.came:
                self.total = self.total + value
            return []
        if here.nz != 4:
            out = [(part, [(a, (a - k) % here.nz) for a in range(here.nz)])]
        elif k == 3:
            self.three = part
            out = [(part, [(0, 1), (3, 2)])]
        elif k == 2:
            self.two = part
            (edge,) = self.came
            out = [(self.three + edge, [(1, 2), (2, 1)]), (part, [(0, 1), (3, 2)])]
        else:
            across, edge = self.came
            out = [
                (part + across, [(0, 1), (1, 0), (2, 3), (3, 2)]),
                (self.two + edge, [(1, 2), (2, 1)]),
            ]
        self.moves = [moves for _, moves in out]
        return [value.astype(jnp.bfloat16) for value, _ in out]

    def send(self, values):
        return [self.here.along_line(v, m) for v, m in zip(values, self.moves, strict=True)]

    def land(self, arrays):
        came = [value.astype(jnp.float32) for value in arrays]
        self.came = came if self.here.nz == 4 else self.came + came
        self.moves = []


def grid_of(count):
    if count % 32 == 0:
        return (count // 16, 4, 4)
    if count % 4 == 0:
        return (count // 4, 2, 2)
    return (count, 1, 1)


class Places:
    def __init__(self):
        self.count = lax.axis_size("expert")
        self.cores = lax.axis_size("dp")
        self.nz, self.ny, self.nx = grid_of(self.count)
        self.plane = self.ny * self.nx
        self.me = lax.axis_index("expert")
        self.core = lax.axis_index("dp")
        self.z = self.me // self.plane
        self.y = (self.me // self.nx) % self.ny
        self.x = self.me % self.nx
        self.steps = [(dy, dx) for dy in range(self.ny) for dx in range(self.nx)]
        self.square = (self.ny, self.nx) == (2, 2)
        if self.nz == 4:
            self.queue = [[0, 1, 2, 3], [1, 0, 2, 3], [2, 3, 1, 0], [3, 2, 1, 0]]
        else:
            self.queue = [[(z - k) % self.nz for k in range(self.nz)] for z in range(self.nz)]

    def at(self, z, y, x):
        return (z * self.ny + y) * self.nx + x

    def shift_plane(self, value, dy, dx):
        pairs = [
            (self.at(z, y, x), self.at(z, (y + dy) % self.ny, (x + dx) % self.nx))
            for z in range(self.nz)
            for y in range(self.ny)
            for x in range(self.nx)
        ]
        return lax.ppermute(value, "expert", pairs)

    def along_line(self, value, moves):
        pairs = [
            (self.at(a, y, x), self.at(b, y, x))
            for a, b in moves
            for y in range(self.ny)
            for x in range(self.nx)
        ]
        return lax.ppermute(value, "expert", pairs)

    def other_core(self, value, step):
        pairs = [(c, (c + step) % self.cores) for c in range(self.cores)]
        return lax.ppermute(value, "dp", pairs)

    def arrival(self, rows):
        shard = rows // (self.cores * self.count)
        order = jnp.arange(rows, dtype=jnp.int32)
        inside, rest = order % shard, order // shard
        step, rest = rest % self.plane, rest // self.plane
        core, k = rest % self.cores, rest // self.cores
        zed = self.queue_of(k)
        y = (self.y - step // self.nx) % self.ny
        x = (self.x - step % self.nx) % self.nx
        core = (self.core - core) % self.cores
        source = (core * self.count + self.at(zed, y, x)) * shard + inside
        return (order[:, None] == source[None, :]).astype(jnp.bfloat16)

    def queue_of(self, k):
        table = jnp.asarray(self.queue, jnp.int32)[self.z]
        zed = jnp.zeros_like(k)
        for q in range(self.nz):
            zed = jnp.where(k == q, table[q], zed)
        return zed

    def deal(self, rows):
        return [
            rows[i] if s == (0, 0) else self.shift_plane(rows[i], *s)
            for i, s in enumerate(self.steps)
        ]

    def deal_back(self, rows):
        return [
            rows[i] if s == (0, 0) else self.shift_plane(rows[i], -s[0], -s[1])
            for i, s in enumerate(self.steps)
        ]

    def along_plane(self, values):
        return [
            v if s == (0, 0) else self.shift_plane(v, *s)
            for v, s in zip(values, self.steps, strict=True)
        ]

    def along_whole_line(self, parts):
        return [
            part
            if k == 0
            else self.along_line(part, [(a, (a + k) % self.nz) for a in range(self.nz)])
            for k, part in enumerate(parts)
        ]

    def target_order(self, width, lead):
        shard = width // self.count
        order = jnp.arange(width, dtype=jnp.int32)
        inside, rest = order % shard, order // shard
        k, rest = rest % self.nz, rest // self.nz
        if lead == "x":
            dy, dx = rest % self.ny, rest // self.ny
        else:
            dx, dy = rest % self.nx, rest // self.nx
        y, x = (self.y + dy) % self.ny, (self.x + dx) % self.nx
        source = self.at((self.z + k) % self.nz, y, x) * shard + inside
        return (order[:, None] == source[None, :]).astype(jnp.bfloat16)

    def scatter_terms(self, by_x, by_y, right):
        wire = jnp.bfloat16
        if not self.square:
            line = by_x.shape[1] // self.plane
            starts = [(dx * self.ny + dy) * line for dy, dx in self.steps]
            parts = [contract_rows(by_x[:, start : start + line], right) for start in starts]
            return parts[:1] + [part.astype(wire) for part in parts[1:]]
        half, far = right.shape[1] // 2, by_x.shape[1] // 2
        return [
            contract_rows(by_x[:, far:], right[:, :half]).astype(wire),
            contract_rows(by_y[:, far:], right[:, half:]).astype(wire),
            contract_rows(by_x[:, :far], right[:, :half]),
            contract_rows(by_y[:, :far], right[:, half:]),
        ]

    def scatter_sums(self, terms):
        wire, full = jnp.bfloat16, jnp.float32
        from_x, from_y, near_x, near_y = terms
        line = near_x.shape[0] // 2
        return [
            (near_x[line:] + from_x[line:].astype(full)).astype(wire),
            (near_y[line:] + from_y[line:].astype(full)).astype(wire),
            near_x[:line] + from_x[:line].astype(full),
            near_y[:line] + from_y[:line].astype(full),
        ]

    def line_parts(self, terms):
        full = jnp.float32
        if not self.square:
            total = sum(t.astype(full) for t in terms)
        else:
            from_y, from_x, near_x, near_y = terms
            total = jnp.concatenate(
                [near_x + from_y.astype(full), near_y + from_x.astype(full)], axis=1
            )
        shard = total.shape[0] // self.nz
        parts = [total[k * shard : (k + 1) * shard] for k in range(self.nz)]
        return parts[:1] + [part.astype(jnp.bfloat16) for part in parts[1:]]

    def all_tokens(self, value):
        return jnp.concatenate(
            [value] + [self.other_core(value, step) for step in range(1, self.cores)], axis=0
        )

    def own_columns(self, value):
        width = value.shape[1] // self.cores
        pieces = []
        for step in range(self.cores):
            start = ((self.core + step) % self.cores) * width
            piece = lax.dynamic_slice(value, (0, start), (value.shape[0], width))
            pieces.append(piece if step == 0 else self.other_core(piece, step))
        return jnp.concatenate(pieces, axis=0)


COLUMNS = 1024


def times_gathered(left, pieces, start, stop, so_far=None):
    plane, _, shard, width = pieces[0].shape
    rows, tiles = plane * shard, width // COLUMNS

    def body(left_ref, *refs):
        *piece_refs, out_ref = refs
        total = None if so_far is None else piece_refs.pop()[...]
        for i, piece_ref in enumerate(piece_refs):
            part = left_ref[:, i * rows : (i + 1) * rows]
            term = jnp.dot(
                part, piece_ref[...].reshape(rows, COLUMNS), preferred_element_type=jnp.float32
            )
            total = term if total is None else total + term
        out_ref[...] = total

    depth = (stop - start) * width
    out_spec = pl.BlockSpec((left.shape[0], COLUMNS), lambda w, j: (0, w * tiles + j))
    piece_spec = pl.BlockSpec((plane, 1, shard, COLUMNS), lambda w, j: (0, w + start, 0, j))
    return pl.pallas_call(
        body,
        grid=(stop - start, tiles),
        in_specs=[pl.BlockSpec(left.shape, lambda w, j: (0, 0))]
        + [piece_spec] * len(pieces)
        + [out_spec] * (so_far is not None),
        out_specs=out_spec,
        out_shape=jax.ShapeDtypeStruct((left.shape[0], depth), jnp.float32),
        compiler_params=pltpu.CompilerParams(vmem_limit_bytes=40 << 20),
        cost_estimate=pl.CostEstimate(
            flops=2 * left.shape[0] * left.shape[1] * depth,
            bytes_accessed=2 * left.shape[1] * depth + 8 * left.shape[0] * depth,
            transcendentals=0,
        ),
    )(left, *pieces, *([] if so_far is None else [so_far]))


def times_transposed(left, pieces, start, stop):
    plane, _, shard, width = pieces[0].shape
    rows, tiles = plane * shard, width // COLUMNS
    out_shape = (left.shape[0], rows * len(pieces))

    def body(left_ref, *refs):
        *piece_refs, out_ref = refs

        @pl.when((pl.program_id(0) == 0) & (pl.program_id(1) == 0))
        def _():
            out_ref[...] = jnp.zeros_like(out_ref)

        for i, piece_ref in enumerate(piece_refs):
            out_ref[:, i * rows : (i + 1) * rows] += lax.dot_general(
                left_ref[...],
                piece_ref[...].reshape(rows, COLUMNS),
                (((1,), (1,)), ((), ())),
                preferred_element_type=jnp.float32,
            )

    piece_spec = pl.BlockSpec((plane, 1, shard, COLUMNS), lambda w, j: (0, w + start, 0, j))
    return pl.pallas_call(
        body,
        grid=(stop - start, tiles),
        in_specs=[pl.BlockSpec((left.shape[0], COLUMNS), lambda w, j: (0, w * tiles + j))]
        + [piece_spec] * len(pieces),
        out_specs=pl.BlockSpec(out_shape, lambda w, j: (0, 0)),
        out_shape=jax.ShapeDtypeStruct(out_shape, jnp.float32),
        compiler_params=pltpu.CompilerParams(vmem_limit_bytes=40 << 20),
        cost_estimate=pl.CostEstimate(
            flops=2 * left.size * out_shape[1],
            bytes_accessed=2 * left.shape[1] * out_shape[1] + 4 * left.shape[0] * out_shape[1],
            transcendentals=0,
        ),
    )(left, *pieces)


def on_device(
    tokens,
    segments,
    expert_ids,
    norm_gains,
    w_query,
    w_key,
    w_value,
    w_out,
    w_router,
    expert_gate,
    expert_up,
    expert_down,
    cotangent,
):
    bfloat = jnp.bfloat16
    here = Places()
    length, width = tokens.shape
    topk = expert_ids.shape[1]
    experts = here.count
    capacity = length * topk // experts
    heads = width // HD
    shard = w_query.shape[0]
    plane = here.plane
    gate_w, up_w, down_w = expert_gate[0], expert_up[0], expert_down[0]

    labels = jnp.arange(experts, dtype=jnp.int32)
    named = jnp.any(expert_ids[:, :, None] == labels[None, None, :], axis=1)
    places = jnp.arange(length, dtype=jnp.int32)
    earlier = (places[:, None] < places[None, :]).astype(bfloat)
    slots = contract_rows(named.astype(bfloat), earlier)
    slots = jnp.where(named.T & (slots < capacity), slots, -1.0).astype(bfloat)

    order = range(here.nz)
    arrival = here.arrival(width)
    extra = norm_gains.shape[0] + w_router.shape[1]
    smalls = jnp.concatenate(
        [norm_gains.T, w_router, jnp.zeros((shard, -extra % LANES), jnp.float32)], axis=1
    ).astype(bfloat)
    smalls = jnp.concatenate([smalls, slots.reshape(-1, LANES)], axis=0)
    smalls = here.along_whole_line([smalls] * here.nz)
    plane_expert = jnp.stack(
        [
            here.at(here.z, (here.y + dy) % here.ny, (here.x + dx) % here.nx)
            for dy, dx in here.steps
        ]
    )
    chosen = plane_expert[:, None] == labels[None, :]
    slot_ids = jnp.arange(capacity, dtype=jnp.int32)
    spreads = []

    def spread_of(part):
        picked = jnp.sum(
            jnp.where(chosen[:, :, None], part[None].astype(jnp.float32), 0.0), axis=1
        ).astype(jnp.int32)
        hit = picked[:, None, :] == slot_ids[None, :, None]
        return hit.astype(bfloat).reshape(plane * capacity, length)

    def rows_of(spread, part):
        return list(product(spread, part).astype(bfloat).reshape(plane, capacity, -1))

    def parted(rows):
        return list(rows.reshape(plane, capacity, -1))

    def joined(rows):
        return jnp.concatenate(rows, axis=0)

    inputs = tokens.astype(jnp.float32)
    weights = jnp.stack([w_query, w_key, w_value, w_out]).astype(bfloat)
    line, cot_line = Spread(here, weights), Spread(here, cotangent)
    half = weights.shape[0] // 2
    got, pieces = [], []
    projected = None
    depth = width // here.nz
    cot_rows, rows_cot = [None] * here.nz, [None] * here.nz

    def stacked(rows):
        return rows.reshape(-1, shard, width)

    def share(blocks):
        chunk = jnp.concatenate(blocks, axis=0).reshape(plane, *weights.shape)
        return [chunk] + [here.other_core(chunk, s) for s in range(1, here.cores)]

    def project(k):
        return times_gathered(
            in_order[:, k * depth : (k + 1) * depth], pieces[k], 0, 3, projected
        )

    for k in range(here.nz + 2):
        outs = []
        if here.square:
            by_x, by_y = [], []
            if k < here.nz:
                by_x.append(line.queue[k])
                by_y.append(line.queue[k])
            if 0 < k <= here.nz:
                by_x.append(got[k - 1][2][:half])
                by_y.append(got[k - 1][1][half:])
            if k >= here.nz:
                by_x.append(stacked(cot_rows[k - here.nz][1]))
                by_y.append(stacked(cot_rows[k - here.nz][2]))
            outs = [jnp.concatenate(by_x, axis=0), jnp.concatenate(by_y, axis=0)]
            if k > here.nz:
                outs.append(jnp.concatenate([cot_rows[0][3], cot_rows[1][3]], axis=0))
        elif k < here.nz:
            outs = [line.queue[k]] * plane
        else:
            outs = cot_rows[k - here.nz]
        if k == 1:
            turned = jnp.stack(smalls).reshape(here.nz, -1)
            near = (here.z - here.queue_of(jnp.arange(here.nz))) % here.nz
            pick = (near[:, None] == jnp.arange(here.nz)[None, :]).astype(bfloat)
            turned = product(pick, turned).astype(bfloat).reshape(here.nz, -1, LANES)
            smalls, slots = turned[:, :shard], turned[:, shard:]
        outs, smalls, got, pieces, line.queue, cot_line.queue, cot_rows, cotangent = tie(
            outs, smalls, got, pieces, line.queue, cot_line.queue, cot_rows, cotangent
        )
        if here.square:
            ins = [here.shift_plane(outs[0], 0, 1), here.shift_plane(outs[1], 1, 0)]
            if k > here.nz:
                ins.append(here.shift_plane(outs[2], 1, 1))
        else:
            ins = here.along_plane(outs)
        moving = line.step() if k < here.nz else []
        moving_cot = cot_line.step() if k >= here.nz - 1 else []
        if k == 1:
            spreads = [spread_of(part.reshape(experts, length)) for part in slots]
            smalls = here.along_plane([smalls] * plane)
        if k > 1:
            pieces.append(share(got[k - 2]))
        if k == 2:
            smalls = jnp.stack(smalls, axis=1)
            smalls = [smalls] + [here.other_core(smalls, s) for s in range(1, here.cores)]
            smalls = jnp.stack(smalls, axis=1).reshape(width, -1)
        if k == 3:
            smalls = product(arrival, smalls).astype(bfloat)
            gains_f = smalls[:, : norm_gains.shape[0]].T.astype(jnp.float32)
            wr = smalls[:, norm_gains.shape[0] : extra]
            normed_in_f, normed_one, inverse_one = norm_rows(inputs, gains_f[0])
            normed_in = normed_in_f.astype(bfloat)
            in_order = product(normed_in, arrival).astype(bfloat)
        if k > 2:
            projected = project(k - 3)
        if k >= here.nz - 1 and k - here.nz + 1 < here.nz:
            at = k - here.nz + 1
            cot_rows[at] = rows_of(spreads[at], cot_line.queue[at])
        ins, moving, moving_cot, smalls, projected, cot_rows, spreads = tie(
            ins, moving, moving_cot, smalls, projected, cot_rows, spreads
        )
        line.land(moving)
        cot_line.land(moving_cot)
        if here.square:
            by_x, by_y = ins[:2]
            if k < here.nz:
                got.append([line.queue[k], by_x[: 2 * half], by_y[: 2 * half]])
                by_x, by_y = by_x[2 * half :], by_y[2 * half :]
            if 0 < k <= here.nz:
                got[k - 1] += [by_x[:half], by_y[:half]]
                by_x, by_y = by_x[half:], by_y[half:]
            if k >= here.nz:
                own = cot_rows[k - here.nz][0]
                rows_cot[k - here.nz] = [own, by_x.reshape(own.shape), by_y.reshape(own.shape)]
            if k > here.nz:
                for i in (0, 1):
                    rows_cot[i].append(ins[2][i * capacity : (i + 1) * capacity])
        elif k < here.nz:
            got.append(ins)
        else:
            rows_cot[k - here.nz] = ins

    order_x = here.target_order(width // here.cores, "x")
    order_y = here.target_order(width // here.cores, "y")

    def targeted(value):
        columns = here.own_columns(value)
        return [product(columns, o).astype(bfloat) for o in (order_x, order_y)]

    if here.nz > 2:
        cot_rows[2:], pieces, projected = tie(cot_rows[2:], pieces, projected)
        rows_cot[2] = here.along_plane(cot_rows[2])
        cot_rows[3] = rows_of(spreads[3], cot_line.queue[3])
    projected = project(here.nz - 1)
    pieces = [piece for chunk in pieces for piece in chunk]
    query_raw = projected[:, :width]
    key_raw = projected[:, width : 2 * width]
    values = projected[:, 2 * width :].astype(bfloat)
    query_n, query_normed, query_inverse = norm_rows(query_raw, gains_f[1])
    key_n, key_normed, key_inverse = norm_rows(key_raw, gains_f[2])
    cosine, sine = rope_tables(length, HD)
    query_rot = rotate(query_n.reshape(length, heads, HD), cosine, sine).astype(bfloat)
    key_rot = rotate(key_n.reshape(length, heads, HD), cosine, sine).astype(bfloat)
    if here.nz > 2:
        targets = targeted(normed_in)
        query_rot, key_rot, values, cot_rows[3], rows_cot[2], targets = tie(
            query_rot, key_rot, values, cot_rows[3], rows_cot[2], targets
        )
        rows_cot[3] = here.along_plane(cot_rows[3])
    else:
        targets = targeted(normed_in)
    value_heads = values.reshape(length, heads, HD)
    doc_ids = segments[0]
    visible = (doc_ids[:, None] == doc_ids[None, :]) & (places[:, None] >= places[None, :])
    score_scale = HD ** (-0.5)
    scores = (
        jnp.einsum("qhd,khd->hqk", query_rot, key_rot, preferred_element_type=jnp.float32)
        * score_scale
    )
    scores = jnp.where(visible[None], scores, MASKED)
    row_max = jnp.max(scores, axis=-1, keepdims=True)
    expo = jnp.exp(scores - row_max)
    probs = expo / jnp.sum(expo, axis=-1, keepdims=True)
    probs_low = probs.astype(bfloat)
    attended = (
        jnp.einsum("hqk,khd->qhd", probs_low, value_heads, preferred_element_type=jnp.float32)
        .reshape(length, width)
        .astype(bfloat)
    )
    residual = inputs + times_gathered(
        product(attended, arrival).astype(bfloat), pieces, 3, 4
    )
    normed_mid_f, normed_two, inverse_two = norm_rows(residual, gains_f[3])
    normed_mid = normed_mid_f.astype(bfloat)

    own_label = labels[None, :] == here.me

    def expert_forward(arrived):
        route_here = jax.nn.softmax(product(arrived, wr), axis=-1)
        gate = jnp.sum(jnp.where(own_label, route_here, 0.0), axis=-1)
        gate = gate.astype(bfloat).astype(jnp.float32)[:, None]
        pre_gate = product(arrived, gate_w)
        pre_up = product(arrived, up_w)
        activated = (jax.nn.silu(pre_gate) * pre_up).astype(bfloat)
        result = product(activated, down_w).astype(bfloat)
        gated = (gate * result.astype(jnp.float32)).astype(bfloat)
        return (gate, pre_gate, pre_up, activated, result, gated)

    def expert_backward(kept, cot):
        gate, pre_gate, pre_up, activated, result, _ = kept
        cot_f, result_f = cot.astype(jnp.float32), result.astype(jnp.float32)
        grad_y = (gate * cot_f).astype(bfloat)
        grad_g = jnp.sum(cot_f * result_f, axis=-1, keepdims=True)
        grad_act = contract_cols(grad_y, down_w)
        sigmoid_g = jax.nn.sigmoid(pre_gate)
        slope = sigmoid_g * (1.0 + pre_gate * (1.0 - sigmoid_g))
        grad_a = (grad_act * pre_up * slope).astype(bfloat)
        grad_b = (grad_act * (pre_gate * sigmoid_g)).astype(bfloat)
        grad_e = contract_cols(grad_a, gate_w) + contract_cols(grad_b, up_w)
        high = grad_g.astype(bfloat)
        low = (grad_g - high.astype(jnp.float32)).astype(bfloat)
        lanes = jnp.arange(LANES, dtype=jnp.int32)[None, :]
        tail = jnp.where(lanes == here.me, high, jnp.zeros((), bfloat))
        tail = jnp.where(lanes == here.me + LANES // 2, low, tail)
        back = jnp.concatenate([grad_e.astype(bfloat), tail], axis=1)
        return (back, grad_y, grad_a, grad_b)

    rows_next = rows_of(spreads[0], normed_mid)
    normed_mid, rows_next, rows_cot[-1] = tie(normed_mid, rows_next, rows_cot[-1])
    line = Spread(here, normed_mid)
    rows_in, forward = [], []
    for k in order:
        if k > 0:
            rows_next = rows_of(spreads[k], line.queue[k])
        rows_next, rows_in, line.queue = tie(rows_next, rows_in, line.queue)
        moving = line.step()
        rows = here.along_plane(rows_next)
        if k > 0:
            rows_in[-1] = joined(rows_in[-1])
            forward.append(expert_forward(rows_in[-1]))
        if k == here.nz // 2:
            targets_out = targeted(attended)
            rows, targets_out = tie(rows, targets_out)
        moving, rows, forward = tie(moving, rows, forward)
        rows_in.append(rows)
        line.land(moving)

    half = here.nz // 2
    back_y = [None] * here.nz
    backward = [None] * here.nz
    todo = ["forward", *reversed(order)]

    def work():
        k = todo.pop(0) if todo else None
        if k == "forward":
            rows_in[-1] = joined(rows_in[-1])
            forward.append(expert_forward(rows_in[-1]))
        elif k is not None:
            backward[k] = expert_backward(forward[k], joined(rows_cot[k]))

    for k in order[:half]:
        rows_next = parted(forward[k][5])
        rows_next, forward, backward, rows_in, rows_cot = tie(
            rows_next, forward, backward, rows_in, rows_cot
        )
        rows = here.deal_back(rows_next)
        work()
        rows, forward, backward = tie(rows, forward, backward)
        back_y[k] = rows
    collect = Collect(here)
    moving, back = [], None
    for k in reversed(order):
        if backward[k] is None:
            work()
        rows_next = parted(backward[k][0])
        rows_next, forward, backward, moving, back = tie(
            rows_next, forward, backward, moving, back
        )
        rows = here.deal_back(rows_next)
        if back is not None:
            collect.land(moving)
            moving = collect.add(k + 1, contract_rows(spreads[k + 1], joined(back)))
            if k == 0:
                arrived, activated = joined(rows_in), joined([kept[3] for kept in forward])
                grad_y, grad_a, grad_b = [
                    joined([kept[i] for kept in backward]) for i in (1, 2, 3)
                ]
                moving, activated, grad_y, arrived, grad_a, grad_b = tie(
                    moving, activated, grad_y, arrived, grad_a, grad_b
                )
            moving = collect.send(moving)
        if k > 0:
            work()
            moving, rows, forward, backward = tie(moving, rows, forward, backward)
        else:
            grad_down = contract_rows(activated, grad_y)
            moving, rows, grad_down = tie(moving, rows, grad_down)
        back = rows
    collect.land(moving)
    rows_next = parted(forward[-1][5])
    back, rows_next = tie(back, rows_next)
    collect.add(0, contract_rows(spreads[0], joined(back)))
    returned = collect.total
    rows_y = here.deal_back(rows_next)

    grad_mid = returned[:, :width]
    grad_route = (
        returned[:, width : width + experts]
        + returned[:, width + LANES // 2 : width + LANES // 2 + experts]
    )
    route = jax.nn.softmax(product(normed_mid, wr), axis=-1)
    grad_logits = (
        route * (grad_route - jnp.sum(route * grad_route, axis=-1, keepdims=True))
    ).astype(bfloat)
    grad_router = contract_rows(normed_mid, grad_logits)
    grad_mid = grad_mid + contract_cols(grad_logits, wr)
    grad_res_two, grad_gain_mid = norm_back(grad_mid, gains_f[3], normed_two, inverse_two)
    grad_residual = cotangent.astype(jnp.float32) + grad_res_two
    grad_attn = grad_residual.astype(bfloat)
    out_tokens = here.all_tokens(grad_attn)
    grad_attended = times_transposed(grad_attn, pieces, 3, 4).astype(bfloat)
    grad_attended = contract_cols(grad_attended, arrival).astype(bfloat)
    terms = here.scatter_terms(*targets_out, out_tokens)
    rows_next = [parted(forward[k][5]) for k in order[half : here.nz - 1]]
    grad_attended, terms, rows_y, rows_next = tie(grad_attended, terms, rows_y, rows_next)
    back_y[-1] = rows_y

    collect_y, adds_y = Collect(here), list(reversed(order))

    def next_y():
        if not adds_y:
            return []
        k = adds_y.pop(0)
        return collect_y.add(k, contract_rows(spreads[k], joined(back_y[k])))

    sending_y = next_y()
    sending_y, rows_next, grad_attended = tie(sending_y, rows_next, grad_attended)
    for k in reversed(order[half : here.nz - 1]):
        back_y[k] = here.deal_back(rows_next[k - half])
    moving = collect_y.send(sending_y)
    grad_attended = grad_attended.reshape(length, heads, HD)
    grad_probs = jnp.einsum(
        "qhd,khd->hqk", grad_attended, value_heads, preferred_element_type=jnp.float32
    )
    grad_values = jnp.einsum(
        "hqk,qhd->khd", probs_low, grad_attended, preferred_element_type=jnp.float32
    )
    grad_values = grad_values.reshape(length, width).astype(bfloat)
    inner = jnp.sum(probs * grad_probs, axis=-1, keepdims=True)
    grad_scores = (probs * (grad_probs - inner)).astype(bfloat)
    right = here.all_tokens(grad_values)
    grad_scores, grad_values, right, moving, back_y = tie(
        grad_scores, grad_values, right, moving, back_y
    )
    collect_y.land(moving)

    def leave(terms, sums, more_x, more_y):
        if not here.square:
            return list(terms)
        by_x, by_y = list(terms[:1]), list(terms[1:2])
        if sums:
            by_x.append(sums[1])
            by_y.append(sums[0])
        return [jnp.concatenate(by_x + more_x, axis=0), jnp.concatenate(by_y + more_y, axis=0)]

    def arrive(outs):
        if not here.square:
            return here.along_plane(outs) if outs else []
        return [here.shift_plane(outs[0], 0, 1), here.shift_plane(outs[1], 1, 0)]

    sending_y = next_y()
    outs = leave(terms, [], [], [])
    near, near_last = terms[2:], []
    outs, sending_y, grad_scores, right = tie(outs, sending_y, grad_scores, right)
    ins = arrive(outs)
    moving = collect_y.send(sending_y)
    terms = here.scatter_terms(*targets, right)
    grad_query_rot = (
        jnp.einsum("hqk,khd->qhd", grad_scores, key_rot, preferred_element_type=jnp.float32)
        * score_scale
    )
    grad_key_rot = (
        jnp.einsum("hqk,qhd->khd", grad_scores, query_rot, preferred_element_type=jnp.float32)
        * score_scale
    )
    grad_query_n = rotate_back(grad_query_rot, cosine, sine).reshape(length, width)
    grad_key_n = rotate_back(grad_key_rot, cosine, sine).reshape(length, width)
    grad_query_f, grad_gain_query = norm_back(grad_query_n, gains_f[1], query_normed, query_inverse)
    grad_key_f, grad_gain_key = norm_back(grad_key_n, gains_f[2], key_normed, key_inverse)
    grad_query = grad_query_f.astype(bfloat)
    grad_key = grad_key_f.astype(bfloat)

    grad_query, grad_key, terms, ins, moving = tie(grad_query, grad_key, terms, ins, moving)
    expert_sums = [(arrived, grad_a), (arrived, grad_b)]
    firsts, lasts, shares = [], [], []
    small_rows = 4 + experts
    jobs, small = 4, [None]
    for i in range(1, jobs + 2):
        collect_y.land(moving)
        if here.square:
            by_x, by_y = ins
            if i <= jobs:
                rows = near[0].shape[0]
                firsts.append([by_x[:rows], by_y[:rows], *near])
                by_x, by_y = by_x[rows:], by_y[rows:]
            if i > 1:
                rows = near_last[0].shape[0]
                lasts.append([by_y[:rows], by_x[:rows], *near_last])
                by_x, by_y = by_x[rows:], by_y[rows:]
        elif i <= jobs:
            lasts.append(ins)
        sums, parts, more_x, more_y, outs = [], [], [], [], []
        if here.square:
            sums = here.scatter_sums(firsts[i - 1]) if i <= jobs else []
            columns = small[0].shape[1] // 2 if small[0] is not None else 0
            if i == 3:
                more_x = [small[0][:, columns:].astype(bfloat).reshape(-1, width // 2)]
                small = [small[0][:, :columns]]
            elif i == 4:
                got_small = by_x.reshape(small[0].shape).astype(jnp.float32)
                small = [small[0] + got_small]
                more_y = [small[0][:, columns:].astype(bfloat).reshape(-1, width // 2)]
                small = [small[0][:, :columns]]
            elif i == 5:
                small = [small[0] + by_y.reshape(small[0].shape).astype(jnp.float32)]
            if i < jobs:
                near = terms[2:]
                outs = leave(terms, sums, more_x, more_y)
            elif i == jobs:
                outs = [
                    jnp.concatenate([sums[1], *more_x], axis=0),
                    jnp.concatenate([sums[0], *more_y], axis=0),
                ]
            near_last = sums[2:]
        elif i < jobs:
            outs = leave(terms, [], [], [])
        at = i - 2 if here.square else i - 1
        if 0 <= at < jobs:
            parts = here.line_parts(lasts[at])
            if here.square and at == jobs - 1:
                flat = [
                    piece.reshape(-1, width)
                    for piece in jnp.split(small[0], here.nz, axis=1)
                ]
                parts = [
                    jnp.concatenate([part, piece.astype(part.dtype)], axis=0)
                    for part, piece in zip(parts, flat, strict=True)
                ]
        sending_y = next_y()
        outs, parts, sending_y, terms, expert_sums, near, near_last, small = tie(
            outs, parts, sending_y, terms, expert_sums, near, near_last, small
        )
        ins = arrive(outs) if outs else []
        if parts:
            parts = here.along_whole_line(parts)
        moving = collect_y.send(sending_y)
        if i == 1:
            both = jnp.stack([grad_key, grad_query])
            others = [here.other_core(both, step) for step in range(1, here.cores)]
            rights = [jnp.concatenate([v[j] for v in [both, *others]], axis=0) for j in (0, 1)]
            grad_in_norm = times_transposed(
                jnp.concatenate([grad_query, grad_key, grad_values], axis=1), pieces, 0, 3
            )
            high = grad_in_norm.astype(bfloat)
            low = (grad_in_norm - high.astype(jnp.float32)).astype(bfloat)
            grad_in_norm = contract_cols(high, arrival) + contract_cols(low, arrival)
            grad_res_one, grad_gain_in = norm_back(
                grad_in_norm, gains_f[0], normed_one, inverse_one
            )
            grad_tokens = (grad_residual + grad_res_one).astype(bfloat)
            smalls = jnp.concatenate(
                [
                    jnp.stack(
                        [grad_gain_in, grad_gain_query, grad_gain_key, grad_gain_mid], axis=0
                    ),
                    grad_router.T,
                    jnp.zeros((-small_rows % 32, width), jnp.float32),
                ],
                axis=0,
            )
            if here.square:
                rows = smalls.shape[0]
                smalls = here.own_columns(smalls)
                smalls = sum(smalls[c * rows : (c + 1) * rows] for c in range(here.cores))
                small = [product(smalls.astype(bfloat), order_x)]
            else:
                smalls = lax.psum(smalls, ("dp", "expert"))
                smalls = lax.dynamic_slice(
                    smalls,
                    (0, (here.core * here.count + here.me) * shard),
                    (smalls.shape[0], shard),
                )
            ins, grad_tokens, small, rights = tie(ins, grad_tokens, small, rights)
        if i < jobs - 1:
            terms = here.scatter_terms(*targets, rights[i - 1])
        if 1 < i < 4:
            grad = contract_rows(*expert_sums[i - 2])
            ins, expert_sums[i - 2] = tie(ins, grad)
        ins, parts, moving, terms = tie(ins, parts, moving, terms)
        if parts:
            shares.append(sum(part.astype(jnp.float32) for part in parts))
    if here.square:
        smalls = shares[-1][shard:].reshape(-1, shard)
        shares[-1] = shares[-1][:shard]
    mixed = (residual + collect_y.total).astype(bfloat)
    grad_wo, grad_wv, grad_wk, grad_wq = shares
    grad_gate_w, grad_up_w = expert_sums
    return (
        mixed,
        grad_tokens,
        smalls[:4],
        grad_wq,
        grad_wk,
        grad_wv,
        grad_wo,
        smalls[4:small_rows].T,
        grad_gate_w[None, None],
        grad_up_w[None, None],
        grad_down[None, None],
    )


def solution(mesh):
    return jax.shard_map(
        on_device,
        mesh=mesh,
        in_specs=(
            P(("dp", "expert"), None),
            P(("dp", "expert"), None),
            P(("dp", "expert"), None),
            P(None, ("dp", "expert")),
            P(("dp", "expert"), None),
            P(("dp", "expert"), None),
            P(("dp", "expert"), None),
            P(("dp", "expert"), None),
            P(("dp", "expert"), None),
            P("expert", None, None),
            P("expert", None, None),
            P("expert", None, None),
            P(("dp", "expert"), None),
        ),
        out_specs=(
            P(("dp", "expert"), None),
            P(("dp", "expert"), None),
            P(None, ("dp", "expert")),
            P(("dp", "expert"), None),
            P(("dp", "expert"), None),
            P(("dp", "expert"), None),
            P(("dp", "expert"), None),
            P(("dp", "expert"), None),
            P("dp", "expert", None, None),
            P("dp", "expert", None, None),
            P("dp", "expert", None, None),
        ),
        check_vma=False,
    )
```

```python
import jax
import jax.numpy as jnp
from jax import lax
from jax.experimental import pallas as pl
from jax.experimental.pallas import tpu as pltpu
from jax.sharding import PartitionSpec as P

HD = 128


EPS = 1e-05
THETA = 10000.0
MASKED = -1e30
LANES = 128


def norm_rows(value, gain):
    inverse = lax.rsqrt(jnp.mean(value * value, axis=-1, keepdims=True) + EPS)
    normed = value * inverse
    return (normed * gain, normed, inverse)


def norm_back(grad_in, gain, normed, inverse):
    grad_normed = grad_in * gain
    grad_gain = jnp.sum(grad_in * normed, axis=0)
    inner = jnp.mean(grad_normed * normed, axis=-1, keepdims=True)
    return (inverse * (grad_normed - normed * inner), grad_gain)


def contract_rows(left, right):
    return lax.dot_general(
        left, right, (((0,), (0,)), ((), ())), preferred_element_type=jnp.float32
    )


def contract_cols(left, right):
    return lax.dot_general(
        left, right, (((1,), (1,)), ((), ())), preferred_element_type=jnp.float32
    )


def product(left, right):
    return jnp.dot(left, right, preferred_element_type=jnp.float32)


def tie(*values):
    return lax.optimization_barrier(values)


class Spread:
    def __init__(self, here, own):
        self.here, self.queue, self.done = here, [own], 0

    def step(self):
        here, own = self.here, self.queue[0]
        self.done += 1
        if self.done >= here.nz:
            return []
        if here.nz != 4:
            moves = [(a, (a + self.done) % here.nz) for a in range(here.nz)]
            return [here.along_line(own, moves)]
        if self.done == 1:
            return [
                here.along_line(own, [(0, 1), (1, 0), (2, 3), (3, 2)]),
                here.along_line(own, [(1, 2), (2, 1)]),
            ]
        if self.done == 2:
            return [
                here.along_line(self.middle, [(1, 0), (2, 3)]),
                here.along_line(self.queue[1], [(1, 2), (2, 1)]),
            ]
        return [here.along_line(self.across, [(1, 0), (2, 3)])]

    def land(self, arrays):
        here = self.here
        if not arrays:
            return
        if here.nz != 4:
            self.queue += arrays
            return
        inner = (here.z == 1) | (here.z == 2)
        if self.done == 1:
            one, self.middle = arrays
            self.queue.append(one)
        elif self.done == 2:
            edge, self.across = arrays
            self.queue.append(jnp.where(inner, self.middle, edge))
        else:
            self.queue.append(jnp.where(inner, self.across, arrays[0]))

    def finish(self):
        while len(self.queue) < self.here.nz:
            self.land(self.step())
        return self.queue


class Collect:
    def __init__(self, here):
        self.here, self.came, self.moves = here, [], []

    def add(self, k, part):
        here = self.here
        if k == 0:
            self.total = part
            for value in self.came:
                self.total = self.total + value
            return []
        if here.nz != 4:
            out = [(part, [(a, (a - k) % here.nz) for a in range(here.nz)])]
        elif k == 3:
            self.three = part
            out = [(part, [(0, 1), (3, 2)])]
        elif k == 2:
            self.two = part
            (edge,) = self.came
            out = [(self.three + edge, [(1, 2), (2, 1)]), (part, [(0, 1), (3, 2)])]
        else:
            across, edge = self.came
            out = [
                (part + across, [(0, 1), (1, 0), (2, 3), (3, 2)]),
                (self.two + edge, [(1, 2), (2, 1)]),
            ]
        self.moves = [moves for _, moves in out]
        return [value.astype(jnp.bfloat16) for value, _ in out]

    def send(self, values):
        return [self.here.along_line(v, m) for v, m in zip(values, self.moves, strict=True)]

    def land(self, arrays):
        came = [value.astype(jnp.float32) for value in arrays]
        self.came = came if self.here.nz == 4 else self.came + came
        self.moves = []


def grid_of(count):
    if count % 32 == 0:
        return (count // 16, 4, 4)
    if count % 4 == 0:
        return (count // 4, 2, 2)
    return (count, 1, 1)


class Places:
    def __init__(self):
        self.count = lax.axis_size("expert")
        self.cores = lax.axis_size("dp")
        self.nz, self.ny, self.nx = grid_of(self.count)
        self.plane = self.ny * self.nx
        self.me = lax.axis_index("expert")
        self.core = lax.axis_index("dp")
        self.z = self.me // self.plane
        self.y = (self.me // self.nx) % self.ny
        self.x = self.me % self.nx
        self.steps = [(dy, dx) for dy in range(self.ny) for dx in range(self.nx)]
        self.square = (self.ny, self.nx) == (2, 2)
        if self.nz == 4:
            self.queue = [[0, 1, 2, 3], [1, 0, 2, 3], [2, 3, 1, 0], [3, 2, 1, 0]]
        else:
            self.queue = [[(z - k) % self.nz for k in range(self.nz)] for z in range(self.nz)]

    def at(self, z, y, x):
        return (z * self.ny + y) * self.nx + x

    def shift_plane(self, value, dy, dx):
        pairs = [
            (self.at(z, y, x), self.at(z, (y + dy) % self.ny, (x + dx) % self.nx))
            for z in range(self.nz)
            for y in range(self.ny)
            for x in range(self.nx)
        ]
        return lax.ppermute(value, "expert", pairs)

    def along_line(self, value, moves):
        pairs = [
            (self.at(a, y, x), self.at(b, y, x))
            for a, b in moves
            for y in range(self.ny)
            for x in range(self.nx)
        ]
        return lax.ppermute(value, "expert", pairs)

    def other_core(self, value, step):
        pairs = [(c, (c + step) % self.cores) for c in range(self.cores)]
        return lax.ppermute(value, "dp", pairs)

    def arrival(self, rows):
        shard = rows // (self.cores * self.count)
        order = jnp.arange(rows, dtype=jnp.int32)
        inside, rest = order % shard, order // shard
        step, rest = rest % self.plane, rest // self.plane
        core, k = rest % self.cores, rest // self.cores
        zed = self.queue_of(k)
        y = (self.y - step // self.nx) % self.ny
        x = (self.x - step % self.nx) % self.nx
        core = (self.core - core) % self.cores
        source = (core * self.count + self.at(zed, y, x)) * shard + inside
        return (order[:, None] == source[None, :]).astype(jnp.bfloat16)

    def queue_of(self, k):
        table = jnp.asarray(self.queue, jnp.int32)[self.z]
        zed = jnp.zeros_like(k)
        for q in range(self.nz):
            zed = jnp.where(k == q, table[q], zed)
        return zed

    def deal(self, rows):
        return [
            rows[i] if s == (0, 0) else self.shift_plane(rows[i], *s)
            for i, s in enumerate(self.steps)
        ]

    def deal_back(self, rows):
        return [
            rows[i] if s == (0, 0) else self.shift_plane(rows[i], -s[0], -s[1])
            for i, s in enumerate(self.steps)
        ]

    def along_plane(self, values):
        return [
            v if s == (0, 0) else self.shift_plane(v, *s)
            for v, s in zip(values, self.steps, strict=True)
        ]

    def along_whole_line(self, parts):
        return [
            part
            if k == 0
            else self.along_line(part, [(a, (a + k) % self.nz) for a in range(self.nz)])
            for k, part in enumerate(parts)
        ]

    def target_order(self, width, lead):
        shard = width // self.count
        order = jnp.arange(width, dtype=jnp.int32)
        inside, rest = order % shard, order // shard
        k, rest = rest % self.nz, rest // self.nz
        if lead == "x":
            dy, dx = rest % self.ny, rest // self.ny
        else:
            dx, dy = rest % self.nx, rest // self.nx
        y, x = (self.y + dy) % self.ny, (self.x + dx) % self.nx
        source = self.at((self.z + k) % self.nz, y, x) * shard + inside
        return (order[:, None] == source[None, :]).astype(jnp.bfloat16)

    def scatter_far(self, by_x, by_y, right):
        wire = jnp.bfloat16
        if not self.square:
            line = by_x.shape[1] // self.plane
            starts = [(dx * self.ny + dy) * line for dy, dx in self.steps]
            parts = [contract_rows(by_x[:, start : start + line], right) for start in starts]
            return parts[:1] + [part.astype(wire) for part in parts[1:]]
        half, far = right.shape[1] // 2, by_x.shape[1] // 2
        return [
            contract_rows(by_x[:, far:], right[:, :half]).astype(wire),
            contract_rows(by_y[:, far:], right[:, half:]).astype(wire),
        ]

    def scatter_near(self, by_x, by_y, right):
        if not self.square:
            return []
        half, far = right.shape[1] // 2, by_x.shape[1] // 2
        return [
            contract_rows(by_x[:, :far], right[:, :half]),
            contract_rows(by_y[:, :far], right[:, half:]),
        ]

    def scatter_sums(self, terms):
        wire, full = jnp.bfloat16, jnp.float32
        from_x, from_y, near_x, near_y = terms
        line = near_x.shape[0] // 2
        return [
            (near_x[line:] + from_x[line:].astype(full)).astype(wire),
            (near_y[line:] + from_y[line:].astype(full)).astype(wire),
            near_x[:line] + from_x[:line].astype(full),
            near_y[:line] + from_y[:line].astype(full),
        ]

    def line_parts(self, terms):
        full = jnp.float32
        if not self.square:
            total = sum(t.astype(full) for t in terms)
        else:
            from_y, from_x, near_x, near_y = terms
            total = jnp.concatenate(
                [near_x + from_y.astype(full), near_y + from_x.astype(full)], axis=1
            )
        shard = total.shape[0] // self.nz
        parts = [total[k * shard : (k + 1) * shard] for k in range(self.nz)]
        return parts[:1] + [part.astype(jnp.bfloat16) for part in parts[1:]]

    def all_tokens(self, value):
        return jnp.concatenate(
            [value] + [self.other_core(value, step) for step in range(1, self.cores)], axis=0
        )

    def core_columns(self, value):
        width = value.shape[1] // self.cores
        starts = [((self.core + step) % self.cores) * width for step in range(self.cores)]
        return [lax.dynamic_slice(value, (0, start), (value.shape[0], width)) for start in starts]

    def to_cores(self, pieces):
        return [
            piece if step == 0 else self.other_core(piece, step)
            for step, piece in enumerate(pieces)
        ]


COLUMNS = 1024


def times_gathered(left, pieces, start, stop, so_far=None):
    plane, _, shard, width = pieces[0].shape
    rows, tiles = plane * shard, width // COLUMNS

    def body(left_ref, *refs):
        *piece_refs, out_ref = refs
        total = None if so_far is None else piece_refs.pop()[...]
        for i, piece_ref in enumerate(piece_refs):
            part = left_ref[:, i * rows : (i + 1) * rows]
            term = jnp.dot(
                part, piece_ref[...].reshape(rows, COLUMNS), preferred_element_type=jnp.float32
            )
            total = term if total is None else total + term
        out_ref[...] = total

    depth = (stop - start) * width
    out_spec = pl.BlockSpec((left.shape[0], COLUMNS), lambda w, j: (0, w * tiles + j))
    piece_spec = pl.BlockSpec((plane, 1, shard, COLUMNS), lambda w, j: (0, w + start, 0, j))
    return pl.pallas_call(
        body,
        grid=(stop - start, tiles),
        in_specs=[pl.BlockSpec(left.shape, lambda w, j: (0, 0))]
        + [piece_spec] * len(pieces)
        + [out_spec] * (so_far is not None),
        out_specs=out_spec,
        out_shape=jax.ShapeDtypeStruct((left.shape[0], depth), jnp.float32),
        compiler_params=pltpu.CompilerParams(vmem_limit_bytes=40 << 20),
        cost_estimate=pl.CostEstimate(
            flops=2 * left.shape[0] * left.shape[1] * depth,
            bytes_accessed=2 * left.shape[1] * depth + 8 * left.shape[0] * depth,
            transcendentals=0,
        ),
    )(left, *pieces, *([] if so_far is None else [so_far]))


def times_transposed(left, pieces, start, stop):
    plane, _, shard, width = pieces[0].shape
    rows, tiles = plane * shard, width // COLUMNS
    out_shape = (left.shape[0], rows * len(pieces))

    def body(left_ref, *refs):
        *piece_refs, out_ref = refs

        @pl.when((pl.program_id(0) == 0) & (pl.program_id(1) == 0))
        def _():
            out_ref[...] = jnp.zeros_like(out_ref)

        for i, piece_ref in enumerate(piece_refs):
            out_ref[:, i * rows : (i + 1) * rows] += lax.dot_general(
                left_ref[...],
                piece_ref[...].reshape(rows, COLUMNS),
                (((1,), (1,)), ((), ())),
                preferred_element_type=jnp.float32,
            )

    piece_spec = pl.BlockSpec((plane, 1, shard, COLUMNS), lambda w, j: (0, w + start, 0, j))
    return pl.pallas_call(
        body,
        grid=(stop - start, tiles),
        in_specs=[pl.BlockSpec((left.shape[0], COLUMNS), lambda w, j: (0, w * tiles + j))]
        + [piece_spec] * len(pieces),
        out_specs=pl.BlockSpec(out_shape, lambda w, j: (0, 0)),
        out_shape=jax.ShapeDtypeStruct(out_shape, jnp.float32),
        compiler_params=pltpu.CompilerParams(vmem_limit_bytes=40 << 20),
        cost_estimate=pl.CostEstimate(
            flops=2 * left.size * out_shape[1],
            bytes_accessed=2 * left.shape[1] * out_shape[1] + 4 * left.shape[0] * out_shape[1],
            transcendentals=0,
        ),
    )(left, *pieces)


def attention(projected, gains, tables, doc_ids, heads):
    length, width = projected.shape[0], projected.shape[1] // 3
    low, full = jnp.bfloat16, jnp.float32
    scale = HD ** (-0.5)

    def body(raw_ref, gain_ref, cos_ref, sin_ref, row_ref, col_ref,
             query_ref, key_ref, value_ref, out_ref, prob_ref, inv_ref, seen_ref):
        head = pl.program_id(0)

        @pl.when(head == 0)
        def _():
            for i in (0, 1):
                raw = raw_ref[:, i * width : (i + 1) * width]
                mean = jnp.mean(raw * raw, axis=-1, keepdims=True)
                inv_ref[:, i : i + 1] = lax.rsqrt(mean + EPS)
            at = lax.broadcasted_iota(jnp.int32, (length, length), 0)
            to = lax.broadcasted_iota(jnp.int32, (length, length), 1)
            seen = (row_ref[...] == col_ref[...]) & (at >= to)
            seen_ref[...] = jnp.where(seen, 1.0, 0.0)

        here = pl.multiple_of(head * HD, HD)

        def turned(i):
            raw = raw_ref[:, pl.ds(pl.multiple_of(i * width + head * HD, HD), HD)]
            value = raw * inv_ref[:, i : i + 1] * gain_ref[i + 1 : i + 2, pl.ds(here, HD)]
            return (value * cos_ref[...] + pltpu.roll(value, HD // 2, 1) * sin_ref[...]).astype(low)

        query, key = turned(0), turned(1)
        value = raw_ref[:, pl.ds(pl.multiple_of(2 * width + head * HD, HD), HD)].astype(low)
        scores = lax.dot_general(
            query, key, (((1,), (1,)), ((), ())), preferred_element_type=full
        ) * scale
        scores = jnp.where(seen_ref[...] > 0.0, scores, MASKED)
        expo = jnp.exp(scores - jnp.max(scores, axis=-1, keepdims=True))
        probs = expo / jnp.sum(expo, axis=-1, keepdims=True)
        prob_ref[0] = probs
        out_ref[...] = jnp.dot(probs.astype(low), value, preferred_element_type=full).astype(low)
        query_ref[...], key_ref[...], value_ref[...] = query, key, value

    def whole(shape):
        return pl.BlockSpec(shape, lambda h: (0,) * len(shape))

    part = pl.BlockSpec((length, HD), lambda h: (0, h))
    flat = jax.ShapeDtypeStruct((length, width), low)
    return pl.pallas_call(
        body,
        grid=(heads,),
        in_specs=[
            whole(projected.shape), whole(gains.shape), whole((length, HD)), whole((length, HD)),
            whole((length, 1)), whole((1, length)),
        ],
        out_specs=[part, part, part, part,
                   pl.BlockSpec((1, length, length), lambda h: (h, 0, 0)), whole((length, LANES))],
        out_shape=[flat, flat, flat, flat,
                   jax.ShapeDtypeStruct((heads, length, length), full),
                   jax.ShapeDtypeStruct((length, LANES), full)],
        scratch_shapes=[pltpu.VMEM((length, length), full)],
        compiler_params=pltpu.CompilerParams(vmem_limit_bytes=40 << 20),
        cost_estimate=pl.CostEstimate(
            flops=4 * heads * length * length * HD,
            bytes_accessed=4 * projected.size + 8 * length * width + 4 * heads * length * length,
            transcendentals=heads * length * length,
        ),
    )(projected, gains, *tables, doc_ids.reshape(length, 1), doc_ids.reshape(1, length))


def attention_back(grad_out, query, key, value, probs, projected, inverses, gains, tables, heads):
    length, width = grad_out.shape
    low, full = jnp.bfloat16, jnp.float32
    scale = HD ** (-0.5)

    def body(grad_ref, query_ref, key_ref, value_ref, prob_ref, raw_ref, inv_ref, gain_ref,
             cos_ref, sin_ref, dq_ref, dk_ref, dv_ref, dgain_ref, turned_ref, inner_ref):
        head = pl.program_id(0)
        here = pl.multiple_of(head * HD, HD)
        grad, probs = grad_ref[...], prob_ref[0]
        grad_probs = lax.dot_general(
            grad, value_ref[...], (((1,), (1,)), ((), ())), preferred_element_type=full
        )
        dv_ref[...] = lax.dot_general(
            probs.astype(low), grad, (((0,), (0,)), ((), ())), preferred_element_type=full
        ).astype(low)
        inner = jnp.sum(probs * grad_probs, axis=-1, keepdims=True)
        grad_scores = (probs * (grad_probs - inner)).astype(low)
        rotated = (
            jnp.dot(grad_scores, key_ref[...], preferred_element_type=full) * scale,
            lax.dot_general(
                grad_scores, query_ref[...], (((0,), (0,)), ((), ())), preferred_element_type=full
            ) * scale,
        )

        @pl.when(head == 0)
        def _():
            inner_ref[...] = jnp.zeros_like(inner_ref)

        for i in (0, 1):
            back = rotated[i] * cos_ref[...] - pltpu.roll(rotated[i], HD // 2, 1) * sin_ref[...]
            at = pl.ds(pl.multiple_of(i * width + head * HD, HD), HD)
            turned_ref[:, at] = back
            normed = raw_ref[:, at] * inv_ref[:, i : i + 1]
            dgain_ref[i : i + 1, pl.ds(here, HD)] = jnp.sum(back * normed, axis=0, keepdims=True)
            weighed = back * gain_ref[i + 1 : i + 2, pl.ds(here, HD)]
            inner_ref[:, i : i + 1] += jnp.sum(weighed * normed, axis=-1, keepdims=True)

        @pl.when(head == heads - 1)
        def _():
            for i, out_ref in ((0, dq_ref), (1, dk_ref)):
                inverse = inv_ref[:, i : i + 1]
                inner = inner_ref[:, i : i + 1] * (1.0 / width)

                @pl.loop(0, heads)
                def _(j):
                    at = pl.ds(pl.multiple_of(i * width + j * HD, HD), HD)
                    there = pl.ds(pl.multiple_of(j * HD, HD), HD)
                    weighed = turned_ref[:, at] * gain_ref[i + 1 : i + 2, there]
                    normed = raw_ref[:, at] * inverse
                    out_ref[:, there] = (inverse * (weighed - normed * inner)).astype(low)

    def whole(shape):
        return pl.BlockSpec(shape, lambda h: (0,) * len(shape))

    part = pl.BlockSpec((length, HD), lambda h: (0, h))
    flat = jax.ShapeDtypeStruct((length, width), low)
    return pl.pallas_call(
        body,
        grid=(heads,),
        in_specs=[
            part, part, part, part,
            pl.BlockSpec((1, length, length), lambda h: (h, 0, 0)),
            whole((length, 2 * width)), whole(inverses.shape), whole(gains.shape),
            whole((length, HD)), whole((length, HD)),
        ],
        out_specs=[whole((length, width)), whole((length, width)), part, whole((8, width))],
        out_shape=[flat, flat, flat, jax.ShapeDtypeStruct((8, width), full)],
        scratch_shapes=[pltpu.VMEM((length, 2 * width), full), pltpu.VMEM((length, LANES), full)],
        compiler_params=pltpu.CompilerParams(vmem_limit_bytes=40 << 20),
        cost_estimate=pl.CostEstimate(
            flops=8 * heads * length * length * HD,
            bytes_accessed=8 * length * width + 14 * length * width + 4 * heads * length * length,
            transcendentals=0,
        ),
    )(grad_out, query, key, value, probs, projected, inverses, gains, *tables)


BESIDE = pl.CostEstimate(flops=1, bytes_accessed=1, transcendentals=0)


def expert_back(cot, gate, result, pre_gate, pre_up, gate_w, up_w, down_w, own):
    total, width = cot.shape
    rows = min(512, total)
    hidden = pre_gate.shape[1]
    low, full = jnp.bfloat16, jnp.float32
    tile = min(512, hidden)

    def body(own_ref, cot_ref, gate_ref, result_ref, a_ref, b_ref, gate_w_ref, up_w_ref, down_w_ref,
             back_ref, grad_y_ref, grad_a_ref, grad_b_ref, sum_ref):
        step = pl.program_id(1)

        @pl.when(step == 0)
        def _():
            cot_f = cot_ref[...].astype(full)
            grad_y_ref[...] = (gate_ref[...] * cot_f).astype(low)
            grad_g = jnp.sum(cot_f * result_ref[...].astype(full), axis=-1, keepdims=True)
            high = grad_g.astype(low).astype(full)
            lanes = lax.broadcasted_iota(jnp.int32, (rows, LANES), 1)
            tail = jnp.where(lanes == own_ref[0], high, 0.0)
            tail = jnp.where(lanes == own_ref[0] + LANES // 2, grad_g - high, tail)
            back_ref[:, width:] = tail.astype(low)
            sum_ref[...] = jnp.zeros_like(sum_ref)

        grad_act = lax.dot_general(
            grad_y_ref[...], down_w_ref[...], (((1,), (1,)), ((), ())), preferred_element_type=full
        )
        pre_gate, pre_up = a_ref[...], b_ref[...]
        sigmoid_g = jax.nn.sigmoid(pre_gate)
        slope = sigmoid_g * (1.0 + pre_gate * (1.0 - sigmoid_g))
        grad_a = (grad_act * pre_up * slope).astype(low)
        grad_b = (grad_act * (pre_gate * sigmoid_g)).astype(low)
        grad_a_ref[...], grad_b_ref[...] = grad_a, grad_b
        contract = (((1,), (1,)), ((), ()))
        sum_ref[...] += lax.dot_general(
            grad_a, gate_w_ref[...], contract, preferred_element_type=full
        ) + lax.dot_general(grad_b, up_w_ref[...], contract, preferred_element_type=full)

        @pl.when(step == hidden // tile - 1)
        def _():
            back_ref[:, :width] = sum_ref[...].astype(low)

    def whole(columns):
        return pl.BlockSpec((rows, columns), lambda r, f: (r, 0))

    inner = pl.BlockSpec((rows, tile), lambda r, f: (r, f))
    into = pl.BlockSpec((width, tile), lambda r, f: (0, f))
    return pl.pallas_call(
        body,
        grid=(total // rows, hidden // tile),
        in_specs=[
            pl.BlockSpec(memory_space=pltpu.SMEM),
            whole(width), whole(1), whole(width), inner, inner, into, into,
            pl.BlockSpec((tile, width), lambda r, f: (f, 0)),
        ],
        out_specs=[whole(width + LANES), whole(width), inner, inner],
        out_shape=[
            jax.ShapeDtypeStruct((total, width + LANES), low),
            jax.ShapeDtypeStruct(cot.shape, low),
            jax.ShapeDtypeStruct(pre_gate.shape, low),
            jax.ShapeDtypeStruct(pre_gate.shape, low),
        ],
        scratch_shapes=[pltpu.VMEM((rows, width), full)],
        compiler_params=pltpu.CompilerParams(vmem_limit_bytes=52 << 20),
        cost_estimate=BESIDE,
    )(own.reshape(1), cot, gate, result, pre_gate, pre_up, gate_w, up_w, down_w)


def rows_product(lefts, rights):
    rows, height = lefts[0].shape
    width = rights[0].shape[1]
    tile = min(512, height)

    def body(*refs):
        out_ref = refs[-1]
        total = None
        for left_ref, right_ref in zip(refs[: len(lefts)], refs[len(lefts) : -1], strict=True):
            term = lax.dot_general(
                left_ref[...], right_ref[...], (((0,), (0,)), ((), ())),
                preferred_element_type=jnp.float32,
            )
            total = term if total is None else total + term
        out_ref[...] = total

    return pl.pallas_call(
        body,
        grid=(height // tile,),
        in_specs=[pl.BlockSpec((rows, tile), lambda i: (0, i))] * len(lefts)
        + [pl.BlockSpec((rows, width), lambda i: (0, 0))] * len(rights),
        out_specs=pl.BlockSpec((tile, width), lambda i: (i, 0)),
        out_shape=jax.ShapeDtypeStruct((height, width), jnp.float32),
        compiler_params=pltpu.CompilerParams(vmem_limit_bytes=52 << 20),
        cost_estimate=BESIDE,
    )(*lefts, *rights)


def rope_tables(length):
    half = HD // 2
    freq = THETA ** (-(jnp.arange(half, dtype=jnp.float32) * 2.0) / HD)
    angle = jnp.arange(length, dtype=jnp.float32)[:, None] * freq[None, :]
    sine = jnp.sin(angle)
    cosine = jnp.cos(angle)
    return (
        jnp.concatenate([cosine, cosine], axis=-1),
        jnp.concatenate([-sine, sine], axis=-1),
    )


def on_device(
    tokens,
    segments,
    expert_ids,
    norm_gains,
    w_query,
    w_key,
    w_value,
    w_out,
    w_router,
    expert_gate,
    expert_up,
    expert_down,
    cotangent,
):
    bfloat = jnp.bfloat16
    here = Places()
    length, width = tokens.shape
    topk = expert_ids.shape[1]
    experts = here.count
    capacity = length * topk // experts
    heads = width // HD
    shard = w_query.shape[0]
    plane = here.plane
    gate_w, up_w, down_w = expert_gate[0], expert_up[0], expert_down[0]

    labels = jnp.arange(experts, dtype=jnp.int32)
    named = jnp.any(expert_ids[:, :, None] == labels[None, None, :], axis=1)
    places = jnp.arange(length, dtype=jnp.int32)
    earlier = (places[:, None] < places[None, :]).astype(bfloat)
    slots = contract_rows(named.astype(bfloat), earlier)
    slots = jnp.where(named.T & (slots < capacity), slots, -1.0).astype(bfloat)

    order = range(here.nz)
    arrival = here.arrival(width)
    extra = norm_gains.shape[0] + w_router.shape[1]
    smalls = jnp.concatenate(
        [norm_gains.T, w_router, jnp.zeros((shard, -extra % LANES), jnp.float32)], axis=1
    ).astype(bfloat)
    smalls = jnp.concatenate([smalls, slots.reshape(-1, LANES)], axis=0)
    smalls = here.along_whole_line([smalls] * here.nz)
    plane_expert = jnp.stack(
        [
            here.at(here.z, (here.y + dy) % here.ny, (here.x + dx) % here.nx)
            for dy, dx in here.steps
        ]
    )
    chosen = plane_expert[:, None] == labels[None, :]
    slot_ids = jnp.arange(capacity, dtype=jnp.int32)
    spreads = []

    def spread_of(part):
        picked = jnp.sum(
            jnp.where(chosen[:, :, None], part[None].astype(jnp.float32), 0.0), axis=1
        ).astype(jnp.int32)
        hit = picked[:, None, :] == slot_ids[None, :, None]
        return hit.astype(bfloat).reshape(plane * capacity, length)

    def rows_of(spread, part):
        return list(product(spread, part).astype(bfloat).reshape(plane, capacity, -1))

    def parted(rows):
        return list(rows.reshape(plane, capacity, -1))

    def joined(rows):
        return jnp.concatenate(rows, axis=0)

    inputs = tokens.astype(jnp.float32)
    weights = jnp.stack([w_query, w_key, w_value, w_out]).astype(bfloat)
    line, cot_line = Spread(here, weights), Spread(here, cotangent)
    half = weights.shape[0] // 2
    raw, chunks, pieces = [], [], []
    projected = None
    depth = width // here.nz
    cot_rows, rows_cot = [None] * here.nz, [None] * here.nz

    def stacked(rows):
        return rows.reshape(-1, shard, width)

    def chunk_of(k):
        if here.square:
            at = 2 * half if k + 1 < here.nz else 0
            blocks = [line.queue[k]] + [by[: 2 * half] for by in raw[k][:2]]
            blocks += [by[at : at + half] for by in raw[k + 1][:2]]
        else:
            blocks = raw[k]
        return jnp.concatenate(blocks, axis=0).reshape(plane, *weights.shape)

    def share(chunk):
        return [chunk] + [here.other_core(chunk, s) for s in range(1, here.cores)]

    def project(k):
        return times_gathered(
            in_order[:, k * depth : (k + 1) * depth], pieces[k], 0, 3, projected
        )

    for k in range(here.nz + 2):
        outs = []
        if here.square:
            by_x, by_y = [], []
            if k < here.nz:
                by_x.append(line.queue[k])
                by_y.append(line.queue[k])
            if 0 < k <= here.nz:
                by_x.append(raw[k - 1][1][:half])
                by_y.append(raw[k - 1][0][half : 2 * half])
            if k >= here.nz:
                by_x.append(stacked(cot_rows[k - here.nz][1]))
                by_y.append(stacked(cot_rows[k - here.nz][2]))
            outs = [jnp.concatenate(by_x, axis=0), jnp.concatenate(by_y, axis=0)]
            if k > here.nz:
                outs.append(jnp.concatenate([cot_rows[0][3], cot_rows[1][3]], axis=0))
        elif k < here.nz:
            outs = [line.queue[k]] * plane
        else:
            outs = cot_rows[k - here.nz]
        if k == 1:
            outs, smalls, raw, line.queue = tie(outs, smalls, raw, line.queue)
            turned = jnp.stack(smalls).reshape(here.nz, -1)
            near = (here.z - here.queue_of(jnp.arange(here.nz))) % here.nz
            pick = (near[:, None] == jnp.arange(here.nz)[None, :]).astype(bfloat)
            turned = product(pick, turned).astype(bfloat).reshape(here.nz, -1, LANES)
            smalls, slots = turned[:, :shard], turned[:, shard:]
            smalls = here.along_plane([smalls] * plane)
        outs, smalls, slots, raw, chunks, line.queue, cot_line.queue, cot_rows, cotangent = tie(
            outs, smalls, slots, raw, chunks, line.queue, cot_line.queue, cot_rows, cotangent
        )
        if here.square:
            ins = [here.shift_plane(outs[0], 0, 1), here.shift_plane(outs[1], 1, 0)]
            if k > here.nz:
                ins.append(here.shift_plane(outs[2], 1, 1))
        else:
            ins = here.along_plane(outs)
        moving = line.step() if k < here.nz else []
        moving_cot = cot_line.step() if k >= here.nz - 1 else []
        if k == 1:
            spreads = [spread_of(part.reshape(experts, length)) for part in slots]
        if k > 2:
            pieces.append(share(chunks[k - 3]))
        if k > 1:
            chunks.append(chunk_of(k - 2))
        if k == 2:
            smalls = jnp.stack(smalls, axis=1)
            smalls = [smalls] + [here.other_core(smalls, s) for s in range(1, here.cores)]
            smalls = jnp.stack(smalls, axis=1).reshape(width, -1)
        if k == 3:
            smalls = product(arrival, smalls).astype(bfloat)
            gains_f = smalls[:, : norm_gains.shape[0]].T.astype(jnp.float32)
            wr = smalls[:, norm_gains.shape[0] : extra]
            normed_in_f, normed_one, inverse_one = norm_rows(inputs, gains_f[0])
            normed_in = normed_in_f.astype(bfloat)
            in_order = product(normed_in, arrival).astype(bfloat)
        if k > 2:
            projected = project(k - 3)
        if k == 1:
            both_w = jnp.concatenate([gate_w, up_w], axis=1)
            spreads, both_w = tie(spreads, both_w)
        if k >= here.nz - 1 and k - here.nz + 1 < here.nz:
            at = k - here.nz + 1
            cot_rows[at] = rows_of(spreads[at], cot_line.queue[at])
        ins, moving, moving_cot, smalls, projected, cot_rows, spreads, chunks = tie(
            ins, moving, moving_cot, smalls, projected, cot_rows, spreads, chunks
        )
        line.land(moving)
        cot_line.land(moving_cot)
        raw.append(ins)
        if k >= here.nz:
            rows_cot[k - here.nz] = ins
            if here.square:
                own = cot_rows[k - here.nz][0]
                skip = half if k == here.nz else 0
                rows_cot[k - here.nz] = [own] + [by[skip:].reshape(own.shape) for by in ins[:2]]
            if here.square and k > here.nz:
                for i in (0, 1):
                    rows_cot[i].append(ins[2][i * capacity : (i + 1) * capacity])

    order_x = here.target_order(width // here.cores, "x")
    order_y = here.target_order(width // here.cores, "y")

    def targeted(columns):
        columns = jnp.concatenate(columns, axis=0)
        return [product(columns, o).astype(bfloat) for o in (order_x, order_y)]

    merged = []
    if here.nz > 2:
        cot_rows[3] = rows_of(spreads[3], cot_line.queue[3])
        merged = [joined(pair) for pair in zip(*cot_rows[2:], strict=True)]
    in_columns = here.core_columns(normed_in)
    merged, chunks, projected, pieces, in_columns = tie(
        merged, chunks, projected, pieces, in_columns
    )
    ins = here.along_plane(merged) if merged else []
    pieces.append(share(chunks[-1]))
    in_columns = here.to_cores(in_columns)
    projected = project(here.nz - 1)
    pieces = [piece for chunk in pieces for piece in chunk]
    tables = rope_tables(length)
    query_rot, key_rot, values, attended, probs, inverses = attention(
        projected, gains_f, tables, segments[0], heads
    )
    residual = inputs + times_gathered(product(attended, arrival).astype(bfloat), pieces, 3, 4)
    normed_mid_f, normed_two, inverse_two = norm_rows(residual, gains_f[3])
    normed_mid = normed_mid_f.astype(bfloat)

    own_label = labels[None, :] == here.me

    def expert_forward(arrived):
        route_here = jax.nn.softmax(product(arrived, wr), axis=-1)
        gate = jnp.sum(jnp.where(own_label, route_here, 0.0), axis=-1)
        gate = gate.astype(bfloat).astype(jnp.float32)[:, None]
        pre_gate = product(arrived, gate_w)
        pre_up = product(arrived, up_w)
        activated = (jax.nn.silu(pre_gate) * pre_up).astype(bfloat)
        result = product(activated, down_w).astype(bfloat)
        gated = (gate * result.astype(jnp.float32)).astype(bfloat)
        return (gate, pre_gate, pre_up, activated, result, gated)

    def expert_backward(kept, cot):
        gate, pre_gate, pre_up, _, result, _ = kept
        return expert_back(cot, gate, result, pre_gate, pre_up, gate_w, up_w, down_w, here.me)

    rows_next = rows_of(spreads[0], normed_mid)
    out_columns = here.core_columns(attended)
    normed_mid, rows_next, ins, in_columns, out_columns = tie(
        normed_mid, rows_next, ins, in_columns, out_columns
    )
    if here.nz > 2:
        rows_cot[2:] = [[row[i : i + capacity] for row in ins] for i in (0, capacity)]
    line = Spread(here, normed_mid)
    rows_in, forward = [], []
    for k in order:
        if k > 0:
            rows_next = rows_of(spreads[k], line.queue[k])
        rows_next, rows_in, line.queue, out_columns = tie(
            rows_next, rows_in, line.queue, out_columns
        )
        moving = line.step()
        rows = here.along_plane(rows_next)
        if k > 0:
            rows_in[-1] = joined(rows_in[-1])
            forward.append(expert_forward(rows_in[-1]))
        if k == 0:
            targets = targeted(in_columns)
            rows, targets = tie(rows, targets)
        if k == here.nz // 2:
            out_columns = here.to_cores(out_columns)
        moving, rows, forward, out_columns = tie(moving, rows, forward, out_columns)
        rows_in.append(rows)
        line.land(moving)

    targets_out = targeted(out_columns)
    half = here.nz // 2
    back_y = [None] * here.nz
    backward = [None] * here.nz
    todo = ["forward", *reversed(order)]

    def work():
        k = todo.pop(0) if todo else None
        if k == "forward":
            rows_in[-1] = joined(rows_in[-1])
            forward.append(expert_forward(rows_in[-1]))
        elif k is not None:
            backward[k] = expert_backward(forward[k], joined(rows_cot[k]))

    rows_next = parted(forward[0][5])
    rows_next, forward, rows_in, rows_cot, out_columns = tie(
        rows_next, forward, rows_in, rows_cot, out_columns
    )
    rows = here.deal_back(rows_next)
    work()
    work()
    rows, forward, backward = tie(rows, forward, backward)
    back_y[0] = rows
    collect, parts = Collect(here), [None] * here.nz
    moving, sending, back = [], [], None
    for k in reversed(order):
        rows_next = parted(backward[k][0])
        if k + 2 < here.nz:
            collect.land(moving)
            sending = collect.add(k + 2, parts[k + 2])
        rows_next, sending, forward, backward, back = tie(
            rows_next, sending, forward, backward, back
        )
        rows = here.deal_back(rows_next)
        moving = collect.send(sending)
        if k > 0:
            work()
        else:
            grad_down = rows_product(
                [kept[3] for kept in forward], [kept[1] for kept in backward]
            )
            rows, grad_down = tie(rows, grad_down)
        if back is not None:
            parts[k + 1] = contract_rows(spreads[k + 1], joined(back))
        moving, rows, forward, backward, parts = tie(moving, rows, forward, backward, parts)
        back = rows
    late = list(order[:0:-1])
    collect.land(moving)
    sending = collect.add(1, parts[1])
    rows_next = parted(forward[late[0]][5])
    rows_next, sending, back = tie(rows_next, sending, back)
    rows = here.deal_back(rows_next)
    moving = collect.send(sending)
    parts[0] = contract_rows(spreads[0], joined(back))
    rows_next = [parted(forward[k][5]) for k in late[1:]]
    moving, rows, parts, rows_next = tie(moving, rows, parts, rows_next)
    collect.land(moving)
    collect.add(0, parts[0])
    returned = collect.total
    back_y[late[0]] = rows
    parts_y = [None] * here.nz
    if rows_next:
        back_y[late[1]] = here.deal_back(rows_next[0])

    def add_up_y(k):
        parts_y[k] = contract_rows(spreads[k], joined(back_y[k]))

    add_up_y(late[0])

    grad_mid = returned[:, :width]
    grad_route = (
        returned[:, width : width + experts]
        + returned[:, width + LANES // 2 : width + LANES // 2 + experts]
    )
    route = jax.nn.softmax(product(normed_mid, wr), axis=-1)
    grad_logits = (
        route * (grad_route - jnp.sum(route * grad_route, axis=-1, keepdims=True))
    ).astype(bfloat)
    grad_router = contract_rows(normed_mid, grad_logits)
    grad_mid = grad_mid + contract_cols(grad_logits, wr)
    grad_res_two, grad_gain_mid = norm_back(grad_mid, gains_f[3], normed_two, inverse_two)
    grad_residual = cotangent.astype(jnp.float32) + grad_res_two
    grad_attn = grad_residual.astype(bfloat)
    grad_attended = times_transposed(grad_attn, pieces, 3, 4).astype(bfloat)
    grad_attended = contract_cols(grad_attended, arrival).astype(bfloat)
    collect_y, adds_y = Collect(here), list(reversed(order))
    grad_attended, grad_attn, back_y, parts_y = tie(grad_attended, grad_attn, back_y, parts_y)
    sending_y = collect_y.add(adds_y[0], parts_y[adds_y.pop(0)])
    sending_y, grad_attended, grad_attn, back_y, rows_next = tie(
        sending_y, grad_attended, grad_attn, back_y, rows_next
    )
    if rows_next:
        back_y[late[2]] = here.deal_back(rows_next[1])
    moving = collect_y.send(sending_y)
    out_tokens = here.all_tokens(grad_attn)
    grad_query, grad_key, grad_values, grad_gain_heads = attention_back(
        grad_attended, query_rot, key_rot, values, probs, projected, inverses, gains_f, tables, heads
    )
    far = here.scatter_far(*targets_out, out_tokens)
    grads = jnp.stack([grad_values, grad_key, grad_query])
    for k in [0, *late[1:2]]:
        add_up_y(k)
    grads, far, back_y, parts_y, moving, out_tokens = tie(
        grads, far, back_y, parts_y, moving, out_tokens
    )

    def leave(far, sums, more_x, more_y):
        if not here.square:
            return list(far)
        by_x, by_y = list(far[:1]), list(far[1:])
        if sums:
            by_x.append(sums[1])
            by_y.append(sums[0])
        return [jnp.concatenate(by_x + more_x, axis=0), jnp.concatenate(by_y + more_y, axis=0)]

    def arrive(outs):
        if not here.square:
            return here.along_plane(outs) if outs else []
        return [here.shift_plane(outs[0], 0, 1), here.shift_plane(outs[1], 1, 0)]

    jobs = 4
    lefts, rights = [targets_out, targets, targets, targets], [out_tokens]
    firsts, lasts, shares = [], [], []
    near, near_last, ins, small, smalls, expert_grads = [], [], [], [None], [], []
    for i in range(jobs + 2):
        if here.square and i > 0:
            by_x, by_y = ins
            if i <= jobs:
                rows = near[0].shape[0]
                firsts.append([by_x[:rows], by_y[:rows], *near])
                by_x, by_y = by_x[rows:], by_y[rows:]
            if i > 1:
                rows = near_last[0].shape[0]
                lasts.append([by_y[:rows], by_x[:rows], *near_last])
                by_x, by_y = by_x[rows:], by_y[rows:]
        elif 0 < i <= jobs:
            lasts.append(ins)
        sums, parts, more_x, more_y, outs = [], [], [], [], []
        if here.square:
            sums = here.scatter_sums(firsts[i - 1]) if 0 < i <= jobs else []
            near_last = sums[2:]
            columns = small[0].shape[1] // 2 if small[0] is not None else 0
            if i == 2:
                more_x = [small[0][:, columns:].astype(bfloat).reshape(-1, width // 2)]
                small = [small[0][:, :columns]]
            elif i == 3:
                small = [small[0] + by_x.reshape(small[0].shape).astype(jnp.float32)]
                more_y = [small[0][:, columns:].astype(bfloat).reshape(-1, width // 2)]
                small = [small[0][:, :columns]]
            elif i == 4:
                small = [small[0] + by_y.reshape(small[0].shape).astype(jnp.float32)]
            if i < jobs:
                outs = leave(far, sums, more_x, more_y)
            elif i == jobs:
                outs = [sums[1], sums[0]]
        elif i < jobs:
            outs = leave(far, [], [], [])
        at = i - 2 if here.square else i - 1
        if 0 <= at < jobs:
            parts = here.line_parts(lasts[at])
            if here.square and i == 4:
                parts = [
                    jnp.concatenate([part, piece.reshape(-1, width).astype(part.dtype)], axis=0)
                    for part, piece in zip(
                        parts, jnp.split(small[0], here.nz, axis=1), strict=True
                    )
                ]
        sending_y = []
        if adds_y:
            collect_y.land(moving)
            sending_y = collect_y.add(adds_y[0], parts_y[adds_y.pop(0)])
        outs, parts, sending_y, near_last, small, rights, smalls, grads, back_y, rows_in = tie(
            outs, parts, sending_y, near_last, small, rights, smalls, grads, back_y, rows_in
        )
        ins = arrive(outs) if outs else []
        if parts:
            parts = here.along_whole_line(parts)
        moving = collect_y.send(sending_y) if sending_y else []
        if here.square and i == 5:
            smalls = here.to_cores(smalls)
        if i < jobs:
            near = here.scatter_near(*lefts[i], rights[i])
        if i == 0:
            others = [here.other_core(grads, step) for step in range(1, here.cores)]
            rights += [jnp.concatenate([v[j] for v in [grads, *others]], axis=0) for j in range(3)]
        if i + 1 < jobs:
            far = here.scatter_far(*lefts[i + 1], rights[i + 1])
        if i == 0:
            grad_in_norm = times_transposed(
                jnp.concatenate([grads[2], grads[1], grads[0]], axis=1), pieces, 0, 3
            )
            high = grad_in_norm.astype(bfloat)
            low = (grad_in_norm - high.astype(jnp.float32)).astype(bfloat)
            high, low, ins = tie(high, low, ins)
        if i == 1:
            grad_in_norm = contract_cols(high, arrival) + contract_cols(low, arrival)
            grad_res_one, grad_gain_in = norm_back(
                grad_in_norm, gains_f[0], normed_one, inverse_one
            )
            grad_tokens = (grad_residual + grad_res_one).astype(bfloat)
            small_rows = 4 + experts
            smalls = jnp.concatenate(
                [
                    grad_gain_in[None],
                    grad_gain_heads[:2],
                    grad_gain_mid[None],
                    grad_router.T,
                    jnp.zeros((-small_rows % 32, width), jnp.float32),
                ],
                axis=0,
            )
            if here.square:
                smalls = jnp.concatenate(here.core_columns(smalls), axis=0)
                small = [product(smalls.astype(bfloat), order_x)]
            grad_tokens, small, smalls, ins = tie(grad_tokens, small, smalls, ins)
        if i == 0 and len(late) > 2:
            add_up_y(late[2])
        if 2 <= i <= 3:
            grad = rows_product(rows_in, [kept[i] for kept in backward])
            expert_grads.append(grad)
            ins, expert_grads = tie(ins, expert_grads)
        ins, parts, moving, far, near, rights, smalls, parts_y = tie(
            ins, parts, moving, far, near, rights, smalls, parts_y
        )
        if parts:
            share = sum(part.astype(jnp.float32) for part in parts)
            if here.square and i == 4:
                smalls = jnp.split(share[shard:].reshape(-1, shard), here.cores, axis=0)
            shares.append(share[:shard])
    if here.square:
        smalls = sum(smalls)
    else:
        smalls = lax.psum(smalls, ("dp", "expert"))
        smalls = lax.dynamic_slice(
            smalls, (0, (here.core * here.count + here.me) * shard), (smalls.shape[0], shard)
        )
    mixed = (residual + collect_y.total).astype(bfloat)
    grad_wo, grad_wv, grad_wk, grad_wq = shares
    grad_gate_w, grad_up_w = expert_grads
    return (
        mixed,
        grad_tokens,
        smalls[:4],
        grad_wq,
        grad_wk,
        grad_wv,
        grad_wo,
        smalls[4:small_rows].T,
        grad_gate_w[None, None],
        grad_up_w[None, None],
        grad_down[None, None],
    )


def solution(mesh):
    return jax.shard_map(
        on_device,
        mesh=mesh,
        in_specs=(
            P(("dp", "expert"), None),
            P(("dp", "expert"), None),
            P(("dp", "expert"), None),
            P(None, ("dp", "expert")),
            P(("dp", "expert"), None),
            P(("dp", "expert"), None),
            P(("dp", "expert"), None),
            P(("dp", "expert"), None),
            P(("dp", "expert"), None),
            P("expert", None, None),
            P("expert", None, None),
            P("expert", None, None),
            P(("dp", "expert"), None),
        ),
        out_specs=(
            P(("dp", "expert"), None),
            P(("dp", "expert"), None),
            P(None, ("dp", "expert")),
            P(("dp", "expert"), None),
            P(("dp", "expert"), None),
            P(("dp", "expert"), None),
            P(("dp", "expert"), None),
            P(("dp", "expert"), None),
            P("dp", "expert", None, None),
            P("dp", "expert", None, None),
            P("dp", "expert", None, None),
        ),
        check_vma=False,
    )
```

```python
import jax
import jax.numpy as jnp
from jax import lax
from jax.experimental import pallas as pl
from jax.experimental.pallas import tpu as pltpu
from jax.sharding import PartitionSpec as P

HD = 128


EPS = 1e-05
THETA = 10000.0
MASKED = -1e30
LANES = 128


def norm_rows(value, gain):
    inverse = lax.rsqrt(jnp.mean(value * value, axis=-1, keepdims=True) + EPS)
    normed = value * inverse
    return (normed * gain, normed, inverse)


def norm_back(grad_in, gain, normed, inverse):
    grad_normed = grad_in * gain
    grad_gain = jnp.sum(grad_in * normed, axis=0)
    inner = jnp.mean(grad_normed * normed, axis=-1, keepdims=True)
    return (inverse * (grad_normed - normed * inner), grad_gain)


def contract_rows(left, right):
    return lax.dot_general(
        left, right, (((0,), (0,)), ((), ())), preferred_element_type=jnp.float32
    )


def contract_cols(left, right):
    return lax.dot_general(
        left, right, (((1,), (1,)), ((), ())), preferred_element_type=jnp.float32
    )


def product(left, right):
    return jnp.dot(left, right, preferred_element_type=jnp.float32)


def tie(*values):
    return lax.optimization_barrier(values)


class Spread:
    def __init__(self, here, own):
        self.here, self.queue, self.done = here, [own], 0

    def step(self):
        here, own = self.here, self.queue[0]
        self.done += 1
        if self.done >= here.nz:
            return []
        if here.nz != 4:
            moves = [(a, (a + self.done) % here.nz) for a in range(here.nz)]
            return [here.along_line(own, moves)]
        if self.done == 1:
            return [
                here.along_line(own, [(0, 1), (1, 0), (2, 3), (3, 2)]),
                here.along_line(own, [(1, 2), (2, 1)]),
            ]
        if self.done == 2:
            return [
                here.along_line(self.middle, [(1, 0), (2, 3)]),
                here.along_line(self.queue[1], [(1, 2), (2, 1)]),
            ]
        return [here.along_line(self.across, [(1, 0), (2, 3)])]

    def land(self, arrays):
        here = self.here
        if not arrays:
            return
        if here.nz != 4:
            self.queue += arrays
            return
        inner = (here.z == 1) | (here.z == 2)
        if self.done == 1:
            one, self.middle = arrays
            self.queue.append(one)
        elif self.done == 2:
            edge, self.across = arrays
            self.queue.append(jnp.where(inner, self.middle, edge))
        else:
            self.queue.append(jnp.where(inner, self.across, arrays[0]))

    def finish(self):
        while len(self.queue) < self.here.nz:
            self.land(self.step())
        return self.queue


class Collect:
    def __init__(self, here):
        self.here, self.came, self.moves = here, [], []

    def add(self, k, part):
        here = self.here
        if k == 0:
            self.total = part
            for value in self.came:
                self.total = self.total + value
            return []
        if here.nz != 4:
            out = [(part, [(a, (a - k) % here.nz) for a in range(here.nz)])]
        elif k == 3:
            self.three = part
            out = [(part, [(0, 1), (3, 2)])]
        elif k == 2:
            self.two = part
            (edge,) = self.came
            out = [(self.three + edge, [(1, 2), (2, 1)]), (part, [(0, 1), (3, 2)])]
        else:
            across, edge = self.came
            out = [
                (part + across, [(0, 1), (1, 0), (2, 3), (3, 2)]),
                (self.two + edge, [(1, 2), (2, 1)]),
            ]
        self.moves = [moves for _, moves in out]
        return [value.astype(jnp.bfloat16) for value, _ in out]

    def send(self, values):
        return [self.here.along_line(v, m) for v, m in zip(values, self.moves, strict=True)]

    def land(self, arrays):
        came = [value.astype(jnp.float32) for value in arrays]
        self.came = came if self.here.nz == 4 else self.came + came
        self.moves = []


def grid_of(count):
    if count % 32 == 0:
        return (count // 16, 4, 4)
    if count % 4 == 0:
        return (count // 4, 2, 2)
    return (count, 1, 1)


class Places:
    def __init__(self):
        self.count = lax.axis_size("expert")
        self.cores = lax.axis_size("dp")
        self.nz, self.ny, self.nx = grid_of(self.count)
        self.plane = self.ny * self.nx
        self.me = lax.axis_index("expert")
        self.core = lax.axis_index("dp")
        self.z = self.me // self.plane
        self.y = (self.me // self.nx) % self.ny
        self.x = self.me % self.nx
        self.steps = [(dy, dx) for dy in range(self.ny) for dx in range(self.nx)]
        self.square = (self.ny, self.nx) == (2, 2)
        if self.nz == 4:
            self.queue = [[0, 1, 2, 3], [1, 0, 2, 3], [2, 3, 1, 0], [3, 2, 1, 0]]
        else:
            self.queue = [[(z - k) % self.nz for k in range(self.nz)] for z in range(self.nz)]

    def at(self, z, y, x):
        return (z * self.ny + y) * self.nx + x

    def shift_plane(self, value, dy, dx):
        pairs = [
            (self.at(z, y, x), self.at(z, (y + dy) % self.ny, (x + dx) % self.nx))
            for z in range(self.nz)
            for y in range(self.ny)
            for x in range(self.nx)
        ]
        return lax.ppermute(value, "expert", pairs)

    def along_line(self, value, moves):
        pairs = [
            (self.at(a, y, x), self.at(b, y, x))
            for a, b in moves
            for y in range(self.ny)
            for x in range(self.nx)
        ]
        return lax.ppermute(value, "expert", pairs)

    def other_core(self, value, step):
        pairs = [(c, (c + step) % self.cores) for c in range(self.cores)]
        return lax.ppermute(value, "dp", pairs)

    def arrival(self, rows):
        shard = rows // (self.cores * self.count)
        order = jnp.arange(rows, dtype=jnp.int32)
        inside, rest = order % shard, order // shard
        step, rest = rest % self.plane, rest // self.plane
        core, k = rest % self.cores, rest // self.cores
        zed = self.queue_of(k)
        y = (self.y - step // self.nx) % self.ny
        x = (self.x - step % self.nx) % self.nx
        core = (self.core - core) % self.cores
        source = (core * self.count + self.at(zed, y, x)) * shard + inside
        return (order[:, None] == source[None, :]).astype(jnp.bfloat16), source[None, :]

    def queue_of(self, k):
        table = jnp.asarray(self.queue, jnp.int32)[self.z]
        zed = jnp.zeros_like(k)
        for q in range(self.nz):
            zed = jnp.where(k == q, table[q], zed)
        return zed

    def deal(self, rows):
        return [
            rows[i] if s == (0, 0) else self.shift_plane(rows[i], *s)
            for i, s in enumerate(self.steps)
        ]

    def deal_back(self, rows):
        return [
            rows[i] if s == (0, 0) else self.shift_plane(rows[i], -s[0], -s[1])
            for i, s in enumerate(self.steps)
        ]

    def along_plane(self, values):
        return [
            v if s == (0, 0) else self.shift_plane(v, *s)
            for v, s in zip(values, self.steps, strict=True)
        ]

    def along_whole_line(self, parts):
        return [
            part
            if k == 0
            else self.along_line(part, [(a, (a + k) % self.nz) for a in range(self.nz)])
            for k, part in enumerate(parts)
        ]

    def target_order(self, width, lead):
        shard = width // self.count
        order = jnp.arange(width, dtype=jnp.int32)
        inside, rest = order % shard, order // shard
        k, rest = rest % self.nz, rest // self.nz
        if lead == "x":
            dy, dx = rest % self.ny, rest // self.ny
        else:
            dx, dy = rest % self.nx, rest // self.nx
        y, x = (self.y + dy) % self.ny, (self.x + dx) % self.nx
        source = self.at((self.z + k) % self.nz, y, x) * shard + inside
        return (order[:, None] == source[None, :]).astype(jnp.bfloat16)

    def scatter_far(self, by_x, by_y, right):
        wire = jnp.bfloat16
        if not self.square:
            line = by_x.shape[1] // self.plane
            starts = [(dx * self.ny + dy) * line for dy, dx in self.steps]
            parts = [contract_rows(by_x[:, start : start + line], right) for start in starts]
            return parts[:1] + [part.astype(wire) for part in parts[1:]]
        half, far = right.shape[1] // 2, by_x.shape[1] // 2
        return [
            contract_rows(by_x[:, far:], right[:, :half]).astype(wire),
            contract_rows(by_y[:, far:], right[:, half:]).astype(wire),
        ]

    def scatter_near(self, by_x, by_y, right):
        if not self.square:
            return []
        half, far = right.shape[1] // 2, by_x.shape[1] // 2
        return [
            contract_rows(by_x[:, :far], right[:, :half]),
            contract_rows(by_y[:, :far], right[:, half:]),
        ]

    def rows_first(self, width):
        return width // self.cores // self.nx

    def line_parts(self, terms):
        full = jnp.float32
        if not self.square:
            total = sum(t.astype(full) for t in terms)
        else:
            from_y, from_x, near_x, near_y = terms
            total = jnp.concatenate(
                [near_x + from_y.astype(full), near_y + from_x.astype(full)], axis=1
            )
        shard = total.shape[0] // self.nz
        parts = [total[k * shard : (k + 1) * shard] for k in range(self.nz)]
        return parts[:1] + [part.astype(jnp.bfloat16) for part in parts[1:]]

    def all_tokens(self, value):
        return jnp.concatenate(
            [value] + [self.other_core(value, step) for step in range(1, self.cores)], axis=0
        )

    def core_columns(self, value):
        width = value.shape[1] // self.cores
        starts = [((self.core + step) % self.cores) * width for step in range(self.cores)]
        return [lax.dynamic_slice(value, (0, start), (value.shape[0], width)) for start in starts]

    def to_cores(self, pieces):
        return [
            piece if step == 0 else self.other_core(piece, step)
            for step, piece in enumerate(pieces)
        ]


COLUMNS = 1024
BESIDE = pl.CostEstimate(flops=1, bytes_accessed=1, transcendentals=0)


def fold(came, near, far, more):
    rows, width = near[0].shape
    line = rows // 2
    ahead = rows if far else 0
    extra = [m.shape[0] if m is not None else 0 for m in more]
    low, full = jnp.bfloat16, jnp.float32

    def body(*refs):
        came_refs, near_refs, refs = refs[:2], refs[2:4], refs[4:]
        far_refs, refs = refs[: len(far)], refs[len(far) :]
        more_refs, (out_x, out_y, keep_x, keep_y) = list(refs[:-4]), refs[-4:]
        sums = [
            n[...] + c[:rows, :].astype(full) for n, c in zip(near_refs, came_refs, strict=True)
        ]
        keep_x[...], keep_y[...] = sums[0][:line], sums[1][:line]
        out_x[ahead : ahead + line, :] = sums[1][line:].astype(low)
        out_y[ahead : ahead + line, :] = sums[0][line:].astype(low)
        for out, far_ref in zip((out_x, out_y), far_refs, strict=False):
            out[:ahead, :] = far_ref[...]
        for out, count in zip((out_x, out_y), extra, strict=True):
            if count:
                out[ahead + line :, :] = more_refs.pop(0)[...]

    outs = [ahead + line + extra[0], ahead + line + extra[1], line, line]
    return pl.pallas_call(
        body,
        out_shape=[
            jax.ShapeDtypeStruct((count, width), dtype)
            for count, dtype in zip(outs, (low, low, full, full), strict=True)
        ],
        compiler_params=pltpu.CompilerParams(vmem_limit_bytes=40 << 20),
        cost_estimate=BESIDE,
    )(*came, *near, *far, *[m for m in more if m is not None])


def times_gathered(left, pieces, start, stop, so_far=None):
    plane, _, shard, width = pieces[0].shape
    rows, tiles = plane * shard, width // COLUMNS

    def body(left_ref, *refs):
        *piece_refs, out_ref = refs
        total = None if so_far is None else piece_refs.pop()[...]
        for i, piece_ref in enumerate(piece_refs):
            part = left_ref[:, i * rows : (i + 1) * rows]
            term = jnp.dot(
                part, piece_ref[...].reshape(rows, COLUMNS), preferred_element_type=jnp.float32
            )
            total = term if total is None else total + term
        out_ref[...] = total

    depth = (stop - start) * width
    out_spec = pl.BlockSpec((left.shape[0], COLUMNS), lambda w, j: (0, w * tiles + j))
    piece_spec = pl.BlockSpec((plane, 1, shard, COLUMNS), lambda w, j: (0, w + start, 0, j))
    return pl.pallas_call(
        body,
        grid=(stop - start, tiles),
        in_specs=[pl.BlockSpec(left.shape, lambda w, j: (0, 0))]
        + [piece_spec] * len(pieces)
        + [out_spec] * (so_far is not None),
        out_specs=out_spec,
        out_shape=jax.ShapeDtypeStruct((left.shape[0], depth), jnp.float32),
        compiler_params=pltpu.CompilerParams(vmem_limit_bytes=40 << 20),
        cost_estimate=BESIDE,
    )(left, *pieces, *([] if so_far is None else [so_far]))


def times_transposed(left, pieces, start, stop):
    plane, _, shard, width = pieces[0].shape
    rows, tiles = plane * shard, width // COLUMNS
    out_shape = (left.shape[1], rows * len(pieces))

    def body(left_ref, *refs):
        *piece_refs, out_ref = refs

        @pl.when((pl.program_id(0) == 0) & (pl.program_id(1) == 0))
        def _():
            out_ref[...] = jnp.zeros_like(out_ref)

        for i, piece_ref in enumerate(piece_refs):
            out_ref[:, i * rows : (i + 1) * rows] += lax.dot_general(
                left_ref[0],
                piece_ref[...].reshape(rows, COLUMNS),
                (((1,), (1,)), ((), ())),
                preferred_element_type=jnp.float32,
            )

    piece_spec = pl.BlockSpec((plane, 1, shard, COLUMNS), lambda w, j: (0, w + start, 0, j))
    return pl.pallas_call(
        body,
        grid=(stop - start, tiles),
        in_specs=[pl.BlockSpec((1, left.shape[1], COLUMNS), lambda w, j: (left.shape[0] - 1 - w, 0, j))]
        + [piece_spec] * len(pieces),
        out_specs=pl.BlockSpec(out_shape, lambda w, j: (0, 0)),
        out_shape=jax.ShapeDtypeStruct(out_shape, jnp.float32),
        compiler_params=pltpu.CompilerParams(vmem_limit_bytes=40 << 20),
        cost_estimate=BESIDE,
    )(left, *pieces)


GROUP = 8


def attention(projected, gains, tables, doc_ids, heads):
    length, width = projected.shape[0], projected.shape[1] // 3
    low, full = jnp.bfloat16, jnp.float32
    scale = HD ** (-0.5)

    def body(raw_ref, gain_ref, cos_ref, sin_ref, row_ref, col_ref,
             query_ref, key_ref, value_ref, out_ref, prob_ref, inv_ref, seen_ref):
        first = pl.program_id(0) * GROUP

        @pl.when(first == 0)
        def _():
            for i in (0, 1):
                raw = raw_ref[:, i * width : (i + 1) * width]
                mean = jnp.mean(raw * raw, axis=-1, keepdims=True)
                inv_ref[:, i : i + 1] = lax.rsqrt(mean + EPS)
            at = lax.broadcasted_iota(jnp.int32, (length, length), 0)
            to = lax.broadcasted_iota(jnp.int32, (length, length), 1)
            seen = (row_ref[...] == col_ref[...]) & (at >= to)
            seen_ref[...] = jnp.where(seen, 1.0, 0.0)

        def turned(i, head):
            raw = raw_ref[:, pl.ds(pl.multiple_of(i * width + head * HD, HD), HD)]
            gain = gain_ref[i + 1 : i + 2, pl.ds(pl.multiple_of(head * HD, HD), HD)]
            value = raw * inv_ref[:, i : i + 1] * gain
            return (value * cos_ref[...] + pltpu.roll(value, HD // 2, 1) * sin_ref[...]).astype(low)

        for g in range(GROUP):
            at = slice(g * HD, (g + 1) * HD)
            query, key = turned(0, first + g), turned(1, first + g)
            value_at = pl.multiple_of(2 * width + (first + g) * HD, HD)
            value = raw_ref[:, pl.ds(value_at, HD)].astype(low)
            scores = lax.dot_general(
                query, key, (((1,), (1,)), ((), ())), preferred_element_type=full
            ) * scale
            scores = jnp.where(seen_ref[...] > 0.0, scores, MASKED)
            expo = jnp.exp(scores - jnp.max(scores, axis=-1, keepdims=True))
            probs = expo / jnp.sum(expo, axis=-1, keepdims=True)
            prob_ref[g] = probs
            out = jnp.dot(probs.astype(low), value, preferred_element_type=full)
            out_ref[:, at] = out.astype(low)
            query_ref[:, at], key_ref[:, at], value_ref[:, at] = query, key, value

    def whole(shape):
        return pl.BlockSpec(shape, lambda h: (0,) * len(shape))

    part = pl.BlockSpec((length, GROUP * HD), lambda h: (0, h))
    flat = jax.ShapeDtypeStruct((length, width), low)
    return pl.pallas_call(
        body,
        grid=(heads // GROUP,),
        in_specs=[
            whole(projected.shape), whole(gains.shape), whole((length, HD)), whole((length, HD)),
            whole((length, 1)), whole((1, length)),
        ],
        out_specs=[part, part, part, part,
                   pl.BlockSpec((GROUP, length, length), lambda h: (h, 0, 0)), whole((length, LANES))],
        out_shape=[flat, flat, flat, flat,
                   jax.ShapeDtypeStruct((heads, length, length), full),
                   jax.ShapeDtypeStruct((length, LANES), full)],
        scratch_shapes=[pltpu.VMEM((length, length), full)],
        compiler_params=pltpu.CompilerParams(vmem_limit_bytes=40 << 20),
        cost_estimate=BESIDE,
    )(projected, gains, *tables, doc_ids.reshape(length, 1), doc_ids.reshape(1, length))


def attention_back(grad_out, query, key, value, probs, projected, inverses, gains, tables, heads):
    length, width = grad_out.shape
    low, full = jnp.bfloat16, jnp.float32
    scale = HD ** (-0.5)

    def body(grad_ref, query_ref, key_ref, value_ref, prob_ref, raw_ref, inv_ref, gain_ref,
             cos_ref, sin_ref, out_ref, dgain_ref, turned_ref, inner_ref):
        first = pl.program_id(0) * GROUP

        @pl.when(first == 0)
        def _():
            inner_ref[...] = jnp.zeros_like(inner_ref)

        for g in range(GROUP):
            head, part = first + g, slice(g * HD, (g + 1) * HD)
            here = pl.multiple_of(head * HD, HD)
            grad, probs = grad_ref[:, part], prob_ref[g]
            grad_probs = lax.dot_general(
                grad, value_ref[:, part], (((1,), (1,)), ((), ())), preferred_element_type=full
            )
            out_ref[0, :, pl.ds(here, HD)] = lax.dot_general(
                probs.astype(low), grad, (((0,), (0,)), ((), ())), preferred_element_type=full
            ).astype(low)
            inner = jnp.sum(probs * grad_probs, axis=-1, keepdims=True)
            grad_scores = (probs * (grad_probs - inner)).astype(low)
            rotated = (
                jnp.dot(grad_scores, key_ref[:, part], preferred_element_type=full) * scale,
                lax.dot_general(
                    grad_scores, query_ref[:, part], (((0,), (0,)), ((), ())),
                    preferred_element_type=full,
                ) * scale,
            )
            for i in (0, 1):
                back = rotated[i] * cos_ref[...] - pltpu.roll(rotated[i], HD // 2, 1) * sin_ref[...]
                at = pl.ds(pl.multiple_of(i * width + head * HD, HD), HD)
                turned_ref[:, at] = back
                normed = raw_ref[:, at] * inv_ref[:, i : i + 1]
                dgain_ref[i : i + 1, pl.ds(here, HD)] = jnp.sum(back * normed, axis=0, keepdims=True)
                weighed = back * gain_ref[i + 1 : i + 2, pl.ds(here, HD)]
                inner_ref[:, i : i + 1] += jnp.sum(weighed * normed, axis=-1, keepdims=True)

        @pl.when(first == heads - GROUP)
        def _():
            for i in (0, 1):
                inverse = inv_ref[:, i : i + 1]
                inner = inner_ref[:, i : i + 1] * (1.0 / width)

                @pl.loop(0, heads)
                def _(j):
                    at = pl.ds(pl.multiple_of(i * width + j * HD, HD), HD)
                    there = pl.ds(pl.multiple_of(j * HD, HD), HD)
                    weighed = turned_ref[:, at] * gain_ref[i + 1 : i + 2, there]
                    normed = raw_ref[:, at] * inverse
                    out_ref[2 - i, :, there] = (inverse * (weighed - normed * inner)).astype(low)

    def whole(shape):
        return pl.BlockSpec(shape, lambda h: (0,) * len(shape))

    part = pl.BlockSpec((length, GROUP * HD), lambda h: (0, h))
    return pl.pallas_call(
        body,
        grid=(heads // GROUP,),
        in_specs=[
            part, part, part, part,
            pl.BlockSpec((GROUP, length, length), lambda h: (h, 0, 0)),
            whole((length, 2 * width)), whole(inverses.shape), whole(gains.shape),
            whole((length, HD)), whole((length, HD)),
        ],
        out_specs=[whole((3, length, width)), whole((8, width))],
        out_shape=[
            jax.ShapeDtypeStruct((3, length, width), low), jax.ShapeDtypeStruct((8, width), full)
        ],
        scratch_shapes=[pltpu.VMEM((length, 2 * width), full), pltpu.VMEM((length, LANES), full)],
        compiler_params=pltpu.CompilerParams(vmem_limit_bytes=40 << 20),
        cost_estimate=BESIDE,
    )(grad_out, query, key, value, probs, projected, inverses, gains, *tables)


def expert_back(pieces, cot, gate, result, pre_gate, pre_up, gate_w, up_w, down_w, own):
    total, width = cot.shape
    rows = min(512, total)
    pieces = pieces if rows == total else 1
    hidden = pre_gate.shape[1]
    low, full = jnp.bfloat16, jnp.float32
    tile = min(512, hidden)

    def body(own_ref, cot_ref, gate_ref, result_ref, a_ref, b_ref, gate_w_ref, up_w_ref, down_w_ref,
             *refs):
        back_refs, (grad_y_ref, grad_a_ref, grad_b_ref, sum_ref) = refs[:pieces], refs[pieces:]
        each = rows // pieces
        step = pl.program_id(1)

        @pl.when(step == 0)
        def _():
            cot_f = cot_ref[...].astype(full)
            grad_y_ref[...] = (gate_ref[...] * cot_f).astype(low)
            grad_g = jnp.sum(cot_f * result_ref[...].astype(full), axis=-1, keepdims=True)
            high = grad_g.astype(low).astype(full)
            lanes = lax.broadcasted_iota(jnp.int32, (rows, LANES), 1)
            tail = jnp.where(lanes == own_ref[0], high, 0.0)
            tail = jnp.where(lanes == own_ref[0] + LANES // 2, grad_g - high, tail)
            for p, back_ref in enumerate(back_refs):
                back_ref[:, width:] = tail[p * each : (p + 1) * each].astype(low)
            sum_ref[...] = jnp.zeros_like(sum_ref)

        grad_act = lax.dot_general(
            grad_y_ref[...], down_w_ref[...], (((1,), (1,)), ((), ())), preferred_element_type=full
        )
        pre_gate, pre_up = a_ref[...], b_ref[...]
        sigmoid_g = jax.nn.sigmoid(pre_gate)
        slope = sigmoid_g * (1.0 + pre_gate * (1.0 - sigmoid_g))
        grad_a = (grad_act * pre_up * slope).astype(low)
        grad_b = (grad_act * (pre_gate * sigmoid_g)).astype(low)
        grad_a_ref[...], grad_b_ref[...] = grad_a, grad_b
        contract = (((1,), (1,)), ((), ()))
        sum_ref[...] += lax.dot_general(
            grad_a, gate_w_ref[...], contract, preferred_element_type=full
        ) + lax.dot_general(grad_b, up_w_ref[...], contract, preferred_element_type=full)

        @pl.when(step == hidden // tile - 1)
        def _():
            for p, back_ref in enumerate(back_refs):
                back_ref[:, :width] = sum_ref[p * each : (p + 1) * each, :].astype(low)

    def whole(columns):
        return pl.BlockSpec((rows, columns), lambda r, f: (r, 0))

    inner = pl.BlockSpec((rows, tile), lambda r, f: (r, f))
    into = pl.BlockSpec((width, tile), lambda r, f: (0, f))
    outs = pl.pallas_call(
        body,
        grid=(total // rows, hidden // tile),
        in_specs=[
            pl.BlockSpec(memory_space=pltpu.SMEM),
            whole(width), whole(1), whole(width), inner, inner, into, into,
            pl.BlockSpec((tile, width), lambda r, f: (f, 0)),
        ],
        out_specs=[pl.BlockSpec((rows // pieces, width + LANES), lambda r, f: (r, 0))] * pieces
        + [whole(width), inner, inner],
        out_shape=[jax.ShapeDtypeStruct((total // pieces, width + LANES), low)] * pieces
        + [
            jax.ShapeDtypeStruct(cot.shape, low),
            jax.ShapeDtypeStruct(pre_gate.shape, low),
            jax.ShapeDtypeStruct(pre_gate.shape, low),
        ],
        scratch_shapes=[pltpu.VMEM((rows, width), full)],
        compiler_params=pltpu.CompilerParams(vmem_limit_bytes=52 << 20),
        cost_estimate=BESIDE,
    )(own.reshape(1), cot, gate, result, pre_gate, pre_up, gate_w, up_w, down_w)
    return (outs[:pieces], *outs[pieces:])


def rows_product(lefts, rights):
    rows, height = lefts[0].shape
    width = rights[0].shape[1]
    tile = min(512, height)

    def body(*refs):
        out_ref = refs[-1]
        total = None
        for left_ref, right_ref in zip(refs[: len(lefts)], refs[len(lefts) : -1], strict=True):
            term = lax.dot_general(
                left_ref[...], right_ref[...], (((0,), (0,)), ((), ())),
                preferred_element_type=jnp.float32,
            )
            total = term if total is None else total + term
        out_ref[...] = total

    return pl.pallas_call(
        body,
        grid=(height // tile,),
        in_specs=[pl.BlockSpec((rows, tile), lambda i: (0, i))] * len(lefts)
        + [pl.BlockSpec((rows, width), lambda i: (0, 0))] * len(rights),
        out_specs=pl.BlockSpec((tile, width), lambda i: (i, 0)),
        out_shape=jax.ShapeDtypeStruct((height, width), jnp.float32),
        compiler_params=pltpu.CompilerParams(vmem_limit_bytes=52 << 20),
        cost_estimate=BESIDE,
    )(*lefts, *rights)


def input_gradient(grad, sources, tokens, inverse, gain, residual):
    length, width = grad.shape
    tile = 512
    low, full = jnp.bfloat16, jnp.float32

    def body(grad_ref, source_ref, token_ref, inverse_ref, gain_ref, residual_ref,
             out_ref, dgain_ref, split_ref, placed_ref, inner_ref):
        step = pl.program_id(0)

        @pl.when(step == 0)
        def _():
            high = grad_ref[...].astype(low)
            split_ref[:length, :] = high
            split_ref[length:, :] = (grad_ref[...] - high.astype(full)).astype(low)
            inner_ref[...] = jnp.zeros_like(inner_ref)

        at = pl.ds(pl.multiple_of(step * tile, tile), tile)
        column = step * tile + lax.broadcasted_iota(jnp.int32, (tile, width), 0)
        arrival = jnp.where(column == source_ref[...], 1.0, 0.0).astype(low)
        placed = lax.dot_general(
            split_ref[...], arrival, (((1,), (1,)), ((), ())), preferred_element_type=full
        )
        placed = placed[:length] + placed[length:]
        placed_ref[:, at] = placed
        normed = token_ref[:, at].astype(full) * inverse_ref[...]
        dgain_ref[:, at] = jnp.broadcast_to(
            jnp.sum(placed * normed, axis=0, keepdims=True), (dgain_ref.shape[0], tile)
        )
        weighed = placed * gain_ref[:, at]
        inner_ref[:, :1] += jnp.sum(weighed * normed, axis=-1, keepdims=True)

        @pl.when(step == width // tile - 1)
        def _():
            inner = inner_ref[:, :1] * (1.0 / width)
            inverse = inverse_ref[...]

            @pl.loop(0, width // tile)
            def _(j):
                at = pl.ds(pl.multiple_of(j * tile, tile), tile)
                normed = token_ref[:, at].astype(full) * inverse
                back = inverse * (placed_ref[:, at] * gain_ref[:, at] - normed * inner)
                out_ref[:, at] = (residual_ref[:, at] + back).astype(low)

    def whole(shape):
        return pl.BlockSpec(shape, lambda j: (0,) * len(shape))

    return pl.pallas_call(
        body,
        grid=(width // tile,),
        in_specs=[
            whole(grad.shape), whole(sources.shape), whole(tokens.shape),
            whole(inverse.shape), whole(gain.shape), whole(residual.shape),
        ],
        out_specs=[whole(tokens.shape), whole((8, width))],
        out_shape=[
            jax.ShapeDtypeStruct(tokens.shape, low), jax.ShapeDtypeStruct((8, width), full)
        ],
        scratch_shapes=[
            pltpu.VMEM((2 * length, width), low),
            pltpu.VMEM((length, width), full),
            pltpu.VMEM((length, LANES), full),
        ],
        compiler_params=pltpu.CompilerParams(vmem_limit_bytes=40 << 20),
        cost_estimate=BESIDE,
    )(grad, sources, tokens, inverse, gain, residual)


def rope_tables(length):
    half = HD // 2
    freq = THETA ** (-(jnp.arange(half, dtype=jnp.float32) * 2.0) / HD)
    angle = jnp.arange(length, dtype=jnp.float32)[:, None] * freq[None, :]
    sine = jnp.sin(angle)
    cosine = jnp.cos(angle)
    return (
        jnp.concatenate([cosine, cosine], axis=-1),
        jnp.concatenate([-sine, sine], axis=-1),
    )


def on_device(
    tokens,
    segments,
    expert_ids,
    norm_gains,
    w_query,
    w_key,
    w_value,
    w_out,
    w_router,
    expert_gate,
    expert_up,
    expert_down,
    cotangent,
):
    bfloat = jnp.bfloat16
    here = Places()
    length, width = tokens.shape
    topk = expert_ids.shape[1]
    experts = here.count
    capacity = length * topk // experts
    heads = width // HD
    shard = w_query.shape[0]
    plane = here.plane
    gate_w, up_w, down_w = expert_gate[0], expert_up[0], expert_down[0]

    labels = jnp.arange(experts, dtype=jnp.int32)
    named = jnp.any(expert_ids[:, :, None] == labels[None, None, :], axis=1)
    places = jnp.arange(length, dtype=jnp.int32)
    earlier = (places[:, None] < places[None, :]).astype(bfloat)
    slots = contract_rows(named.astype(bfloat), earlier)
    slots = jnp.where(named.T & (slots < capacity), slots, -1.0).astype(bfloat)

    order = range(here.nz)
    arrival, sources = here.arrival(width)
    extra = norm_gains.shape[0] + w_router.shape[1]
    smalls = jnp.concatenate(
        [norm_gains.T, w_router, jnp.zeros((shard, -extra % LANES), jnp.float32)], axis=1
    ).astype(bfloat)
    smalls = jnp.concatenate([smalls, slots.reshape(-1, LANES)], axis=0)
    smalls = here.along_whole_line([smalls] * here.nz)
    plane_expert = jnp.stack(
        [
            here.at(here.z, (here.y + dy) % here.ny, (here.x + dx) % here.nx)
            for dy, dx in here.steps
        ]
    )
    chosen = plane_expert[:, None] == labels[None, :]
    slot_ids = jnp.arange(capacity, dtype=jnp.int32)
    spreads = []

    def spread_of(part):
        picked = jnp.sum(
            jnp.where(chosen[:, :, None], part[None].astype(jnp.float32), 0.0), axis=1
        ).astype(jnp.int32)
        hit = picked[:, None, :] == slot_ids[None, :, None]
        return hit.astype(bfloat).reshape(plane * capacity, length)

    def rows_of(spread, part):
        return list(product(spread, part).astype(bfloat).reshape(plane, capacity, -1))

    def parted(rows):
        return list(rows.reshape(plane, capacity, -1))

    def joined(rows):
        return jnp.concatenate(rows, axis=0)

    inputs = tokens.astype(jnp.float32)
    weights = jnp.stack([w_query, w_key, w_value, w_out]).astype(bfloat)
    line, cot_line = Spread(here, weights), Spread(here, cotangent)
    half = weights.shape[0] // 2
    raw, chunks, pieces = [], [], []
    projected = None
    depth = width // here.nz
    cot_rows, rows_cot = [None] * here.nz, [None] * here.nz

    def stacked(rows):
        return rows.reshape(-1, shard, width)

    def chunk_of(k):
        if here.square:
            at = 2 * half if k + 1 < here.nz else 0
            blocks = [line.queue[k]] + [by[: 2 * half] for by in raw[k][:2]]
            blocks += [by[at : at + half] for by in raw[k + 1][:2]]
        else:
            blocks = raw[k]
        return jnp.concatenate(blocks, axis=0).reshape(plane, *weights.shape)

    def share(chunk):
        return [chunk] + [here.other_core(chunk, s) for s in range(1, here.cores)]

    def project(k):
        return times_gathered(
            in_order[:, k * depth : (k + 1) * depth], pieces[k], 0, 3, projected
        )

    for k in range(here.nz + 2):
        outs = []
        if here.square:
            by_x, by_y = [], []
            if k < here.nz:
                by_x.append(line.queue[k])
                by_y.append(line.queue[k])
            if 0 < k <= here.nz:
                by_x.append(raw[k - 1][1][:half])
                by_y.append(raw[k - 1][0][half : 2 * half])
            if k >= here.nz:
                by_x.append(stacked(cot_rows[k - here.nz][1]))
                by_y.append(stacked(cot_rows[k - here.nz][2]))
            outs = [jnp.concatenate(by_x, axis=0), jnp.concatenate(by_y, axis=0)]
            if k > here.nz:
                outs.append(jnp.concatenate([cot_rows[0][3], cot_rows[1][3]], axis=0))
        elif k < here.nz:
            outs = [line.queue[k]] * plane
        else:
            outs = cot_rows[k - here.nz]
        if k == 1:
            outs, smalls, raw, line.queue = tie(outs, smalls, raw, line.queue)
            turned = jnp.stack(smalls).reshape(here.nz, -1)
            near = (here.z - here.queue_of(jnp.arange(here.nz))) % here.nz
            pick = (near[:, None] == jnp.arange(here.nz)[None, :]).astype(bfloat)
            turned = product(pick, turned).astype(bfloat).reshape(here.nz, -1, LANES)
            smalls, slots = turned[:, :shard], turned[:, shard:]
            smalls = here.along_plane([smalls] * plane)
        outs, smalls, slots, raw, chunks, line.queue, cot_line.queue, cot_rows, cotangent = tie(
            outs, smalls, slots, raw, chunks, line.queue, cot_line.queue, cot_rows, cotangent
        )
        if here.square:
            ins = [here.shift_plane(outs[0], 0, 1), here.shift_plane(outs[1], 1, 0)]
            if k > here.nz:
                ins.append(here.shift_plane(outs[2], 1, 1))
        else:
            ins = here.along_plane(outs)
        moving = line.step() if k < here.nz else []
        moving_cot = cot_line.step() if k >= here.nz - 1 else []
        if k == 1:
            spreads = [spread_of(part.reshape(experts, length)) for part in slots]
        if k > 2:
            pieces.append(share(chunks[k - 3]))
        if k > 1:
            chunks.append(chunk_of(k - 2))
        if k == 2:
            smalls = jnp.stack(smalls, axis=1)
            smalls = [smalls] + [here.other_core(smalls, s) for s in range(1, here.cores)]
            smalls = jnp.stack(smalls, axis=1).reshape(width, -1)
            smalls = product(arrival, smalls).astype(bfloat)
            smalls, sources = tie(smalls, sources)
        if k == 3:
            gains_f = smalls[:, : norm_gains.shape[0]].T.astype(jnp.float32)
            wr = smalls[:, norm_gains.shape[0] : extra]
            normed_in_f, normed_one, inverse_one = norm_rows(inputs, gains_f[0])
            normed_in = normed_in_f.astype(bfloat)
            in_order = product(normed_in, arrival).astype(bfloat)
        if k > 2:
            projected = project(k - 3)
        if k == 1:
            both_w = jnp.concatenate([gate_w, up_w], axis=1)
            spreads, both_w = tie(spreads, both_w)
        if k >= here.nz - 1 and k - here.nz + 1 < here.nz:
            at = k - here.nz + 1
            cot_rows[at] = rows_of(spreads[at], cot_line.queue[at])
        ins, moving, moving_cot, smalls, projected, cot_rows, spreads, chunks = tie(
            ins, moving, moving_cot, smalls, projected, cot_rows, spreads, chunks
        )
        line.land(moving)
        cot_line.land(moving_cot)
        raw.append(ins)
        if k >= here.nz:
            rows_cot[k - here.nz] = ins
            if here.square:
                own = cot_rows[k - here.nz][0]
                skip = half if k == here.nz else 0
                rows_cot[k - here.nz] = [own] + [by[skip:].reshape(own.shape) for by in ins[:2]]
            if here.square and k > here.nz:
                for i in (0, 1):
                    rows_cot[i].append(ins[2][i * capacity : (i + 1) * capacity])

    order_x = here.target_order(width // here.cores, "x")
    order_y = here.target_order(width // here.cores, "y")

    def targeted(columns):
        columns = jnp.concatenate(columns, axis=0)
        return [product(columns, o).astype(bfloat) for o in (order_x, order_y)]

    merged = []
    if here.nz > 2:
        cot_rows[3] = rows_of(spreads[3], cot_line.queue[3])
        merged = [joined(pair) for pair in zip(*cot_rows[2:], strict=True)]
    in_columns = here.core_columns(normed_in)
    merged, chunks, projected, pieces, in_columns = tie(
        merged, chunks, projected, pieces, in_columns
    )
    ins = here.along_plane(merged) if merged else []
    pieces.append(share(chunks[-1]))
    in_columns = here.to_cores(in_columns)
    projected = project(here.nz - 1)
    pieces = [piece for chunk in pieces for piece in chunk]
    tables = rope_tables(length)
    query_rot, key_rot, values, attended, probs, inverses = attention(
        projected, gains_f, tables, segments[0], heads
    )
    residual = inputs + times_gathered(product(attended, arrival).astype(bfloat), pieces, 3, 4)
    normed_mid_f, normed_two, inverse_two = norm_rows(residual, gains_f[3])
    normed_mid = normed_mid_f.astype(bfloat)

    own_label = labels[None, :] == here.me

    def expert_forward(arrived):
        route_here = jax.nn.softmax(product(arrived, wr), axis=-1)
        gate = jnp.sum(jnp.where(own_label, route_here, 0.0), axis=-1)
        gate = gate.astype(bfloat).astype(jnp.float32)[:, None]
        pre_gate = product(arrived, gate_w)
        pre_up = product(arrived, up_w)
        activated = (jax.nn.silu(pre_gate) * pre_up).astype(bfloat)
        result = product(activated, down_w).astype(bfloat)
        gated = (gate * result.astype(jnp.float32)).astype(bfloat)
        return (gate, pre_gate, pre_up, activated, result, gated)

    def expert_backward(kept, cot):
        gate, pre_gate, pre_up, _, result, _ = kept
        back, *kept = expert_back(
            plane, cot, gate, result, pre_gate, pre_up, gate_w, up_w, down_w, here.me
        )
        return [back if len(back) == plane else parted(back[0]), *kept]

    rows_next = rows_of(spreads[0], normed_mid)
    out_columns = here.core_columns(attended)
    normed_mid, rows_next, ins, in_columns, out_columns = tie(
        normed_mid, rows_next, ins, in_columns, out_columns
    )
    if here.nz > 2:
        rows_cot[2:] = [[row[i : i + capacity] for row in ins] for i in (0, capacity)]
    line = Spread(here, normed_mid)
    rows_in, forward = [], []
    for k in order:
        if k > 0:
            rows_next = rows_of(spreads[k], line.queue[k])
        rows_next, rows_in, line.queue, out_columns = tie(
            rows_next, rows_in, line.queue, out_columns
        )
        moving = line.step()
        rows = here.along_plane(rows_next)
        if k > 0:
            rows_in[-1] = joined(rows_in[-1])
            forward.append(expert_forward(rows_in[-1]))
        if k == 0:
            targets = targeted(in_columns)
            rows, targets = tie(rows, targets)
        if k == here.nz // 2:
            out_columns = here.to_cores(out_columns)
        if k == here.nz - 1:
            out_columns = targeted(out_columns)
        for j in order[here.nz - k - (k == here.nz - 1) : here.nz - k + 1] if k > 0 else []:
            rows_cot[j] = joined(rows_cot[j])
            rows, rows_cot[j] = tie(rows, rows_cot[j])
        moving, rows, forward, out_columns = tie(moving, rows, forward, out_columns)
        rows_in.append(rows)
        line.land(moving)

    targets_out = out_columns
    half = here.nz // 2
    back_y = [None] * here.nz
    backward = [None] * here.nz
    todo = ["forward", *reversed(order)]

    def work():
        k = todo.pop(0) if todo else None
        if k == "forward":
            rows_in[-1] = joined(rows_in[-1])
            forward.append(expert_forward(rows_in[-1]))
        elif k is not None:
            backward[k] = expert_backward(forward[k], rows_cot[k])

    rows_next = parted(forward[0][5])
    rows_next, forward, rows_in, rows_cot, out_columns = tie(
        rows_next, forward, rows_in, rows_cot, out_columns
    )
    rows = here.deal_back(rows_next)
    work()
    work()
    rows, forward, backward = tie(rows, forward, backward)
    back_y[0] = rows
    collect, parts = Collect(here), [None] * here.nz
    moving, sending, back = [], [], None
    for k in reversed(order):
        rows_next = backward[k][0]
        if k + 2 < here.nz:
            collect.land(moving)
            sending = collect.add(k + 2, parts[k + 2])
        rows_next, sending, forward, backward, back = tie(
            rows_next, sending, forward, backward, back
        )
        rows = here.deal_back(rows_next)
        moving = collect.send(sending)
        if k > 0:
            work()
        else:
            grad_down = rows_product(
                [kept[3] for kept in forward], [kept[1] for kept in backward]
            )
            rows, grad_down = tie(rows, grad_down)
        if back is not None:
            parts[k + 1] = contract_rows(spreads[k + 1], joined(back))
        moving, rows, forward, backward, parts = tie(moving, rows, forward, backward, parts)
        back = rows
    late = list(order[:0:-1])
    collect.land(moving)
    sending = collect.add(1, parts[1])
    rows_next = parted(forward[late[0]][5])
    rows_next, sending, back, back_y = tie(rows_next, sending, back, back_y)
    rows = here.deal_back(rows_next)
    moving = collect.send(sending)
    parts[0] = contract_rows(spreads[0], joined(back))
    part_y = contract_rows(spreads[0], joined(back_y[0]))
    rows_next = [parted(forward[k][5]) for k in late[1:]]
    moving, rows, parts, rows_next, part_y = tie(moving, rows, parts, rows_next, part_y)
    collect.land(moving)
    collect.add(0, parts[0])
    returned = collect.total
    back_y[late[0]] = rows
    parts_y = [None] * here.nz
    parts_y[0] = part_y
    if rows_next:
        back_y[late[1]] = here.deal_back(rows_next[0])

    def add_up_y(k):
        parts_y[k] = contract_rows(spreads[k], joined(back_y[k]))

    add_up_y(late[0])

    grad_mid = returned[:, :width]
    grad_route = (
        returned[:, width : width + experts]
        + returned[:, width + LANES // 2 : width + LANES // 2 + experts]
    )
    route = jax.nn.softmax(product(normed_mid, wr), axis=-1)
    grad_logits = (
        route * (grad_route - jnp.sum(route * grad_route, axis=-1, keepdims=True))
    ).astype(bfloat)
    grad_router = contract_rows(normed_mid, grad_logits)
    grad_mid = grad_mid + contract_cols(grad_logits, wr)
    grad_res_two, grad_gain_mid = norm_back(grad_mid, gains_f[3], normed_two, inverse_two)
    grad_residual = cotangent.astype(jnp.float32) + grad_res_two
    grad_attn = grad_residual.astype(bfloat)
    grad_attended = times_transposed(grad_attn[None], pieces, 3, 4).astype(bfloat)
    grad_attended = contract_cols(grad_attended, arrival).astype(bfloat)
    collect_y, adds_y = Collect(here), list(reversed(order))
    grad_attended, grad_attn, back_y, parts_y = tie(grad_attended, grad_attn, back_y, parts_y)
    sending_y = collect_y.add(adds_y[0], parts_y[adds_y.pop(0)])
    sending_y, grad_attended, grad_attn, back_y, rows_next = tie(
        sending_y, grad_attended, grad_attn, back_y, rows_next
    )
    if rows_next:
        back_y[late[2]] = here.deal_back(rows_next[1])
    moving = collect_y.send(sending_y)
    out_tokens = here.all_tokens(grad_attn)
    grads, grad_gain_heads = attention_back(
        grad_attended, query_rot, key_rot, values, probs, projected, inverses, gains_f, tables, heads
    )
    far = here.scatter_far(*targets_out, out_tokens)
    for k in late[1:2]:
        add_up_y(k)
    grads, far, back_y, parts_y, moving, out_tokens = tie(
        grads, far, back_y, parts_y, moving, out_tokens
    )

    def arrive(outs):
        if not here.square:
            return here.along_plane(outs) if outs else []
        return [here.shift_plane(outs[0], 0, 1), here.shift_plane(outs[1], 1, 0)]

    jobs = 4
    lefts, rights = [targets_out, targets, targets, targets], [out_tokens]
    lasts, shares, others, grad_in_norm = [], [], [], None
    near, near_last, ins, small, smalls, expert_grads = [], [], [], [None], [], []
    for i in range(jobs + 2):
        outs, parts, more = [], [], [None, None]
        if here.square:
            ahead = here.rows_first(width) if i <= jobs else 0
            if i > 1:
                line = ahead + near_last[0].shape[0] if i > 1 else 0
                lasts.append([ins[1][ahead:line], ins[0][ahead:line], *near_last])
            columns = small[0].shape[1] // 2 if small[0] is not None else 0
            if i in (3, 4):
                came = ins[i == 4][line:].reshape(small[0].shape)
                small = [small[0] + came.astype(jnp.float32)]
            if i in (2, 3):
                more[i == 3] = small[0][:, columns:].astype(bfloat).reshape(-1, width // 2)
                small = [small[0][:, :columns]]
            if i == 0:
                outs = far
            elif i <= jobs:
                *outs, keep_x, keep_y = fold(ins, near, far if i < jobs else [], more)
                near_last = [keep_x, keep_y]
        else:
            if 0 < i <= jobs:
                lasts.append(ins)
            outs = far if i < jobs else []
        at = i - 2 if here.square else i - 1
        if 0 <= at < jobs:
            parts = here.line_parts(lasts[at])
            if here.square and i == 4:
                parts = [
                    jnp.concatenate([part, piece.reshape(-1, width).astype(part.dtype)], axis=0)
                    for part, piece in zip(
                        parts, jnp.split(small[0], here.nz, axis=1), strict=True
                    )
                ]
        sending_y = []
        if adds_y:
            collect_y.land(moving)
            sending_y = collect_y.add(adds_y[0], parts_y[adds_y.pop(0)])
        (
            outs, parts, sending_y, near_last, small, rights, smalls, grads, back_y, rows_in, grad_in_norm
        ) = tie(
            outs, parts, sending_y, near_last, small, rights, smalls, grads, back_y, rows_in, grad_in_norm
        )
        ins = arrive(outs) if outs else []
        if parts:
            parts = here.along_whole_line(parts)
        moving = collect_y.send(sending_y) if sending_y else []
        if here.square and i == 5:
            smalls = here.to_cores(smalls)
        if i < jobs:
            near = here.scatter_near(*lefts[i], rights[i])
        if i == 0:
            others = [here.other_core(grads, step) for step in range(1, here.cores)]
        if i + 1 < jobs:
            rights.append(jnp.concatenate([v[i] for v in [grads, *others]], axis=0))
        if i + 1 < jobs:
            far = here.scatter_far(*lefts[i + 1], rights[i + 1])
        if i == 0:
            grads, others = tie(grads, others)
            grad_in_norm = times_transposed(grads, pieces, 0, 3)
        if i == 1:
            grad_tokens, grad_gain_in = input_gradient(
                grad_in_norm, sources, tokens, inverse_one, gains_f[:1], grad_residual
            )
            small_rows = 4 + experts
            smalls = jnp.concatenate(
                [
                    grad_gain_in[:1],
                    grad_gain_heads[:2],
                    grad_gain_mid[None],
                    grad_router.T,
                    jnp.zeros((-small_rows % 32, width), jnp.float32),
                ],
                axis=0,
            )
            if here.square:
                smalls = jnp.concatenate(here.core_columns(smalls), axis=0)
                small = [product(smalls.astype(bfloat), order_x)]
            grad_tokens, small, smalls, ins = tie(grad_tokens, small, smalls, ins)
        if i == 0 and len(late) > 2:
            add_up_y(late[2])
        if 2 <= i <= 3:
            grad = rows_product(rows_in, [kept[i] for kept in backward])
            expert_grads.append(grad)
            ins, expert_grads = tie(ins, expert_grads)
        if i == 3:
            mixed = (residual + collect_y.total).astype(bfloat)
            mixed, ins = tie(mixed, ins)
        ins, parts, moving, far, near, rights, smalls, parts_y, grad_in_norm, others = tie(
            ins, parts, moving, far, near, rights, smalls, parts_y, grad_in_norm, others
        )
        if parts:
            share = sum(part.astype(jnp.float32) for part in parts)
            if here.square and i == 4:
                smalls = jnp.split(share[shard:].reshape(-1, shard), here.cores, axis=0)
            shares.append(share[:shard])
    if here.square:
        smalls = sum(smalls)
    else:
        smalls = lax.psum(smalls, ("dp", "expert"))
        smalls = lax.dynamic_slice(
            smalls, (0, (here.core * here.count + here.me) * shard), (smalls.shape[0], shard)
        )
    grad_wo, grad_wv, grad_wk, grad_wq = shares
    grad_gate_w, grad_up_w = expert_grads
    return (
        mixed,
        grad_tokens,
        smalls[:4],
        grad_wq,
        grad_wk,
        grad_wv,
        grad_wo,
        smalls[4:small_rows].T,
        grad_gate_w[None, None],
        grad_up_w[None, None],
        grad_down[None, None],
    )


def solution(mesh):
    return jax.shard_map(
        on_device,
        mesh=mesh,
        in_specs=(
            P(("dp", "expert"), None),
            P(("dp", "expert"), None),
            P(("dp", "expert"), None),
            P(None, ("dp", "expert")),
            P(("dp", "expert"), None),
            P(("dp", "expert"), None),
            P(("dp", "expert"), None),
            P(("dp", "expert"), None),
            P(("dp", "expert"), None),
            P("expert", None, None),
            P("expert", None, None),
            P("expert", None, None),
            P(("dp", "expert"), None),
        ),
        out_specs=(
            P(("dp", "expert"), None),
            P(("dp", "expert"), None),
            P(None, ("dp", "expert")),
            P(("dp", "expert"), None),
            P(("dp", "expert"), None),
            P(("dp", "expert"), None),
            P(("dp", "expert"), None),
            P(("dp", "expert"), None),
            P("dp", "expert", None, None),
            P("dp", "expert", None, None),
            P("dp", "expert", None, None),
        ),
        check_vma=False,
    )
```

```python
import jax
import jax.numpy as jnp
from jax import lax
from jax.experimental import pallas as pl
from jax.experimental.pallas import tpu as pltpu
from jax.sharding import PartitionSpec as P

HD = 128


EPS = 1e-05
THETA = 10000.0
MASKED = -1e30
LANES = 128


def norm_rows(value, gain):
    inverse = lax.rsqrt(jnp.mean(value * value, axis=-1, keepdims=True) + EPS)
    normed = value * inverse
    return (normed * gain, normed, inverse)


def norm_back(grad_in, gain, normed, inverse):
    grad_normed = grad_in * gain
    grad_gain = jnp.sum(grad_in * normed, axis=0)
    inner = jnp.mean(grad_normed * normed, axis=-1, keepdims=True)
    return (inverse * (grad_normed - normed * inner), grad_gain)


def contract_rows(left, right):
    return lax.dot_general(
        left, right, (((0,), (0,)), ((), ())), preferred_element_type=jnp.float32
    )


def contract_cols(left, right):
    return lax.dot_general(
        left, right, (((1,), (1,)), ((), ())), preferred_element_type=jnp.float32
    )


def product(left, right):
    return jnp.dot(left, right, preferred_element_type=jnp.float32)


def tie(*values):
    return lax.optimization_barrier(values)


class Spread:
    def __init__(self, here, own):
        self.here, self.queue, self.done = here, [own], 0

    def step(self):
        here, own = self.here, self.queue[0]
        self.done += 1
        if self.done >= here.nz:
            return []
        if here.nz != 4:
            moves = [(a, (a + self.done) % here.nz) for a in range(here.nz)]
            return [here.along_line(own, moves)]
        if self.done == 1:
            return [
                here.along_line(own, [(0, 1), (1, 0), (2, 3), (3, 2)]),
                here.along_line(own, [(1, 2), (2, 1)]),
            ]
        if self.done == 2:
            return [
                here.along_line(self.middle, [(1, 0), (2, 3)]),
                here.along_line(self.queue[1], [(1, 2), (2, 1)]),
            ]
        return [here.along_line(self.across, [(1, 0), (2, 3)])]

    def land(self, arrays):
        here = self.here
        if not arrays:
            return
        if here.nz != 4:
            self.queue += arrays
            return
        inner = (here.z == 1) | (here.z == 2)
        if self.done == 1:
            one, self.middle = arrays
            self.queue.append(one)
        elif self.done == 2:
            edge, self.across = arrays
            self.queue.append(jnp.where(inner, self.middle, edge))
        else:
            self.queue.append(jnp.where(inner, self.across, arrays[0]))

    def finish(self):
        while len(self.queue) < self.here.nz:
            self.land(self.step())
        return self.queue


class Collect:
    def __init__(self, here):
        self.here, self.came, self.moves = here, [], []

    def add(self, k, part):
        here = self.here
        if k == 0:
            self.total = part
            for value in self.came:
                self.total = self.total + value
            return []
        if here.nz != 4:
            out = [(part, [(a, (a - k) % here.nz) for a in range(here.nz)])]
        elif k == 3:
            self.three = part
            out = [(part, [(0, 1), (3, 2)])]
        elif k == 2:
            self.two = part
            (edge,) = self.came
            out = [(self.three + edge, [(1, 2), (2, 1)]), (part, [(0, 1), (3, 2)])]
        else:
            across, edge = self.came
            out = [
                (part + across, [(0, 1), (1, 0), (2, 3), (3, 2)]),
                (self.two + edge, [(1, 2), (2, 1)]),
            ]
        self.moves = [moves for _, moves in out]
        return [value.astype(jnp.bfloat16) for value, _ in out]

    def send(self, values):
        return [self.here.along_line(v, m) for v, m in zip(values, self.moves, strict=True)]

    def land(self, arrays):
        came = [value.astype(jnp.float32) for value in arrays]
        self.came = came if self.here.nz == 4 else self.came + came
        self.moves = []


def grid_of(count):
    if count % 32 == 0:
        return (count // 16, 4, 4)
    if count % 4 == 0:
        return (count // 4, 2, 2)
    return (count, 1, 1)


class Places:
    def __init__(self):
        self.count = lax.axis_size("expert")
        self.cores = lax.axis_size("dp")
        self.nz, self.ny, self.nx = grid_of(self.count)
        self.plane = self.ny * self.nx
        self.me = lax.axis_index("expert")
        self.core = lax.axis_index("dp")
        self.z = self.me // self.plane
        self.y = (self.me // self.nx) % self.ny
        self.x = self.me % self.nx
        self.steps = [(dy, dx) for dy in range(self.ny) for dx in range(self.nx)]
        self.square = (self.ny, self.nx) == (2, 2)
        if self.nz == 4:
            self.queue = [[0, 1, 2, 3], [1, 0, 2, 3], [2, 3, 1, 0], [3, 2, 1, 0]]
        else:
            self.queue = [[(z - k) % self.nz for k in range(self.nz)] for z in range(self.nz)]

    def at(self, z, y, x):
        return (z * self.ny + y) * self.nx + x

    def shift_plane(self, value, dy, dx):
        pairs = [
            (self.at(z, y, x), self.at(z, (y + dy) % self.ny, (x + dx) % self.nx))
            for z in range(self.nz)
            for y in range(self.ny)
            for x in range(self.nx)
        ]
        return lax.ppermute(value, "expert", pairs)

    def along_line(self, value, moves):
        pairs = [
            (self.at(a, y, x), self.at(b, y, x))
            for a, b in moves
            for y in range(self.ny)
            for x in range(self.nx)
        ]
        return lax.ppermute(value, "expert", pairs)

    def other_core(self, value, step):
        pairs = [(c, (c + step) % self.cores) for c in range(self.cores)]
        return lax.ppermute(value, "dp", pairs)

    def arrival(self, rows):
        shard = rows // (self.cores * self.count)
        order = jnp.arange(rows, dtype=jnp.int32)
        inside, rest = order % shard, order // shard
        step, rest = rest % self.plane, rest // self.plane
        core, k = rest % self.cores, rest // self.cores
        zed = self.queue_of(k)
        y = (self.y - step // self.nx) % self.ny
        x = (self.x - step % self.nx) % self.nx
        core = (self.core - core) % self.cores
        source = (core * self.count + self.at(zed, y, x)) * shard + inside
        return (order[:, None] == source[None, :]).astype(jnp.bfloat16), source[None, :]

    def queue_of(self, k):
        table = jnp.asarray(self.queue, jnp.int32)[self.z]
        zed = jnp.zeros_like(k)
        for q in range(self.nz):
            zed = jnp.where(k == q, table[q], zed)
        return zed

    def deal(self, rows):
        return [
            rows[i] if s == (0, 0) else self.shift_plane(rows[i], *s)
            for i, s in enumerate(self.steps)
        ]

    def deal_back(self, rows):
        return [
            rows[i] if s == (0, 0) else self.shift_plane(rows[i], -s[0], -s[1])
            for i, s in enumerate(self.steps)
        ]

    def along_plane(self, values):
        return [
            v if s == (0, 0) else self.shift_plane(v, *s)
            for v, s in zip(values, self.steps, strict=True)
        ]

    def along_whole_line(self, parts):
        return [
            part
            if k == 0
            else self.along_line(part, [(a, (a + k) % self.nz) for a in range(self.nz)])
            for k, part in enumerate(parts)
        ]

    def target_order(self, width, lead):
        shard = width // self.count
        order = jnp.arange(width, dtype=jnp.int32)
        inside, rest = order % shard, order // shard
        k, rest = rest % self.nz, rest // self.nz
        if lead == "x":
            dy, dx = rest % self.ny, rest // self.ny
        else:
            dx, dy = rest % self.nx, rest // self.nx
        y, x = (self.y + dy) % self.ny, (self.x + dx) % self.nx
        source = self.at((self.z + k) % self.nz, y, x) * shard + inside
        return (order[:, None] == source[None, :]).astype(jnp.bfloat16)

    def scatter_far(self, by_x, by_y, right):
        wire = jnp.bfloat16
        if not self.square:
            line = by_x.shape[1] // self.plane
            starts = [(dx * self.ny + dy) * line for dy, dx in self.steps]
            parts = [contract_rows(by_x[:, start : start + line], right) for start in starts]
            return parts[:1] + [part.astype(wire) for part in parts[1:]]
        half, far = right.shape[1] // 2, by_x.shape[1] // 2
        return [
            contract_rows(by_x[:, far:], right[:, :half]).astype(wire),
            contract_rows(by_y[:, far:], right[:, half:]).astype(wire),
        ]

    def scatter_near(self, by_x, by_y, right):
        if not self.square:
            return []
        half, far = right.shape[1] // 2, by_x.shape[1] // 2
        return [
            contract_rows(by_x[:, :far], right[:, :half]),
            contract_rows(by_y[:, :far], right[:, half:]),
        ]

    def rows_first(self, width):
        return width // self.cores // self.nx

    def line_parts(self, terms):
        total = sum(t.astype(jnp.float32) for t in terms)
        shard = total.shape[0] // self.nz
        parts = [total[k * shard : (k + 1) * shard] for k in range(self.nz)]
        return parts[:1] + [part.astype(jnp.bfloat16) for part in parts[1:]]

    def all_tokens(self, value):
        return jnp.concatenate(
            [value] + [self.other_core(value, step) for step in range(1, self.cores)], axis=0
        )

    def core_columns(self, value):
        width = value.shape[1] // self.cores
        starts = [((self.core + step) % self.cores) * width for step in range(self.cores)]
        return [lax.dynamic_slice(value, (0, start), (value.shape[0], width)) for start in starts]

    def to_cores(self, pieces):
        return [
            piece if step == 0 else self.other_core(piece, step)
            for step, piece in enumerate(pieces)
        ]


COLUMNS = 1024
BESIDE = pl.CostEstimate(flops=1, bytes_accessed=1, transcendentals=0)


def fold(came, near, far, more):
    rows, width = near[0].shape
    line = rows // 2
    ahead = rows if far else 0
    extra = [m.shape[0] if m is not None else 0 for m in more]
    low, full = jnp.bfloat16, jnp.float32

    def body(*refs):
        came_refs, near_refs, refs = refs[:2], refs[2:4], refs[4:]
        far_refs, refs = refs[: len(far)], refs[len(far) :]
        more_refs, (out_x, out_y, keep_x, keep_y) = list(refs[:-4]), refs[-4:]
        sums = [
            n[...] + c[:rows, :].astype(full) for n, c in zip(near_refs, came_refs, strict=True)
        ]
        keep_x[...], keep_y[...] = sums[0][:line], sums[1][:line]
        out_x[ahead : ahead + line, :] = sums[1][line:].astype(low)
        out_y[ahead : ahead + line, :] = sums[0][line:].astype(low)
        for out, far_ref in zip((out_x, out_y), far_refs, strict=False):
            out[:ahead, :] = far_ref[...]
        for out, count in zip((out_x, out_y), extra, strict=True):
            if count:
                out[ahead + line :, :] = more_refs.pop(0)[...]

    outs = [ahead + line + extra[0], ahead + line + extra[1], line, line]
    return pl.pallas_call(
        body,
        out_shape=[
            jax.ShapeDtypeStruct((count, width), dtype)
            for count, dtype in zip(outs, (low, low, full, full), strict=True)
        ],
        compiler_params=pltpu.CompilerParams(vmem_limit_bytes=40 << 20),
        cost_estimate=BESIDE,
    )(*came, *near, *far, *[m for m in more if m is not None])


def line_fold(came, at, keep, count, more):
    line, width = keep[0].shape
    each = line // count
    full = jnp.float32

    def body(came_x, came_y, keep_x, keep_y, *refs):
        for p, out in enumerate(refs[-count:]):
            rows = slice(p * each, (p + 1) * each)
            out[:each, :width] = (keep_x[rows, :] + came_y[rows, :].astype(full)).astype(out.dtype)
            out[:each, width:] = (keep_y[rows, :] + came_x[rows, :].astype(full)).astype(out.dtype)
            if more:
                out[each:, :] = refs[p][...]

    def whole(shape):
        return pl.BlockSpec(shape, lambda i: (0, 0))

    shape = (each + (more[0].shape[0] if more else 0), 2 * width)
    return pl.pallas_call(
        body,
        grid=(1,),
        in_specs=[pl.BlockSpec((line, width), lambda i: (at // line, 0))] * 2
        + [whole(value.shape) for value in (*keep, *more)],
        out_specs=[whole(shape)] * count,
        out_shape=[
            jax.ShapeDtypeStruct(shape, full if p == 0 else jnp.bfloat16) for p in range(count)
        ],
        compiler_params=pltpu.CompilerParams(vmem_limit_bytes=40 << 20),
        cost_estimate=BESIDE,
    )(*came, *keep, *more)


def times_gathered(left, pieces, start, stop, so_far=None):
    plane, _, shard, width = pieces[0].shape
    rows, tiles = plane * shard, width // COLUMNS

    def body(left_ref, *refs):
        *piece_refs, out_ref = refs
        total = None if so_far is None else piece_refs.pop()[...]
        for i, piece_ref in enumerate(piece_refs):
            part = left_ref[:, i * rows : (i + 1) * rows]
            term = jnp.dot(
                part, piece_ref[...].reshape(rows, COLUMNS), preferred_element_type=jnp.float32
            )
            total = term if total is None else total + term
        out_ref[...] = total

    depth = (stop - start) * width
    out_spec = pl.BlockSpec((left.shape[0], COLUMNS), lambda w, j: (0, w * tiles + j))
    piece_spec = pl.BlockSpec((plane, 1, shard, COLUMNS), lambda w, j: (0, w + start, 0, j))
    return pl.pallas_call(
        body,
        grid=(stop - start, tiles),
        in_specs=[pl.BlockSpec(left.shape, lambda w, j: (0, 0))]
        + [piece_spec] * len(pieces)
        + [out_spec] * (so_far is not None),
        out_specs=out_spec,
        out_shape=jax.ShapeDtypeStruct((left.shape[0], depth), jnp.float32),
        compiler_params=pltpu.CompilerParams(vmem_limit_bytes=40 << 20),
        cost_estimate=BESIDE,
    )(left, *pieces, *([] if so_far is None else [so_far]))


def times_transposed(left, pieces, start, stop):
    plane, _, shard, width = pieces[0].shape
    rows, tiles = plane * shard, width // COLUMNS
    out_shape = (left.shape[1], rows * len(pieces))

    def body(left_ref, *refs):
        *piece_refs, out_ref = refs

        @pl.when((pl.program_id(0) == 0) & (pl.program_id(1) == 0))
        def _():
            out_ref[...] = jnp.zeros_like(out_ref)

        for i, piece_ref in enumerate(piece_refs):
            out_ref[:, i * rows : (i + 1) * rows] += lax.dot_general(
                left_ref[0],
                piece_ref[...].reshape(rows, COLUMNS),
                (((1,), (1,)), ((), ())),
                preferred_element_type=jnp.float32,
            )

    piece_spec = pl.BlockSpec((plane, 1, shard, COLUMNS), lambda w, j: (0, w + start, 0, j))
    return pl.pallas_call(
        body,
        grid=(stop - start, tiles),
        in_specs=[pl.BlockSpec((1, left.shape[1], COLUMNS), lambda w, j: (left.shape[0] - 1 - w, 0, j))]
        + [piece_spec] * len(pieces),
        out_specs=pl.BlockSpec(out_shape, lambda w, j: (0, 0)),
        out_shape=jax.ShapeDtypeStruct(out_shape, jnp.float32),
        compiler_params=pltpu.CompilerParams(vmem_limit_bytes=40 << 20),
        cost_estimate=BESIDE,
    )(left, *pieces)


GROUP = 8


def attention(projected, gains, tables, doc_ids, heads):
    length, width = projected.shape[0], projected.shape[1] // 3
    low, full = jnp.bfloat16, jnp.float32
    scale = HD ** (-0.5)

    def body(raw_ref, gain_ref, cos_ref, sin_ref, row_ref, col_ref,
             query_ref, key_ref, value_ref, out_ref, prob_ref, inv_ref, seen_ref):
        first = pl.program_id(0) * GROUP

        @pl.when(first == 0)
        def _():
            for i in (0, 1):
                raw = raw_ref[:, i * width : (i + 1) * width]
                mean = jnp.mean(raw * raw, axis=-1, keepdims=True)
                inv_ref[:, i : i + 1] = lax.rsqrt(mean + EPS)
            at = lax.broadcasted_iota(jnp.int32, (length, length), 0)
            to = lax.broadcasted_iota(jnp.int32, (length, length), 1)
            seen = (row_ref[...] == col_ref[...]) & (at >= to)
            seen_ref[...] = jnp.where(seen, 1.0, 0.0)

        def turned(i, head):
            raw = raw_ref[:, pl.ds(pl.multiple_of(i * width + head * HD, HD), HD)]
            gain = gain_ref[i + 1 : i + 2, pl.ds(pl.multiple_of(head * HD, HD), HD)]
            value = raw * inv_ref[:, i : i + 1] * gain
            return (value * cos_ref[...] + pltpu.roll(value, HD // 2, 1) * sin_ref[...]).astype(low)

        for g in range(GROUP):
            at = slice(g * HD, (g + 1) * HD)
            query, key = turned(0, first + g), turned(1, first + g)
            value_at = pl.multiple_of(2 * width + (first + g) * HD, HD)
            value = raw_ref[:, pl.ds(value_at, HD)].astype(low)
            scores = lax.dot_general(
                query, key, (((1,), (1,)), ((), ())), preferred_element_type=full
            ) * scale
            scores = jnp.where(seen_ref[...] > 0.0, scores, MASKED)
            expo = jnp.exp(scores - jnp.max(scores, axis=-1, keepdims=True))
            probs = expo / jnp.sum(expo, axis=-1, keepdims=True)
            prob_ref[g] = probs
            out = jnp.dot(probs.astype(low), value, preferred_element_type=full)
            out_ref[:, at] = out.astype(low)
            query_ref[:, at], key_ref[:, at], value_ref[:, at] = query, key, value

    def whole(shape):
        return pl.BlockSpec(shape, lambda h: (0,) * len(shape))

    part = pl.BlockSpec((length, GROUP * HD), lambda h: (0, h))
    flat = jax.ShapeDtypeStruct((length, width), low)
    return pl.pallas_call(
        body,
        grid=(heads // GROUP,),
        in_specs=[
            whole(projected.shape), whole(gains.shape), whole((length, HD)), whole((length, HD)),
            whole((length, 1)), whole((1, length)),
        ],
        out_specs=[part, part, part, part,
                   pl.BlockSpec((GROUP, length, length), lambda h: (h, 0, 0)), whole((length, LANES))],
        out_shape=[flat, flat, flat, flat,
                   jax.ShapeDtypeStruct((heads, length, length), full),
                   jax.ShapeDtypeStruct((length, LANES), full)],
        scratch_shapes=[pltpu.VMEM((length, length), full)],
        compiler_params=pltpu.CompilerParams(vmem_limit_bytes=40 << 20),
        cost_estimate=BESIDE,
    )(projected, gains, *tables, doc_ids.reshape(length, 1), doc_ids.reshape(1, length))


def attention_back(grad_out, query, key, value, probs, projected, inverses, gains, tables, heads):
    length, width = grad_out.shape
    low, full = jnp.bfloat16, jnp.float32
    scale = HD ** (-0.5)

    def body(grad_ref, query_ref, key_ref, value_ref, prob_ref, raw_ref, inv_ref, gain_ref,
             cos_ref, sin_ref, out_ref, dgain_ref, turned_ref, inner_ref):
        first = pl.program_id(0) * GROUP

        @pl.when(first == 0)
        def _():
            inner_ref[...] = jnp.zeros_like(inner_ref)

        for g in range(GROUP):
            head, part = first + g, slice(g * HD, (g + 1) * HD)
            here = pl.multiple_of(head * HD, HD)
            grad, probs = grad_ref[:, part], prob_ref[g]
            grad_probs = lax.dot_general(
                grad, value_ref[:, part], (((1,), (1,)), ((), ())), preferred_element_type=full
            )
            out_ref[0, :, pl.ds(here, HD)] = lax.dot_general(
                probs.astype(low), grad, (((0,), (0,)), ((), ())), preferred_element_type=full
            ).astype(low)
            inner = jnp.sum(probs * grad_probs, axis=-1, keepdims=True)
            grad_scores = (probs * (grad_probs - inner)).astype(low)
            rotated = (
                jnp.dot(grad_scores, key_ref[:, part], preferred_element_type=full) * scale,
                lax.dot_general(
                    grad_scores, query_ref[:, part], (((0,), (0,)), ((), ())),
                    preferred_element_type=full,
                ) * scale,
            )
            for i in (0, 1):
                back = rotated[i] * cos_ref[...] - pltpu.roll(rotated[i], HD // 2, 1) * sin_ref[...]
                at = pl.ds(pl.multiple_of(i * width + head * HD, HD), HD)
                turned_ref[:, at] = back
                normed = raw_ref[:, at] * inv_ref[:, i : i + 1]
                dgain_ref[i : i + 1, pl.ds(here, HD)] = jnp.sum(back * normed, axis=0, keepdims=True)
                weighed = back * gain_ref[i + 1 : i + 2, pl.ds(here, HD)]
                inner_ref[:, i : i + 1] += jnp.sum(weighed * normed, axis=-1, keepdims=True)

        @pl.when(first == heads - GROUP)
        def _():
            for i in (0, 1):
                inverse = inv_ref[:, i : i + 1]
                inner = inner_ref[:, i : i + 1] * (1.0 / width)

                @pl.loop(0, heads)
                def _(j):
                    at = pl.ds(pl.multiple_of(i * width + j * HD, HD), HD)
                    there = pl.ds(pl.multiple_of(j * HD, HD), HD)
                    weighed = turned_ref[:, at] * gain_ref[i + 1 : i + 2, there]
                    normed = raw_ref[:, at] * inverse
                    out_ref[2 - i, :, there] = (inverse * (weighed - normed * inner)).astype(low)

    def whole(shape):
        return pl.BlockSpec(shape, lambda h: (0,) * len(shape))

    part = pl.BlockSpec((length, GROUP * HD), lambda h: (0, h))
    return pl.pallas_call(
        body,
        grid=(heads // GROUP,),
        in_specs=[
            part, part, part, part,
            pl.BlockSpec((GROUP, length, length), lambda h: (h, 0, 0)),
            whole((length, 2 * width)), whole(inverses.shape), whole(gains.shape),
            whole((length, HD)), whole((length, HD)),
        ],
        out_specs=[whole((3, length, width)), whole((8, width))],
        out_shape=[
            jax.ShapeDtypeStruct((3, length, width), low), jax.ShapeDtypeStruct((8, width), full)
        ],
        scratch_shapes=[pltpu.VMEM((length, 2 * width), full), pltpu.VMEM((length, LANES), full)],
        compiler_params=pltpu.CompilerParams(vmem_limit_bytes=40 << 20),
        cost_estimate=BESIDE,
    )(grad_out, query, key, value, probs, projected, inverses, gains, *tables)


def expert_back(pieces, grad_y, tail, pre_gate, pre_up, gate_w, up_w, down_w):
    total, width = grad_y.shape
    rows = min(512, total)
    pieces = pieces if rows == total else 1
    hidden = pre_gate.shape[1]
    low, full = jnp.bfloat16, jnp.float32
    tile = min(512, hidden)

    def body(grad_y_ref, tail_ref, a_ref, b_ref, gate_w_ref, up_w_ref, down_w_ref, *refs):
        back_refs, (grad_a_ref, grad_b_ref, sum_ref) = refs[:pieces], refs[pieces:]
        each = rows // pieces
        step = pl.program_id(1)

        @pl.when(step == 0)
        def _():
            for p, back_ref in enumerate(back_refs):
                back_ref[:, width:] = tail_ref[p * each : (p + 1) * each, :]
            sum_ref[...] = jnp.zeros_like(sum_ref)

        grad_act = lax.dot_general(
            grad_y_ref[...], down_w_ref[...], (((1,), (1,)), ((), ())), preferred_element_type=full
        )
        pre_gate, pre_up = a_ref[...], b_ref[...]
        sigmoid_g = jax.nn.sigmoid(pre_gate)
        slope = sigmoid_g * (1.0 + pre_gate * (1.0 - sigmoid_g))
        grad_a = (grad_act * pre_up * slope).astype(low)
        grad_b = (grad_act * (pre_gate * sigmoid_g)).astype(low)
        grad_a_ref[...], grad_b_ref[...] = grad_a, grad_b
        contract = (((1,), (1,)), ((), ()))
        sum_ref[...] += lax.dot_general(
            grad_a, gate_w_ref[...], contract, preferred_element_type=full
        ) + lax.dot_general(grad_b, up_w_ref[...], contract, preferred_element_type=full)

        @pl.when(step == hidden // tile - 1)
        def _():
            for p, back_ref in enumerate(back_refs):
                back_ref[:, :width] = sum_ref[p * each : (p + 1) * each, :].astype(low)

    def whole(columns):
        return pl.BlockSpec((rows, columns), lambda r, f: (r, 0))

    inner = pl.BlockSpec((rows, tile), lambda r, f: (r, f))
    into = pl.BlockSpec((width, tile), lambda r, f: (0, f))
    outs = pl.pallas_call(
        body,
        grid=(total // rows, hidden // tile),
        in_specs=[
            whole(width), whole(LANES), inner, inner, into, into,
            pl.BlockSpec((tile, width), lambda r, f: (f, 0)),
        ],
        out_specs=[pl.BlockSpec((rows // pieces, width + LANES), lambda r, f: (r, 0))] * pieces
        + [inner, inner],
        out_shape=[jax.ShapeDtypeStruct((total // pieces, width + LANES), low)] * pieces
        + [jax.ShapeDtypeStruct(pre_gate.shape, low)] * 2,
        scratch_shapes=[pltpu.VMEM((rows, width), full)],
        compiler_params=pltpu.CompilerParams(vmem_limit_bytes=52 << 20),
        cost_estimate=BESIDE,
    )(grad_y, tail, pre_gate, pre_up, gate_w, up_w, down_w)
    return (outs[:pieces], *outs[pieces:])


def rows_product(lefts, rights):
    rows, height = lefts[0].shape
    width = rights[0].shape[1]
    tile = min(512, height)

    def body(*refs):
        out_ref = refs[-1]
        total = None
        for left_ref, right_ref in zip(refs[: len(lefts)], refs[len(lefts) : -1], strict=True):
            term = lax.dot_general(
                left_ref[...], right_ref[...], (((0,), (0,)), ((), ())),
                preferred_element_type=jnp.float32,
            )
            total = term if total is None else total + term
        out_ref[...] = total

    return pl.pallas_call(
        body,
        grid=(height // tile,),
        in_specs=[pl.BlockSpec((rows, tile), lambda i: (0, i))] * len(lefts)
        + [pl.BlockSpec((rows, width), lambda i: (0, 0))] * len(rights),
        out_specs=pl.BlockSpec((tile, width), lambda i: (i, 0)),
        out_shape=jax.ShapeDtypeStruct((height, width), jnp.float32),
        compiler_params=pltpu.CompilerParams(vmem_limit_bytes=52 << 20),
        cost_estimate=BESIDE,
    )(*lefts, *rights)


def input_gradient(grad, sources, tokens, inverse, gain, residual):
    length, width = grad.shape
    tile = 512
    low, full = jnp.bfloat16, jnp.float32

    def body(grad_ref, source_ref, token_ref, inverse_ref, gain_ref, residual_ref,
             out_ref, dgain_ref, split_ref, placed_ref, inner_ref):
        step = pl.program_id(0)

        @pl.when(step == 0)
        def _():
            high = grad_ref[...].astype(low)
            split_ref[:length, :] = high
            split_ref[length:, :] = (grad_ref[...] - high.astype(full)).astype(low)
            inner_ref[...] = jnp.zeros_like(inner_ref)

        at = pl.ds(pl.multiple_of(step * tile, tile), tile)
        column = step * tile + lax.broadcasted_iota(jnp.int32, (tile, width), 0)
        arrival = jnp.where(column == source_ref[...], 1.0, 0.0).astype(low)
        placed = lax.dot_general(
            split_ref[...], arrival, (((1,), (1,)), ((), ())), preferred_element_type=full
        )
        placed = placed[:length] + placed[length:]
        placed_ref[:, at] = placed
        normed = token_ref[:, at].astype(full) * inverse_ref[...]
        dgain_ref[:, at] = jnp.broadcast_to(
            jnp.sum(placed * normed, axis=0, keepdims=True), (dgain_ref.shape[0], tile)
        )
        weighed = placed * gain_ref[:, at]
        inner_ref[:, :1] += jnp.sum(weighed * normed, axis=-1, keepdims=True)

        @pl.when(step == width // tile - 1)
        def _():
            inner = inner_ref[:, :1] * (1.0 / width)
            inverse = inverse_ref[...]

            @pl.loop(0, width // tile)
            def _(j):
                at = pl.ds(pl.multiple_of(j * tile, tile), tile)
                normed = token_ref[:, at].astype(full) * inverse
                back = inverse * (placed_ref[:, at] * gain_ref[:, at] - normed * inner)
                out_ref[:, at] = (residual_ref[:, at] + back).astype(low)

    def whole(shape):
        return pl.BlockSpec(shape, lambda j: (0,) * len(shape))

    return pl.pallas_call(
        body,
        grid=(width // tile,),
        in_specs=[
            whole(grad.shape), whole(sources.shape), whole(tokens.shape),
            whole(inverse.shape), whole(gain.shape), whole(residual.shape),
        ],
        out_specs=[whole(tokens.shape), whole((8, width))],
        out_shape=[
            jax.ShapeDtypeStruct(tokens.shape, low), jax.ShapeDtypeStruct((8, width), full)
        ],
        scratch_shapes=[
            pltpu.VMEM((2 * length, width), low),
            pltpu.VMEM((length, width), full),
            pltpu.VMEM((length, LANES), full),
        ],
        compiler_params=pltpu.CompilerParams(vmem_limit_bytes=40 << 20),
        cost_estimate=BESIDE,
    )(grad, sources, tokens, inverse, gain, residual)


def rope_tables(length):
    half = HD // 2
    freq = THETA ** (-(jnp.arange(half, dtype=jnp.float32) * 2.0) / HD)
    angle = jnp.arange(length, dtype=jnp.float32)[:, None] * freq[None, :]
    sine = jnp.sin(angle)
    cosine = jnp.cos(angle)
    return (
        jnp.concatenate([cosine, cosine], axis=-1),
        jnp.concatenate([-sine, sine], axis=-1),
    )


def on_device(
    tokens,
    segments,
    expert_ids,
    norm_gains,
    w_query,
    w_key,
    w_value,
    w_out,
    w_router,
    expert_gate,
    expert_up,
    expert_down,
    cotangent,
):
    bfloat = jnp.bfloat16
    here = Places()
    length, width = tokens.shape
    topk = expert_ids.shape[1]
    experts = here.count
    capacity = length * topk // experts
    heads = width // HD
    shard = w_query.shape[0]
    plane = here.plane
    gate_w, up_w, down_w = expert_gate[0], expert_up[0], expert_down[0]

    labels = jnp.arange(experts, dtype=jnp.int32)
    named = jnp.any(expert_ids[:, :, None] == labels[None, None, :], axis=1)
    places = jnp.arange(length, dtype=jnp.int32)
    earlier = (places[:, None] < places[None, :]).astype(bfloat)
    slots = contract_rows(named.astype(bfloat), earlier)
    slots = jnp.where(named.T & (slots < capacity), slots, -1.0).astype(bfloat)

    order = range(here.nz)
    arrival, sources = here.arrival(width)
    extra = norm_gains.shape[0] + w_router.shape[1]
    smalls = jnp.concatenate(
        [norm_gains.T, w_router, jnp.zeros((shard, -extra % LANES), jnp.float32)], axis=1
    ).astype(bfloat)
    smalls = jnp.concatenate([smalls, slots.reshape(-1, LANES)], axis=0)
    smalls = here.along_whole_line([smalls] * here.nz)
    plane_expert = jnp.stack(
        [
            here.at(here.z, (here.y + dy) % here.ny, (here.x + dx) % here.nx)
            for dy, dx in here.steps
        ]
    )
    chosen = plane_expert[:, None] == labels[None, :]
    slot_ids = jnp.arange(capacity, dtype=jnp.int32)
    spreads = []

    def spread_of(part):
        picked = jnp.sum(
            jnp.where(chosen[:, :, None], part[None].astype(jnp.float32), 0.0), axis=1
        ).astype(jnp.int32)
        hit = picked[:, None, :] == slot_ids[None, :, None]
        return hit.astype(bfloat).reshape(plane * capacity, length)

    def rows_of(spread, part):
        return list(product(spread, part).astype(bfloat).reshape(plane, capacity, -1))

    def parted(rows):
        return list(rows.reshape(plane, capacity, -1))

    def joined(rows):
        return jnp.concatenate(rows, axis=0)

    inputs = tokens.astype(jnp.float32)
    weights = jnp.stack([w_query, w_key, w_value, w_out]).astype(bfloat)
    line, cot_line = Spread(here, weights), Spread(here, cotangent)
    half = weights.shape[0] // 2
    raw, chunks, pieces = [], [], []
    projected = None
    depth = width // here.nz
    cot_rows, rows_cot = [None] * here.nz, [None] * here.nz

    def stacked(rows):
        return rows.reshape(-1, shard, width)

    def chunk_of(k):
        if here.square:
            at = 2 * half if k + 1 < here.nz else 0
            blocks = [line.queue[k]] + [by[: 2 * half] for by in raw[k][:2]]
            blocks += [by[at : at + half] for by in raw[k + 1][:2]]
        else:
            blocks = raw[k]
        return jnp.concatenate(blocks, axis=0).reshape(plane, *weights.shape)

    def share(chunk):
        return [chunk] + [here.other_core(chunk, s) for s in range(1, here.cores)]

    def project(k):
        return times_gathered(
            in_order[:, k * depth : (k + 1) * depth], pieces[k], 0, 3, projected
        )

    for k in range(here.nz + 2):
        outs = []
        if here.square:
            by_x, by_y = [], []
            if k < here.nz:
                by_x.append(line.queue[k])
                by_y.append(line.queue[k])
            if 0 < k <= here.nz:
                by_x.append(raw[k - 1][1][:half])
                by_y.append(raw[k - 1][0][half : 2 * half])
            if k >= here.nz:
                by_x.append(stacked(cot_rows[k - here.nz][1]))
                by_y.append(stacked(cot_rows[k - here.nz][2]))
            outs = [jnp.concatenate(by_x, axis=0), jnp.concatenate(by_y, axis=0)]
            if k > here.nz:
                outs.append(jnp.concatenate([cot_rows[0][3], cot_rows[1][3]], axis=0))
        elif k < here.nz:
            outs = [line.queue[k]] * plane
        else:
            outs = cot_rows[k - here.nz]
        if k == 1:
            outs, smalls, raw, line.queue = tie(outs, smalls, raw, line.queue)
            turned = jnp.stack(smalls).reshape(here.nz, -1)
            near = (here.z - here.queue_of(jnp.arange(here.nz))) % here.nz
            pick = (near[:, None] == jnp.arange(here.nz)[None, :]).astype(bfloat)
            turned = product(pick, turned).astype(bfloat).reshape(here.nz, -1, LANES)
            smalls, slots = turned[:, :shard], turned[:, shard:]
            smalls = here.along_plane([smalls] * plane)
        outs, smalls, slots, raw, chunks, line.queue, cot_line.queue, cot_rows, cotangent = tie(
            outs, smalls, slots, raw, chunks, line.queue, cot_line.queue, cot_rows, cotangent
        )
        if here.square:
            ins = [here.shift_plane(outs[0], 0, 1), here.shift_plane(outs[1], 1, 0)]
            if k > here.nz:
                ins.append(here.shift_plane(outs[2], 1, 1))
        else:
            ins = here.along_plane(outs)
        moving = line.step() if k < here.nz else []
        moving_cot = cot_line.step() if k >= here.nz - 1 else []
        if k == 1:
            spreads = [spread_of(part.reshape(experts, length)) for part in slots]
        if k > 2:
            pieces.append(share(chunks[k - 3]))
        if k > 1:
            chunks.append(chunk_of(k - 2))
        if k == 1:
            smalls = jnp.stack(smalls, axis=1)
            smalls = [smalls] + [here.other_core(smalls, s) for s in range(1, here.cores)]
            smalls = jnp.stack(smalls, axis=1).reshape(width, -1)
            smalls = product(arrival, smalls).astype(bfloat)
            smalls, sources = tie(smalls, sources)
        if k == 3:
            gains_f = smalls[:, : norm_gains.shape[0]].T.astype(jnp.float32)
            wr = smalls[:, norm_gains.shape[0] : extra]
            normed_in_f, normed_one, inverse_one = norm_rows(inputs, gains_f[0])
            normed_in = normed_in_f.astype(bfloat)
            in_order = product(normed_in, arrival).astype(bfloat)
        if k > 2:
            projected = project(k - 3)
        if k >= here.nz - 1 and k - here.nz + 1 < here.nz:
            at = k - here.nz + 1
            cot_rows[at] = rows_of(spreads[at], cot_line.queue[at])
        ins, moving, moving_cot, smalls, projected, cot_rows, spreads, chunks = tie(
            ins, moving, moving_cot, smalls, projected, cot_rows, spreads, chunks
        )
        line.land(moving)
        cot_line.land(moving_cot)
        raw.append(ins)
        if k >= here.nz:
            rows_cot[k - here.nz] = ins
            if here.square:
                own = cot_rows[k - here.nz][0]
                skip = half if k == here.nz else 0
                rows_cot[k - here.nz] = [own] + [by[skip:].reshape(own.shape) for by in ins[:2]]
            if here.square and k > here.nz:
                for i in (0, 1):
                    rows_cot[i].append(ins[2][i * capacity : (i + 1) * capacity])

    order_x = here.target_order(width // here.cores, "x")
    order_y = here.target_order(width // here.cores, "y")

    def targeted(columns):
        columns = jnp.concatenate(columns, axis=0)
        return [product(columns, o).astype(bfloat) for o in (order_x, order_y)]

    merged = []
    if here.nz > 2:
        cot_rows[3] = rows_of(spreads[3], cot_line.queue[3])
        merged = [joined(pair) for pair in zip(*cot_rows[2:], strict=True)]
    in_columns = here.core_columns(normed_in)
    merged, chunks, projected, pieces, in_columns = tie(
        merged, chunks, projected, pieces, in_columns
    )
    ins = here.along_plane(merged) if merged else []
    pieces.append(share(chunks[-1]))
    in_columns = here.to_cores(in_columns)
    projected = project(here.nz - 1)
    pieces = [piece for chunk in pieces for piece in chunk]
    tables = rope_tables(length)
    query_rot, key_rot, values, attended, probs, inverses = attention(
        projected, gains_f, tables, segments[0], heads
    )
    residual = inputs + times_gathered(product(attended, arrival).astype(bfloat), pieces, 3, 4)
    normed_mid_f, normed_two, inverse_two = norm_rows(residual, gains_f[3])
    normed_mid = normed_mid_f.astype(bfloat)

    own_label = labels[None, :] == here.me

    def expert_forward(arrived, cot):
        route_here = jax.nn.softmax(product(arrived, wr), axis=-1)
        gate = jnp.sum(jnp.where(own_label, route_here, 0.0), axis=-1)
        gate = gate.astype(bfloat).astype(jnp.float32)[:, None]
        pre_gate = product(arrived, gate_w)
        pre_up = product(arrived, up_w)
        activated = (jax.nn.silu(pre_gate) * pre_up).astype(bfloat)
        result = product(activated, down_w).astype(bfloat).astype(jnp.float32)
        gated = (gate * result).astype(bfloat)
        cot = cot.astype(jnp.float32)
        grad_y = (gate * cot).astype(bfloat)
        grad_g = jnp.sum(cot * result, axis=-1, keepdims=True)
        high = grad_g.astype(bfloat)
        low = (grad_g - high.astype(jnp.float32)).astype(bfloat)
        lanes = jnp.arange(LANES, dtype=jnp.int32)[None, :]
        tail = jnp.where(lanes == here.me, high, jnp.zeros((), bfloat))
        tail = jnp.where(lanes == here.me + LANES // 2, low, tail)
        return (pre_gate, pre_up, activated, gated, grad_y, tail)

    def expert_backward(kept):
        pre_gate, pre_up, _, _, grad_y, tail = kept
        back, grad_a, grad_b = expert_back(
            plane, grad_y, tail, pre_gate, pre_up, gate_w, up_w, down_w
        )
        return [back if len(back) == plane else parted(back[0]), grad_y, grad_a, grad_b]

    rows_next = rows_of(spreads[0], normed_mid)
    out_columns = here.core_columns(attended)
    normed_mid, rows_next, ins, in_columns, out_columns = tie(
        normed_mid, rows_next, ins, in_columns, out_columns
    )
    if here.nz > 2:
        rows_cot[2:] = [[row[i : i + capacity] for row in ins] for i in (0, capacity)]
    line = Spread(here, normed_mid)
    rows_in, forward = [], []
    for k in order:
        if k > 0:
            rows_next = rows_of(spreads[k], line.queue[k])
        rows_next, rows_in, line.queue, out_columns = tie(
            rows_next, rows_in, line.queue, out_columns
        )
        moving = line.step()
        rows = here.along_plane(rows_next)
        if k > 0:
            rows_in[-1] = joined(rows_in[-1])
            forward.append(expert_forward(rows_in[-1], joined(rows_cot[k - 1])))
        if k == 0:
            targets = targeted(in_columns)
            rows, targets = tie(rows, targets)
        if k == here.nz // 2:
            out_columns = here.to_cores(out_columns)
        if k == here.nz - 1:
            out_columns = targeted(out_columns)
            rows_cot[k] = joined(rows_cot[k])
            rows, rows_cot[k] = tie(rows, rows_cot[k])
        moving, rows, forward, out_columns = tie(moving, rows, forward, out_columns)
        rows_in.append(rows)
        line.land(moving)

    targets_out = out_columns
    half = here.nz // 2
    back_y = [None] * here.nz
    backward = [None] * here.nz
    todo = ["forward", *reversed(order)]

    def work():
        k = todo.pop(0) if todo else None
        if k == "forward":
            rows_in[-1] = joined(rows_in[-1])
            forward.append(expert_forward(rows_in[-1], rows_cot[-1]))
        elif k is not None:
            backward[k] = expert_backward(forward[k])

    rows_next = parted(forward[0][3])
    rows_next, forward, rows_in, rows_cot, out_columns = tie(
        rows_next, forward, rows_in, rows_cot, out_columns
    )
    rows = here.deal_back(rows_next)
    work()
    work()
    rows, forward, backward = tie(rows, forward, backward)
    back_y[0] = rows
    collect, parts = Collect(here), [None] * here.nz
    moving, sending, back = [], [], None
    for k in reversed(order):
        rows_next = backward[k][0]
        if k + 2 < here.nz:
            collect.land(moving)
            sending = collect.add(k + 2, parts[k + 2])
        rows_next, sending, forward, backward = tie(rows_next, sending, forward, backward)
        rows = here.deal_back(rows_next)
        moving = collect.send(sending)
        if k > 0:
            work()
        else:
            grad_down = rows_product(
                [kept[2] for kept in forward], [kept[1] for kept in backward]
            )
            rows, grad_down = tie(rows, grad_down)
        if back is not None:
            parts[k + 1] = contract_rows(spreads[k + 1], joined(back))
        moving, rows[:-1], forward, backward, parts = tie(
            moving, rows[:-1], forward, backward, parts
        )
        back = rows
    late = list(order[:0:-1])
    collect.land(moving)
    sending = collect.add(1, parts[1])
    rows_next = parted(forward[late[0]][3])
    rows_next, sending, back_y = tie(rows_next, sending, back_y)
    rows = here.deal_back(rows_next)
    moving = collect.send(sending)
    parts[0] = contract_rows(spreads[0], joined(back))
    part_y = contract_rows(spreads[0], joined(back_y[0]))
    rows_next = [parted(forward[k][3]) for k in late[1:]]
    moving, rows, parts, rows_next, part_y = tie(moving, rows, parts, rows_next, part_y)
    collect.land(moving)
    collect.add(0, parts[0])
    returned = collect.total
    back_y[late[0]] = rows
    parts_y = [None] * here.nz
    parts_y[0] = part_y
    if rows_next:
        back_y[late[1]] = here.deal_back(rows_next[0])

    def add_up_y(k):
        parts_y[k] = contract_rows(spreads[k], joined(back_y[k]))

    add_up_y(late[0])

    grad_mid = returned[:, :width]
    grad_route = (
        returned[:, width : width + experts]
        + returned[:, width + LANES // 2 : width + LANES // 2 + experts]
    )
    route = jax.nn.softmax(product(normed_mid, wr), axis=-1)
    grad_logits = (
        route * (grad_route - jnp.sum(route * grad_route, axis=-1, keepdims=True))
    ).astype(bfloat)
    grad_router = contract_rows(normed_mid, grad_logits)
    grad_mid = grad_mid + contract_cols(grad_logits, wr)
    grad_res_two, grad_gain_mid = norm_back(grad_mid, gains_f[3], normed_two, inverse_two)
    grad_residual = cotangent.astype(jnp.float32) + grad_res_two
    grad_attn = grad_residual.astype(bfloat)
    grad_attended = times_transposed(grad_attn[None], pieces, 3, 4).astype(bfloat)
    grad_attended = contract_cols(grad_attended, arrival).astype(bfloat)
    collect_y, adds_y = Collect(here), list(reversed(order))
    grad_attended, grad_attn, back_y, parts_y = tie(grad_attended, grad_attn, back_y, parts_y)
    sending_y = collect_y.add(adds_y[0], parts_y[adds_y.pop(0)])
    sending_y, grad_attended, grad_attn, back_y, rows_next = tie(
        sending_y, grad_attended, grad_attn, back_y, rows_next
    )
    if rows_next:
        back_y[late[2]] = here.deal_back(rows_next[1])
    moving = collect_y.send(sending_y)
    out_tokens = here.all_tokens(grad_attn)
    grads, grad_gain_heads = attention_back(
        grad_attended, query_rot, key_rot, values, probs, projected, inverses, gains_f, tables, heads
    )
    far = here.scatter_far(*targets_out, out_tokens)
    for k in late[1:2]:
        add_up_y(k)
    grads, far, back_y, parts_y, moving, out_tokens = tie(
        grads, far, back_y, parts_y, moving, out_tokens
    )

    def arrive(outs):
        if not here.square:
            return here.along_plane(outs) if outs else []
        return [here.shift_plane(outs[0], 0, 1), here.shift_plane(outs[1], 1, 0)]

    jobs = 4
    lefts, rights = [targets_out, targets, targets, targets], [out_tokens]
    shares, others, grad_in_norm = [], [], None
    near, near_last, ins, small, smalls, expert_grads = [], [], [], [None], [], []
    for i in range(jobs + 2):
        outs, parts, more = [], [], [None, None]
        if here.square:
            ahead = here.rows_first(width) if i <= jobs else 0
            if i > 1:
                line = ahead + near_last[0].shape[0] if i > 1 else 0
            columns = small[0].shape[1] // 2 if small[0] is not None else 0
            if i in (3, 4):
                came = ins[i == 4][line:].reshape(small[0].shape)
                small = [small[0] + came.astype(jnp.float32)]
            if i in (2, 3):
                more[i == 3] = small[0][:, columns:].astype(bfloat).reshape(-1, width // 2)
                small = [small[0][:, :columns]]
            if i > 1:
                pieces_small = []
                if i == 4:
                    pieces_small = [
                        piece.reshape(-1, width).astype(jnp.float32 if p == 0 else bfloat)
                        for p, piece in enumerate(jnp.split(small[0], here.nz, axis=1))
                    ]
                parts = list(line_fold(ins, ahead, near_last, here.nz, pieces_small))
            if i == 0:
                outs = far
            elif i <= jobs:
                *outs, keep_x, keep_y = fold(ins, near, far if i < jobs else [], more)
                near_last = [keep_x, keep_y]
        else:
            outs = far if i < jobs else []
        if not here.square and 0 < i <= jobs:
            parts = here.line_parts(ins)
        sending_y = []
        if adds_y:
            collect_y.land(moving)
            sending_y = collect_y.add(adds_y[0], parts_y[adds_y.pop(0)])
        (
            outs, parts, sending_y, near_last, small, rights, smalls, grads, back_y, rows_in, grad_in_norm
        ) = tie(
            outs, parts, sending_y, near_last, small, rights, smalls, grads, back_y, rows_in, grad_in_norm
        )
        ins = arrive(outs) if outs else []
        if parts:
            parts = here.along_whole_line(parts)
        moving = collect_y.send(sending_y) if sending_y else []
        if here.square and i == 5:
            smalls = here.to_cores(smalls)
        if i < jobs:
            near = here.scatter_near(*lefts[i], rights[i])
        if i == 0:
            others = [here.other_core(grads, step) for step in range(1, here.cores)]
        if i + 1 < jobs:
            rights.append(jnp.concatenate([v[i] for v in [grads, *others]], axis=0))
        if i + 1 < jobs:
            far = here.scatter_far(*lefts[i + 1], rights[i + 1])
        if i == 0:
            grads, others = tie(grads, others)
            grad_in_norm = times_transposed(grads, pieces, 0, 3)
        if i == 1:
            grad_tokens, grad_gain_in = input_gradient(
                grad_in_norm, sources, tokens, inverse_one, gains_f[:1], grad_residual
            )
            small_rows = 4 + experts
            smalls = jnp.concatenate(
                [
                    grad_gain_in[:1],
                    grad_gain_heads[:2],
                    grad_gain_mid[None],
                    grad_router.T,
                    jnp.zeros((-small_rows % 32, width), jnp.float32),
                ],
                axis=0,
            )
            if here.square:
                smalls = jnp.concatenate(here.core_columns(smalls), axis=0)
                small = [product(smalls.astype(bfloat), order_x)]
            grad_tokens, small, smalls, ins = tie(grad_tokens, small, smalls, ins)
        if i == 0 and len(late) > 2:
            add_up_y(late[2])
        if 2 <= i <= 3:
            grad = rows_product(rows_in, [kept[i] for kept in backward])
            expert_grads.append(grad)
            ins, expert_grads = tie(ins, expert_grads)
        if i == 3:
            mixed = (residual + collect_y.total).astype(bfloat)
            mixed, ins = tie(mixed, ins)
        ins, parts, moving, far, near, rights, smalls, parts_y, grad_in_norm, others = tie(
            ins, parts, moving, far, near, rights, smalls, parts_y, grad_in_norm, others
        )
        if parts:
            share = sum(part.astype(jnp.float32) for part in parts)
            if here.square and i == 4:
                smalls = jnp.split(share[shard:].reshape(-1, shard), here.cores, axis=0)
            shares.append(share[:shard])
    if here.square:
        smalls = sum(smalls)
    else:
        smalls = lax.psum(smalls, ("dp", "expert"))
        smalls = lax.dynamic_slice(
            smalls, (0, (here.core * here.count + here.me) * shard), (smalls.shape[0], shard)
        )
    grad_wo, grad_wv, grad_wk, grad_wq = shares
    grad_gate_w, grad_up_w = expert_grads
    return (
        mixed,
        grad_tokens,
        smalls[:4],
        grad_wq,
        grad_wk,
        grad_wv,
        grad_wo,
        smalls[4:small_rows].T,
        grad_gate_w[None, None],
        grad_up_w[None, None],
        grad_down[None, None],
    )


def solution(mesh):
    return jax.shard_map(
        on_device,
        mesh=mesh,
        in_specs=(
            P(("dp", "expert"), None),
            P(("dp", "expert"), None),
            P(("dp", "expert"), None),
            P(None, ("dp", "expert")),
            P(("dp", "expert"), None),
            P(("dp", "expert"), None),
            P(("dp", "expert"), None),
            P(("dp", "expert"), None),
            P(("dp", "expert"), None),
            P("expert", None, None),
            P("expert", None, None),
            P("expert", None, None),
            P(("dp", "expert"), None),
        ),
        out_specs=(
            P(("dp", "expert"), None),
            P(("dp", "expert"), None),
            P(None, ("dp", "expert")),
            P(("dp", "expert"), None),
            P(("dp", "expert"), None),
            P(("dp", "expert"), None),
            P(("dp", "expert"), None),
            P(("dp", "expert"), None),
            P("dp", "expert", None, None),
            P("dp", "expert", None, None),
            P("dp", "expert", None, None),
        ),
        check_vma=False,
    )
```

```python
import jax
import jax.numpy as jnp
from jax import lax
from jax.experimental import pallas as pl
from jax.experimental.pallas import tpu as pltpu
from jax.sharding import PartitionSpec as P

HD = 128


EPS = 1e-05
THETA = 10000.0
MASKED = -1e30
LANES = 128


def norm_rows(value, gain):
    inverse = lax.rsqrt(jnp.mean(value * value, axis=-1, keepdims=True) + EPS)
    normed = value * inverse
    return (normed * gain, normed, inverse)


def norm_back(grad_in, gain, normed, inverse):
    grad_normed = grad_in * gain
    grad_gain = jnp.sum(grad_in * normed, axis=0)
    inner = jnp.mean(grad_normed * normed, axis=-1, keepdims=True)
    return (inverse * (grad_normed - normed * inner), grad_gain)


def contract_rows(left, right):
    return lax.dot_general(
        left, right, (((0,), (0,)), ((), ())), preferred_element_type=jnp.float32
    )


def contract_cols(left, right):
    return lax.dot_general(
        left, right, (((1,), (1,)), ((), ())), preferred_element_type=jnp.float32
    )


def product(left, right):
    return jnp.dot(left, right, preferred_element_type=jnp.float32)


def tie(*values):
    return lax.optimization_barrier(values)


class Spread:
    def __init__(self, here, own):
        self.here, self.queue, self.done = here, [own], 0

    def step(self):
        here, own = self.here, self.queue[0]
        self.done += 1
        if self.done >= here.nz:
            return []
        if here.nz != 4:
            moves = [(a, (a + self.done) % here.nz) for a in range(here.nz)]
            return [here.along_line(own, moves)]
        if self.done == 1:
            return [
                here.along_line(own, [(0, 1), (1, 0), (2, 3), (3, 2)]),
                here.along_line(own, [(1, 2), (2, 1)]),
            ]
        if self.done == 2:
            return [
                here.along_line(self.middle, [(1, 0), (2, 3)]),
                here.along_line(self.queue[1], [(1, 2), (2, 1)]),
            ]
        return [here.along_line(self.across, [(1, 0), (2, 3)])]

    def land(self, arrays):
        here = self.here
        if not arrays:
            return
        if here.nz != 4:
            self.queue += arrays
            return
        inner = (here.z == 1) | (here.z == 2)
        if self.done == 1:
            one, self.middle = arrays
            self.queue.append(one)
        elif self.done == 2:
            edge, self.across = arrays
            self.queue.append(jnp.where(inner, self.middle, edge))
        else:
            self.queue.append(jnp.where(inner, self.across, arrays[0]))

    def finish(self):
        while len(self.queue) < self.here.nz:
            self.land(self.step())
        return self.queue


class Collect:
    def __init__(self, here):
        self.here, self.came, self.moves = here, [], []

    def add(self, k, part):
        here = self.here
        if k == 0:
            self.total = part
            for value in self.came:
                self.total = self.total + value
            return []
        if here.nz != 4:
            out = [(part, [(a, (a - k) % here.nz) for a in range(here.nz)])]
        elif k == 3:
            self.three = part
            out = [(part, [(0, 1), (3, 2)])]
        elif k == 2:
            self.two = part
            (edge,) = self.came
            out = [(self.three + edge, [(1, 2), (2, 1)]), (part, [(0, 1), (3, 2)])]
        else:
            across, edge = self.came
            out = [
                (part + across, [(0, 1), (1, 0), (2, 3), (3, 2)]),
                (self.two + edge, [(1, 2), (2, 1)]),
            ]
        self.moves = [moves for _, moves in out]
        return [value.astype(jnp.bfloat16) for value, _ in out]

    def send(self, values):
        return [self.here.along_line(v, m) for v, m in zip(values, self.moves, strict=True)]

    def land(self, arrays):
        came = [value.astype(jnp.float32) for value in arrays]
        self.came = came if self.here.nz == 4 else self.came + came
        self.moves = []


def grid_of(count):
    if count % 32 == 0:
        return (count // 16, 4, 4)
    if count % 4 == 0:
        return (count // 4, 2, 2)
    return (count, 1, 1)


class Places:
    def __init__(self):
        self.count = lax.axis_size("expert")
        self.cores = lax.axis_size("dp")
        self.nz, self.ny, self.nx = grid_of(self.count)
        self.plane = self.ny * self.nx
        self.me = lax.axis_index("expert")
        self.core = lax.axis_index("dp")
        self.z = self.me // self.plane
        self.y = (self.me // self.nx) % self.ny
        self.x = self.me % self.nx
        self.steps = [(dy, dx) for dy in range(self.ny) for dx in range(self.nx)]
        self.square = (self.ny, self.nx) == (2, 2)
        if self.nz == 4:
            self.queue = [[0, 1, 2, 3], [1, 0, 2, 3], [2, 3, 1, 0], [3, 2, 1, 0]]
        else:
            self.queue = [[(z - k) % self.nz for k in range(self.nz)] for z in range(self.nz)]

    def at(self, z, y, x):
        return (z * self.ny + y) * self.nx + x

    def shift_plane(self, value, dy, dx):
        pairs = [
            (self.at(z, y, x), self.at(z, (y + dy) % self.ny, (x + dx) % self.nx))
            for z in range(self.nz)
            for y in range(self.ny)
            for x in range(self.nx)
        ]
        return lax.ppermute(value, "expert", pairs)

    def along_line(self, value, moves):
        pairs = [
            (self.at(a, y, x), self.at(b, y, x))
            for a, b in moves
            for y in range(self.ny)
            for x in range(self.nx)
        ]
        return lax.ppermute(value, "expert", pairs)

    def other_core(self, value, step):
        pairs = [(c, (c + step) % self.cores) for c in range(self.cores)]
        return lax.ppermute(value, "dp", pairs)

    def arrival(self, rows):
        shard = rows // (self.cores * self.count)
        order = jnp.arange(rows, dtype=jnp.int32)
        inside, rest = order % shard, order // shard
        step, rest = rest % self.plane, rest // self.plane
        core, k = rest % self.cores, rest // self.cores
        zed = self.queue_of(k)
        y = (self.y - step // self.nx) % self.ny
        x = (self.x - step % self.nx) % self.nx
        core = (self.core - core) % self.cores
        source = (core * self.count + self.at(zed, y, x)) * shard + inside
        return (order[:, None] == source[None, :]).astype(jnp.bfloat16), source[None, :]

    def queue_of(self, k):
        table = jnp.asarray(self.queue, jnp.int32)[self.z]
        zed = jnp.zeros_like(k)
        for q in range(self.nz):
            zed = jnp.where(k == q, table[q], zed)
        return zed

    def deal(self, rows):
        return [
            rows[i] if s == (0, 0) else self.shift_plane(rows[i], *s)
            for i, s in enumerate(self.steps)
        ]

    def deal_back(self, rows):
        return [
            rows[i] if s == (0, 0) else self.shift_plane(rows[i], -s[0], -s[1])
            for i, s in enumerate(self.steps)
        ]

    def along_plane(self, values):
        return [
            v if s == (0, 0) else self.shift_plane(v, *s)
            for v, s in zip(values, self.steps, strict=True)
        ]

    def along_whole_line(self, parts):
        return [
            part
            if k == 0
            else self.along_line(part, [(a, (a + k) % self.nz) for a in range(self.nz)])
            for k, part in enumerate(parts)
        ]

    def target_order(self, width, lead):
        shard = width // self.count
        order = jnp.arange(width, dtype=jnp.int32)
        inside, rest = order % shard, order // shard
        k, rest = rest % self.nz, rest // self.nz
        if lead == "x":
            dy, dx = rest % self.ny, rest // self.ny
        else:
            dx, dy = rest % self.nx, rest // self.nx
        y, x = (self.y + dy) % self.ny, (self.x + dx) % self.nx
        source = self.at((self.z + k) % self.nz, y, x) * shard + inside
        return (order[:, None] == source[None, :]).astype(jnp.bfloat16)

    def scatter_far(self, by_x, by_y, right):
        wire = jnp.bfloat16
        if not self.square:
            line = by_x.shape[1] // self.plane
            starts = [(dx * self.ny + dy) * line for dy, dx in self.steps]
            parts = [contract_rows(by_x[:, start : start + line], right) for start in starts]
            return parts[:1] + [part.astype(wire) for part in parts[1:]]
        half, far = right.shape[1] // 2, by_x.shape[1] // 2
        return [
            contract_rows(by_x[:, far:], right[:, :half]).astype(wire),
            contract_rows(by_y[:, far:], right[:, half:]).astype(wire),
        ]

    def scatter_near(self, by_x, by_y, right):
        if not self.square:
            return []
        half, far = right.shape[1] // 2, by_x.shape[1] // 2
        return [
            contract_rows(by_x[:, :far], right[:, :half]),
            contract_rows(by_y[:, :far], right[:, half:]),
        ]

    def rows_first(self, width):
        return width // self.cores // self.nx

    def line_parts(self, terms):
        total = sum(t.astype(jnp.float32) for t in terms)
        shard = total.shape[0] // self.nz
        parts = [total[k * shard : (k + 1) * shard] for k in range(self.nz)]
        return parts[:1] + [part.astype(jnp.bfloat16) for part in parts[1:]]

    def all_tokens(self, value):
        return jnp.concatenate(
            [value] + [self.other_core(value, step) for step in range(1, self.cores)], axis=0
        )

    def core_columns(self, value):
        width = value.shape[1] // self.cores
        starts = [((self.core + step) % self.cores) * width for step in range(self.cores)]
        return [lax.dynamic_slice(value, (0, start), (value.shape[0], width)) for start in starts]

    def to_cores(self, pieces):
        return [
            piece if step == 0 else self.other_core(piece, step)
            for step, piece in enumerate(pieces)
        ]


COLUMNS = 1024
BESIDE = pl.CostEstimate(flops=1, bytes_accessed=1, transcendentals=0)


def fold(came, near, far, more):
    rows, width = near[0].shape
    line = rows // 2
    ahead = rows if far else 0
    extra = [m.shape[0] if m is not None else 0 for m in more]
    low, full = jnp.bfloat16, jnp.float32

    def body(*refs):
        came_refs, near_refs, refs = refs[:2], refs[2:4], refs[4:]
        far_refs, refs = refs[: len(far)], refs[len(far) :]
        more_refs, (out_x, out_y, keep_x, keep_y) = list(refs[:-4]), refs[-4:]
        sums = [
            n[...] + c[:rows, :].astype(full) for n, c in zip(near_refs, came_refs, strict=True)
        ]
        keep_x[...], keep_y[...] = sums[0][:line], sums[1][:line]
        out_x[ahead : ahead + line, :] = sums[1][line:].astype(low)
        out_y[ahead : ahead + line, :] = sums[0][line:].astype(low)
        for out, far_ref in zip((out_x, out_y), far_refs, strict=False):
            out[:ahead, :] = far_ref[...]
        for out, count in zip((out_x, out_y), extra, strict=True):
            if count:
                out[ahead + line :, :] = more_refs.pop(0)[...]

    outs = [ahead + line + extra[0], ahead + line + extra[1], line, line]
    return pl.pallas_call(
        body,
        out_shape=[
            jax.ShapeDtypeStruct((count, width), dtype)
            for count, dtype in zip(outs, (low, low, full, full), strict=True)
        ],
        compiler_params=pltpu.CompilerParams(vmem_limit_bytes=40 << 20),
        cost_estimate=BESIDE,
    )(*came, *near, *far, *[m for m in more if m is not None])


def line_fold(came, at, keep, count, more):
    line, width = keep[0].shape
    each = line // count
    full = jnp.float32

    def body(came_x, came_y, keep_x, keep_y, *refs):
        for p, out in enumerate(refs[-count:]):
            rows = slice(p * each, (p + 1) * each)
            out[:each, :width] = (keep_x[rows, :] + came_y[rows, :].astype(full)).astype(out.dtype)
            out[:each, width:] = (keep_y[rows, :] + came_x[rows, :].astype(full)).astype(out.dtype)
            if more:
                out[each:, :] = refs[p][...]

    def whole(shape):
        return pl.BlockSpec(shape, lambda i: (0, 0))

    shape = (each + (more[0].shape[0] if more else 0), 2 * width)
    return pl.pallas_call(
        body,
        grid=(1,),
        in_specs=[pl.BlockSpec((line, width), lambda i: (at // line, 0))] * 2
        + [whole(value.shape) for value in (*keep, *more)],
        out_specs=[whole(shape)] * count,
        out_shape=[
            jax.ShapeDtypeStruct(shape, full if p == 0 else jnp.bfloat16) for p in range(count)
        ],
        compiler_params=pltpu.CompilerParams(vmem_limit_bytes=40 << 20),
        cost_estimate=BESIDE,
    )(*came, *keep, *more)


def times_gathered(left, pieces, start, stop, so_far=None):
    plane, _, shard, width = pieces[0].shape
    rows, tiles = plane * shard, width // COLUMNS

    def body(left_ref, *refs):
        *piece_refs, out_ref = refs
        total = None if so_far is None else piece_refs.pop()[...]
        for i, piece_ref in enumerate(piece_refs):
            part = left_ref[:, i * rows : (i + 1) * rows]
            term = jnp.dot(
                part, piece_ref[...].reshape(rows, COLUMNS), preferred_element_type=jnp.float32
            )
            total = term if total is None else total + term
        out_ref[...] = total

    depth = (stop - start) * width
    out_spec = pl.BlockSpec((left.shape[0], COLUMNS), lambda w, j: (0, w * tiles + j))
    piece_spec = pl.BlockSpec((plane, 1, shard, COLUMNS), lambda w, j: (0, w + start, 0, j))
    return pl.pallas_call(
        body,
        grid=(stop - start, tiles),
        in_specs=[pl.BlockSpec(left.shape, lambda w, j: (0, 0))]
        + [piece_spec] * len(pieces)
        + [out_spec] * (so_far is not None),
        out_specs=out_spec,
        out_shape=jax.ShapeDtypeStruct((left.shape[0], depth), jnp.float32),
        compiler_params=pltpu.CompilerParams(vmem_limit_bytes=40 << 20),
        cost_estimate=BESIDE,
    )(left, *pieces, *([] if so_far is None else [so_far]))


def times_transposed(left, pieces, start, stop):
    plane, _, shard, width = pieces[0].shape
    rows, tiles = plane * shard, width // COLUMNS
    out_shape = (left.shape[1], rows * len(pieces))

    def body(left_ref, *refs):
        *piece_refs, out_ref = refs

        @pl.when((pl.program_id(0) == 0) & (pl.program_id(1) == 0))
        def _():
            out_ref[...] = jnp.zeros_like(out_ref)

        for i, piece_ref in enumerate(piece_refs):
            out_ref[:, i * rows : (i + 1) * rows] += lax.dot_general(
                left_ref[0],
                piece_ref[...].reshape(rows, COLUMNS),
                (((1,), (1,)), ((), ())),
                preferred_element_type=jnp.float32,
            )

    piece_spec = pl.BlockSpec((plane, 1, shard, COLUMNS), lambda w, j: (0, w + start, 0, j))
    return pl.pallas_call(
        body,
        grid=(stop - start, tiles),
        in_specs=[pl.BlockSpec((1, left.shape[1], COLUMNS), lambda w, j: (left.shape[0] - 1 - w, 0, j))]
        + [piece_spec] * len(pieces),
        out_specs=pl.BlockSpec(out_shape, lambda w, j: (0, 0)),
        out_shape=jax.ShapeDtypeStruct(out_shape, jnp.float32),
        compiler_params=pltpu.CompilerParams(vmem_limit_bytes=40 << 20),
        cost_estimate=BESIDE,
    )(left, *pieces)


GROUP = 8


def attention(projected, gains, tables, doc_ids, heads):
    length, width = projected.shape[0], projected.shape[1] // 3
    low, full = jnp.bfloat16, jnp.float32
    scale = HD ** (-0.5)

    def body(raw_ref, gain_ref, cos_ref, sin_ref, row_ref, col_ref,
             query_ref, key_ref, value_ref, out_ref, prob_ref, inv_ref, seen_ref):
        first = pl.program_id(0) * GROUP

        @pl.when(first == 0)
        def _():
            for i in (0, 1):
                raw = raw_ref[:, i * width : (i + 1) * width]
                mean = jnp.mean(raw * raw, axis=-1, keepdims=True)
                inv_ref[:, i : i + 1] = lax.rsqrt(mean + EPS)
            at = lax.broadcasted_iota(jnp.int32, (length, length), 0)
            to = lax.broadcasted_iota(jnp.int32, (length, length), 1)
            seen = (row_ref[...] == col_ref[...]) & (at >= to)
            seen_ref[...] = jnp.where(seen, 1.0, 0.0)

        def turned(i, head):
            raw = raw_ref[:, pl.ds(pl.multiple_of(i * width + head * HD, HD), HD)]
            gain = gain_ref[i + 1 : i + 2, pl.ds(pl.multiple_of(head * HD, HD), HD)]
            value = raw * inv_ref[:, i : i + 1] * gain
            return (value * cos_ref[...] + pltpu.roll(value, HD // 2, 1) * sin_ref[...]).astype(low)

        for g in range(GROUP):
            at = slice(g * HD, (g + 1) * HD)
            query, key = turned(0, first + g), turned(1, first + g)
            value_at = pl.multiple_of(2 * width + (first + g) * HD, HD)
            value = raw_ref[:, pl.ds(value_at, HD)].astype(low)
            scores = lax.dot_general(
                query, key, (((1,), (1,)), ((), ())), preferred_element_type=full
            ) * scale
            scores = jnp.where(seen_ref[...] > 0.0, scores, MASKED)
            expo = jnp.exp(scores - jnp.max(scores, axis=-1, keepdims=True))
            probs = expo / jnp.sum(expo, axis=-1, keepdims=True)
            prob_ref[g] = probs
            out = jnp.dot(probs.astype(low), value, preferred_element_type=full)
            out_ref[:, at] = out.astype(low)
            query_ref[:, at], key_ref[:, at], value_ref[:, at] = query, key, value

    def whole(shape):
        return pl.BlockSpec(shape, lambda h: (0,) * len(shape))

    part = pl.BlockSpec((length, GROUP * HD), lambda h: (0, h))
    flat = jax.ShapeDtypeStruct((length, width), low)
    return pl.pallas_call(
        body,
        grid=(heads // GROUP,),
        in_specs=[
            whole(projected.shape), whole(gains.shape), whole((length, HD)), whole((length, HD)),
            whole((length, 1)), whole((1, length)),
        ],
        out_specs=[part, part, part, part,
                   pl.BlockSpec((GROUP, length, length), lambda h: (h, 0, 0)), whole((length, LANES))],
        out_shape=[flat, flat, flat, flat,
                   jax.ShapeDtypeStruct((heads, length, length), full),
                   jax.ShapeDtypeStruct((length, LANES), full)],
        scratch_shapes=[pltpu.VMEM((length, length), full)],
        compiler_params=pltpu.CompilerParams(vmem_limit_bytes=40 << 20),
        cost_estimate=BESIDE,
    )(projected, gains, *tables, doc_ids.reshape(length, 1), doc_ids.reshape(1, length))


def attention_back(grad_out, query, key, value, probs, projected, inverses, gains, tables, heads):
    length, width = grad_out.shape
    low, full = jnp.bfloat16, jnp.float32
    scale = HD ** (-0.5)

    def body(grad_ref, query_ref, key_ref, value_ref, prob_ref, raw_ref, inv_ref, gain_ref,
             cos_ref, sin_ref, out_ref, dgain_ref, turned_ref, inner_ref):
        first = pl.program_id(0) * GROUP

        @pl.when(first == 0)
        def _():
            inner_ref[...] = jnp.zeros_like(inner_ref)

        for g in range(GROUP):
            head, part = first + g, slice(g * HD, (g + 1) * HD)
            here = pl.multiple_of(head * HD, HD)
            grad, probs = grad_ref[:, part], prob_ref[g]
            grad_probs = lax.dot_general(
                grad, value_ref[:, part], (((1,), (1,)), ((), ())), preferred_element_type=full
            )
            out_ref[0, :, pl.ds(here, HD)] = lax.dot_general(
                probs.astype(low), grad, (((0,), (0,)), ((), ())), preferred_element_type=full
            ).astype(low)
            inner = jnp.sum(probs * grad_probs, axis=-1, keepdims=True)
            grad_scores = (probs * (grad_probs - inner)).astype(low)
            rotated = (
                jnp.dot(grad_scores, key_ref[:, part], preferred_element_type=full) * scale,
                lax.dot_general(
                    grad_scores, query_ref[:, part], (((0,), (0,)), ((), ())),
                    preferred_element_type=full,
                ) * scale,
            )
            for i in (0, 1):
                back = rotated[i] * cos_ref[...] - pltpu.roll(rotated[i], HD // 2, 1) * sin_ref[...]
                at = pl.ds(pl.multiple_of(i * width + head * HD, HD), HD)
                turned_ref[:, at] = back
                normed = raw_ref[:, at] * inv_ref[:, i : i + 1]
                dgain_ref[i : i + 1, pl.ds(here, HD)] = jnp.sum(back * normed, axis=0, keepdims=True)
                weighed = back * gain_ref[i + 1 : i + 2, pl.ds(here, HD)]
                inner_ref[:, i : i + 1] += jnp.sum(weighed * normed, axis=-1, keepdims=True)

        @pl.when(first == heads - GROUP)
        def _():
            for i in (0, 1):
                inverse = inv_ref[:, i : i + 1]
                inner = inner_ref[:, i : i + 1] * (1.0 / width)

                @pl.loop(0, heads)
                def _(j):
                    at = pl.ds(pl.multiple_of(i * width + j * HD, HD), HD)
                    there = pl.ds(pl.multiple_of(j * HD, HD), HD)
                    weighed = turned_ref[:, at] * gain_ref[i + 1 : i + 2, there]
                    normed = raw_ref[:, at] * inverse
                    out_ref[2 - i, :, there] = (inverse * (weighed - normed * inner)).astype(low)

    def whole(shape):
        return pl.BlockSpec(shape, lambda h: (0,) * len(shape))

    part = pl.BlockSpec((length, GROUP * HD), lambda h: (0, h))
    return pl.pallas_call(
        body,
        grid=(heads // GROUP,),
        in_specs=[
            part, part, part, part,
            pl.BlockSpec((GROUP, length, length), lambda h: (h, 0, 0)),
            whole((length, 2 * width)), whole(inverses.shape), whole(gains.shape),
            whole((length, HD)), whole((length, HD)),
        ],
        out_specs=[whole((3, length, width)), whole((8, width))],
        out_shape=[
            jax.ShapeDtypeStruct((3, length, width), low), jax.ShapeDtypeStruct((8, width), full)
        ],
        scratch_shapes=[pltpu.VMEM((length, 2 * width), full), pltpu.VMEM((length, LANES), full)],
        compiler_params=pltpu.CompilerParams(vmem_limit_bytes=40 << 20),
        cost_estimate=BESIDE,
    )(grad_out, query, key, value, probs, projected, inverses, gains, *tables)


def expert_back(pieces, grad_y, tail, pre_gate, pre_up, gate_w, up_w, down_w):
    total, width = grad_y.shape
    rows = min(512, total)
    pieces = pieces if rows == total else 1
    hidden = pre_gate.shape[1]
    low, full = jnp.bfloat16, jnp.float32
    tile = min(512, hidden)

    def body(grad_y_ref, tail_ref, a_ref, b_ref, gate_w_ref, up_w_ref, down_w_ref, *refs):
        back_refs, (grad_a_ref, grad_b_ref, sum_ref) = refs[:pieces], refs[pieces:]
        each = rows // pieces
        step = pl.program_id(1)

        @pl.when(step == 0)
        def _():
            for p, back_ref in enumerate(back_refs):
                back_ref[:, width:] = tail_ref[p * each : (p + 1) * each, :]
            sum_ref[...] = jnp.zeros_like(sum_ref)

        grad_act = lax.dot_general(
            grad_y_ref[...], down_w_ref[...], (((1,), (1,)), ((), ())), preferred_element_type=full
        )
        pre_gate, pre_up = a_ref[...], b_ref[...]
        sigmoid_g = jax.nn.sigmoid(pre_gate)
        slope = sigmoid_g * (1.0 + pre_gate * (1.0 - sigmoid_g))
        grad_a = (grad_act * pre_up * slope).astype(low)
        grad_b = (grad_act * (pre_gate * sigmoid_g)).astype(low)
        grad_a_ref[...], grad_b_ref[...] = grad_a, grad_b
        contract = (((1,), (1,)), ((), ()))
        sum_ref[...] += lax.dot_general(
            grad_a, gate_w_ref[...], contract, preferred_element_type=full
        ) + lax.dot_general(grad_b, up_w_ref[...], contract, preferred_element_type=full)

        @pl.when(step == hidden // tile - 1)
        def _():
            for p, back_ref in enumerate(back_refs):
                back_ref[:, :width] = sum_ref[p * each : (p + 1) * each, :].astype(low)

    def whole(columns):
        return pl.BlockSpec((rows, columns), lambda r, f: (r, 0))

    inner = pl.BlockSpec((rows, tile), lambda r, f: (r, f))
    into = pl.BlockSpec((width, tile), lambda r, f: (0, f))
    outs = pl.pallas_call(
        body,
        grid=(total // rows, hidden // tile),
        in_specs=[
            whole(width), whole(LANES), inner, inner, into, into,
            pl.BlockSpec((tile, width), lambda r, f: (f, 0)),
        ],
        out_specs=[pl.BlockSpec((rows // pieces, width + LANES), lambda r, f: (r, 0))] * pieces
        + [inner, inner],
        out_shape=[jax.ShapeDtypeStruct((total // pieces, width + LANES), low)] * pieces
        + [jax.ShapeDtypeStruct(pre_gate.shape, low)] * 2,
        scratch_shapes=[pltpu.VMEM((rows, width), full)],
        compiler_params=pltpu.CompilerParams(vmem_limit_bytes=52 << 20),
        cost_estimate=BESIDE,
    )(grad_y, tail, pre_gate, pre_up, gate_w, up_w, down_w)
    return (outs[:pieces], *outs[pieces:])


def rows_product(lefts, rights):
    rows, height = lefts[0].shape
    width = rights[0].shape[1]
    tile = min(512, height)

    def body(*refs):
        out_ref = refs[-1]
        total = None
        for left_ref, right_ref in zip(refs[: len(lefts)], refs[len(lefts) : -1], strict=True):
            term = lax.dot_general(
                left_ref[...], right_ref[...], (((0,), (0,)), ((), ())),
                preferred_element_type=jnp.float32,
            )
            total = term if total is None else total + term
        out_ref[...] = total

    return pl.pallas_call(
        body,
        grid=(height // tile,),
        in_specs=[pl.BlockSpec((rows, tile), lambda i: (0, i))] * len(lefts)
        + [pl.BlockSpec((rows, width), lambda i: (0, 0))] * len(rights),
        out_specs=pl.BlockSpec((tile, width), lambda i: (i, 0)),
        out_shape=jax.ShapeDtypeStruct((height, width), jnp.float32),
        compiler_params=pltpu.CompilerParams(vmem_limit_bytes=52 << 20),
        cost_estimate=BESIDE,
    )(*lefts, *rights)


def input_gradient(grad, sources, tokens, inverse, gain, residual):
    length, width = grad.shape
    tile = 512
    low, full = jnp.bfloat16, jnp.float32

    def body(grad_ref, source_ref, token_ref, inverse_ref, gain_ref, residual_ref,
             out_ref, dgain_ref, split_ref, placed_ref, inner_ref):
        step = pl.program_id(0)

        @pl.when(step == 0)
        def _():
            high = grad_ref[...].astype(low)
            split_ref[:length, :] = high
            split_ref[length:, :] = (grad_ref[...] - high.astype(full)).astype(low)
            inner_ref[...] = jnp.zeros_like(inner_ref)

        at = pl.ds(pl.multiple_of(step * tile, tile), tile)
        column = step * tile + lax.broadcasted_iota(jnp.int32, (tile, width), 0)
        arrival = jnp.where(column == source_ref[...], 1.0, 0.0).astype(low)
        placed = lax.dot_general(
            split_ref[...], arrival, (((1,), (1,)), ((), ())), preferred_element_type=full
        )
        placed = placed[:length] + placed[length:]
        placed_ref[:, at] = placed
        normed = token_ref[:, at].astype(full) * inverse_ref[...]
        dgain_ref[:, at] = jnp.broadcast_to(
            jnp.sum(placed * normed, axis=0, keepdims=True), (dgain_ref.shape[0], tile)
        )
        weighed = placed * gain_ref[:, at]
        inner_ref[:, :1] += jnp.sum(weighed * normed, axis=-1, keepdims=True)

        @pl.when(step == width // tile - 1)
        def _():
            inner = inner_ref[:, :1] * (1.0 / width)
            inverse = inverse_ref[...]

            @pl.loop(0, width // tile)
            def _(j):
                at = pl.ds(pl.multiple_of(j * tile, tile), tile)
                normed = token_ref[:, at].astype(full) * inverse
                back = inverse * (placed_ref[:, at] * gain_ref[:, at] - normed * inner)
                out_ref[:, at] = (residual_ref[:, at] + back).astype(low)

    def whole(shape):
        return pl.BlockSpec(shape, lambda j: (0,) * len(shape))

    return pl.pallas_call(
        body,
        grid=(width // tile,),
        in_specs=[
            whole(grad.shape), whole(sources.shape), whole(tokens.shape),
            whole(inverse.shape), whole(gain.shape), whole(residual.shape),
        ],
        out_specs=[whole(tokens.shape), whole((8, width))],
        out_shape=[
            jax.ShapeDtypeStruct(tokens.shape, low), jax.ShapeDtypeStruct((8, width), full)
        ],
        scratch_shapes=[
            pltpu.VMEM((2 * length, width), low),
            pltpu.VMEM((length, width), full),
            pltpu.VMEM((length, LANES), full),
        ],
        compiler_params=pltpu.CompilerParams(vmem_limit_bytes=40 << 20),
        cost_estimate=BESIDE,
    )(grad, sources, tokens, inverse, gain, residual)


def rope_tables(length):
    half = HD // 2
    freq = THETA ** (-(jnp.arange(half, dtype=jnp.float32) * 2.0) / HD)
    angle = jnp.arange(length, dtype=jnp.float32)[:, None] * freq[None, :]
    sine = jnp.sin(angle)
    cosine = jnp.cos(angle)
    return (
        jnp.concatenate([cosine, cosine], axis=-1),
        jnp.concatenate([-sine, sine], axis=-1),
    )


def on_device(
    tokens,
    segments,
    expert_ids,
    norm_gains,
    w_query,
    w_key,
    w_value,
    w_out,
    w_router,
    expert_gate,
    expert_up,
    expert_down,
    cotangent,
):
    bfloat = jnp.bfloat16
    here = Places()
    length, width = tokens.shape
    topk = expert_ids.shape[1]
    experts = here.count
    capacity = length * topk // experts
    heads = width // HD
    shard = w_query.shape[0]
    plane = here.plane
    gate_w, up_w, down_w = expert_gate[0], expert_up[0], expert_down[0]

    labels = jnp.arange(experts, dtype=jnp.int32)
    named = jnp.any(expert_ids[:, :, None] == labels[None, None, :], axis=1)
    places = jnp.arange(length, dtype=jnp.int32)
    earlier = (places[:, None] < places[None, :]).astype(bfloat)
    slots = contract_rows(named.astype(bfloat), earlier)
    slots = jnp.where(named.T & (slots < capacity), slots, -1.0).astype(bfloat)

    order = range(here.nz)
    arrival, sources = here.arrival(width)
    extra = norm_gains.shape[0] + w_router.shape[1]
    smalls = jnp.concatenate(
        [norm_gains.T, w_router, jnp.zeros((shard, -extra % LANES), jnp.float32)], axis=1
    ).astype(bfloat)
    smalls = jnp.concatenate([smalls, slots.reshape(-1, LANES)], axis=0)
    smalls = here.along_whole_line([smalls] * here.nz)
    plane_expert = jnp.stack(
        [
            here.at(here.z, (here.y + dy) % here.ny, (here.x + dx) % here.nx)
            for dy, dx in here.steps
        ]
    )
    chosen = plane_expert[:, None] == labels[None, :]
    slot_ids = jnp.arange(capacity, dtype=jnp.int32)
    spreads = []

    def spread_of(part):
        picked = jnp.sum(
            jnp.where(chosen[:, :, None], part[None].astype(jnp.float32), 0.0), axis=1
        ).astype(jnp.int32)
        hit = picked[:, None, :] == slot_ids[None, :, None]
        return hit.astype(bfloat).reshape(plane * capacity, length)

    def rows_of(spread, part):
        return list(product(spread, part).astype(bfloat).reshape(plane, capacity, -1))

    def parted(rows):
        return list(rows.reshape(plane, capacity, -1))

    def joined(rows):
        return jnp.concatenate(rows, axis=0)

    inputs = tokens.astype(jnp.float32)
    weights = jnp.stack([w_query, w_key, w_value, w_out]).astype(bfloat)
    line, cot_line = Spread(here, weights), Spread(here, cotangent)
    half = weights.shape[0] // 2
    raw, chunks, pieces = [], [], []
    projected = None
    depth = width // here.nz
    cot_rows, rows_cot = [None] * here.nz, [None] * here.nz

    def stacked(rows):
        return rows.reshape(-1, shard, width)

    def chunk_of(k):
        if here.square:
            at = 2 * half if k + 1 < here.nz else 0
            blocks = [line.queue[k]] + [by[: 2 * half] for by in raw[k][:2]]
            blocks += [by[at : at + half] for by in raw[k + 1][:2]]
        else:
            blocks = raw[k]
        return jnp.concatenate(blocks, axis=0).reshape(plane, *weights.shape)

    def share(chunk):
        return [chunk] + [here.other_core(chunk, s) for s in range(1, here.cores)]

    def project(k):
        return times_gathered(
            in_order[:, k * depth : (k + 1) * depth], pieces[k], 0, 3, projected
        )

    for k in range(here.nz + 2):
        outs = []
        if here.square:
            by_x, by_y = [], []
            if k < here.nz:
                by_x.append(line.queue[k])
                by_y.append(line.queue[k])
            if 0 < k <= here.nz:
                by_x.append(raw[k - 1][1][:half])
                by_y.append(raw[k - 1][0][half : 2 * half])
            if k >= here.nz:
                by_x.append(stacked(cot_rows[k - here.nz][1]))
                by_y.append(stacked(cot_rows[k - here.nz][2]))
            outs = [jnp.concatenate(by_x, axis=0), jnp.concatenate(by_y, axis=0)]
            if k > here.nz:
                outs.append(jnp.concatenate([cot_rows[0][3], cot_rows[1][3]], axis=0))
        elif k < here.nz:
            outs = [line.queue[k]] * plane
        else:
            outs = cot_rows[k - here.nz]
        if k == 1:
            outs, smalls, raw, line.queue = tie(outs, smalls, raw, line.queue)
            turned = jnp.stack(smalls).reshape(here.nz, -1)
            near = (here.z - here.queue_of(jnp.arange(here.nz))) % here.nz
            pick = (near[:, None] == jnp.arange(here.nz)[None, :]).astype(bfloat)
            turned = product(pick, turned).astype(bfloat).reshape(here.nz, -1, LANES)
            smalls, slots = turned[:, :shard], turned[:, shard:]
            smalls = here.along_plane([smalls] * plane)
        outs, smalls, slots, raw, chunks, line.queue, cot_line.queue, cot_rows, cotangent = tie(
            outs, smalls, slots, raw, chunks, line.queue, cot_line.queue, cot_rows, cotangent
        )
        if here.square:
            ins = [here.shift_plane(outs[0], 0, 1), here.shift_plane(outs[1], 1, 0)]
            if k > here.nz:
                ins.append(here.shift_plane(outs[2], 1, 1))
        else:
            ins = here.along_plane(outs)
        moving = line.step() if k < here.nz else []
        moving_cot = cot_line.step() if k >= here.nz - 1 else []
        if k == 1:
            spreads = [spread_of(part.reshape(experts, length)) for part in slots]
        if k > 2:
            pieces.append(share(chunks[k - 3]))
        if k > 1:
            chunks.append(chunk_of(k - 2))
        if k == 1:
            smalls = jnp.stack(smalls, axis=1)
            smalls = [smalls] + [here.other_core(smalls, s) for s in range(1, here.cores)]
            smalls = jnp.stack(smalls, axis=1).reshape(width, -1)
            smalls = product(arrival, smalls).astype(bfloat)
            smalls, sources = tie(smalls, sources)
        if k == 3:
            gains_f = smalls[:, : norm_gains.shape[0]].T.astype(jnp.float32)
            wr = smalls[:, norm_gains.shape[0] : extra]
            normed_in_f, normed_one, inverse_one = norm_rows(inputs, gains_f[0])
            normed_in = normed_in_f.astype(bfloat)
            in_order = product(normed_in, arrival).astype(bfloat)
        if k > 2:
            projected = project(k - 3)
        if k >= here.nz - 1 and k - here.nz + 1 < here.nz:
            at = k - here.nz + 1
            cot_rows[at] = rows_of(spreads[at], cot_line.queue[at])
        ins, moving, moving_cot, smalls, projected, cot_rows, spreads, chunks = tie(
            ins, moving, moving_cot, smalls, projected, cot_rows, spreads, chunks
        )
        line.land(moving)
        cot_line.land(moving_cot)
        raw.append(ins)
        if k >= here.nz:
            rows_cot[k - here.nz] = ins
            if here.square:
                own = cot_rows[k - here.nz][0]
                skip = half if k == here.nz else 0
                rows_cot[k - here.nz] = [own] + [by[skip:].reshape(own.shape) for by in ins[:2]]
            if here.square and k > here.nz:
                for i in (0, 1):
                    rows_cot[i].append(ins[2][i * capacity : (i + 1) * capacity])

    order_x = here.target_order(width // here.cores, "x")
    order_y = here.target_order(width // here.cores, "y")

    def targeted(columns):
        columns = jnp.concatenate(columns, axis=0)
        return [product(columns, o).astype(bfloat) for o in (order_x, order_y)]

    merged = []
    if here.nz > 2:
        cot_rows[3] = rows_of(spreads[3], cot_line.queue[3])
        merged = [joined(pair) for pair in zip(*cot_rows[2:], strict=True)]
    in_columns = here.core_columns(normed_in)
    merged, chunks, projected, pieces, in_columns = tie(
        merged, chunks, projected, pieces, in_columns
    )
    ins = here.along_plane(merged) if merged else []
    pieces.append(share(chunks[-1]))
    in_columns = here.to_cores(in_columns)
    projected = project(here.nz - 1)
    pieces = [piece for chunk in pieces for piece in chunk]
    tables = rope_tables(length)
    query_rot, key_rot, values, attended, probs, inverses = attention(
        projected, gains_f, tables, segments[0], heads
    )
    residual = inputs + times_gathered(product(attended, arrival).astype(bfloat), pieces, 3, 4)
    normed_mid_f, normed_two, inverse_two = norm_rows(residual, gains_f[3])
    normed_mid = normed_mid_f.astype(bfloat)

    own_label = labels[None, :] == here.me

    def expert_forward(arrived, cot):
        route_here = jax.nn.softmax(product(arrived, wr), axis=-1)
        gate = jnp.sum(jnp.where(own_label, route_here, 0.0), axis=-1)
        gate = gate.astype(bfloat).astype(jnp.float32)[:, None]
        pre_gate = product(arrived, gate_w)
        pre_up = product(arrived, up_w)
        activated = (jax.nn.silu(pre_gate) * pre_up).astype(bfloat)
        result = product(activated, down_w).astype(bfloat).astype(jnp.float32)
        gated = (gate * result).astype(bfloat)
        cot = cot.astype(jnp.float32)
        grad_y = (gate * cot).astype(bfloat)
        grad_g = jnp.sum(cot * result, axis=-1, keepdims=True)
        high = grad_g.astype(bfloat)
        low = (grad_g - high.astype(jnp.float32)).astype(bfloat)
        lanes = jnp.arange(LANES, dtype=jnp.int32)[None, :]
        tail = jnp.where(lanes == here.me, high, jnp.zeros((), bfloat))
        tail = jnp.where(lanes == here.me + LANES // 2, low, tail)
        return (pre_gate, pre_up, activated, gated, grad_y, tail)

    def expert_backward(kept):
        pre_gate, pre_up, _, _, grad_y, tail = kept
        back, grad_a, grad_b = expert_back(
            plane, grad_y, tail, pre_gate, pre_up, gate_w, up_w, down_w
        )
        return [back if len(back) == plane else parted(back[0]), grad_y, grad_a, grad_b]

    rows_next = rows_of(spreads[0], normed_mid)
    out_columns = here.core_columns(attended)
    normed_mid, rows_next, ins, in_columns, out_columns = tie(
        normed_mid, rows_next, ins, in_columns, out_columns
    )
    if here.nz > 2:
        rows_cot[2:] = [[row[i : i + capacity] for row in ins] for i in (0, capacity)]
    line = Spread(here, normed_mid)
    rows_in, forward = [], []
    for k in order:
        if k > 0:
            rows_next = rows_of(spreads[k], line.queue[k])
        rows_next, rows_in, line.queue, out_columns = tie(
            rows_next, rows_in, line.queue, out_columns
        )
        moving = line.step()
        rows = here.along_plane(rows_next)
        if k > 0:
            rows_in[-1] = joined(rows_in[-1])
            forward.append(expert_forward(rows_in[-1], joined(rows_cot[k - 1])))
        if k == 0:
            targets = targeted(in_columns)
            rows, targets = tie(rows, targets)
        if k == here.nz // 2:
            out_columns = here.to_cores(out_columns)
        if k == here.nz - 1:
            out_columns = targeted(out_columns)
            rows_cot[k] = joined(rows_cot[k])
            rows, rows_cot[k] = tie(rows, rows_cot[k])
        moving, rows, forward, out_columns = tie(moving, rows, forward, out_columns)
        rows_in.append(rows)
        line.land(moving)

    targets_out = out_columns
    half = here.nz // 2
    back_y = [None] * here.nz
    backward = [None] * here.nz
    todo = ["forward", *reversed(order)]

    def work():
        k = todo.pop(0) if todo else None
        if k == "forward":
            rows_in[-1] = joined(rows_in[-1])
            forward.append(expert_forward(rows_in[-1], rows_cot[-1]))
        elif k is not None:
            backward[k] = expert_backward(forward[k])

    rows_next = parted(forward[0][3])
    rows_next, forward, rows_in, rows_cot, out_columns = tie(
        rows_next, forward, rows_in, rows_cot, out_columns
    )
    rows = here.deal_back(rows_next)
    work()
    work()
    rows, forward, backward = tie(rows, forward, backward)
    back_y[0] = rows
    collect, parts = Collect(here), [None] * here.nz
    moving, sending, back = [], [], None
    for k in reversed(order):
        rows_next = backward[k][0]
        if k + 2 < here.nz:
            collect.land(moving)
            sending = collect.add(k + 2, parts[k + 2])
        rows_next, sending, forward, backward = tie(rows_next, sending, forward, backward)
        rows = here.deal_back(rows_next)
        moving = collect.send(sending)
        if k > 0:
            work()
        else:
            grad_down = rows_product(
                [kept[2] for kept in forward], [kept[1] for kept in backward]
            )
            rows, grad_down = tie(rows, grad_down)
        if back is not None:
            parts[k + 1] = contract_rows(spreads[k + 1], joined(back))
        moving, rows[:-1], forward, backward, parts = tie(
            moving, rows[:-1], forward, backward, parts
        )
        back = rows
    late = list(order[:0:-1])
    collect.land(moving)
    sending = collect.add(1, parts[1])
    rows_next = parted(forward[late[0]][3])
    rows_next, sending, back_y = tie(rows_next, sending, back_y)
    rows = here.deal_back(rows_next)
    moving = collect.send(sending)
    parts[0] = contract_rows(spreads[0], joined(back))
    part_y = contract_rows(spreads[0], joined(back_y[0]))
    rows_next = [parted(forward[k][3]) for k in late[1:]]
    moving, rows[:-1], parts, rows_next, part_y = tie(
        moving, rows[:-1], parts, rows_next, part_y
    )
    collect.land(moving)
    collect.add(0, parts[0])
    returned = collect.total
    back_y[late[0]] = rows
    parts_y = [None] * here.nz
    parts_y[0] = part_y
    if rows_next:
        back_y[late[1]] = here.deal_back(rows_next[0])

    def add_up_y(k):
        parts_y[k] = contract_rows(spreads[k], joined(back_y[k]))

    add_up_y(late[0])

    grad_mid = returned[:, :width]
    grad_route = (
        returned[:, width : width + experts]
        + returned[:, width + LANES // 2 : width + LANES // 2 + experts]
    )
    route = jax.nn.softmax(product(normed_mid, wr), axis=-1)
    grad_logits = (
        route * (grad_route - jnp.sum(route * grad_route, axis=-1, keepdims=True))
    ).astype(bfloat)
    grad_router = contract_rows(normed_mid, grad_logits)
    grad_mid = grad_mid + contract_cols(grad_logits, wr)
    grad_res_two, grad_gain_mid = norm_back(grad_mid, gains_f[3], normed_two, inverse_two)
    grad_residual = cotangent.astype(jnp.float32) + grad_res_two
    grad_attn = grad_residual.astype(bfloat)
    grad_attended = times_transposed(grad_attn[None], pieces, 3, 4).astype(bfloat)
    grad_attended = contract_cols(grad_attended, arrival).astype(bfloat)
    collect_y, adds_y = Collect(here), list(reversed(order))
    grad_attended, grad_attn, back_y, parts_y = tie(grad_attended, grad_attn, back_y, parts_y)
    sending_y = collect_y.add(adds_y[0], parts_y[adds_y.pop(0)])
    sending_y, grad_attended, grad_attn, back_y, rows_next = tie(
        sending_y, grad_attended, grad_attn, back_y, rows_next
    )
    if rows_next:
        back_y[late[2]] = here.deal_back(rows_next[1])
    moving = collect_y.send(sending_y)
    out_tokens = here.all_tokens(grad_attn)
    grads, grad_gain_heads = attention_back(
        grad_attended, query_rot, key_rot, values, probs, projected, inverses, gains_f, tables, heads
    )
    far = here.scatter_far(*targets_out, out_tokens)
    for k in late[1:2]:
        add_up_y(k)
    grads, far, back_y, parts_y, moving, out_tokens = tie(
        grads, far, back_y, parts_y, moving, out_tokens
    )

    def arrive(outs):
        if not here.square:
            return here.along_plane(outs) if outs else []
        return [here.shift_plane(outs[0], 0, 1), here.shift_plane(outs[1], 1, 0)]

    jobs = 4
    lefts, rights = [targets_out, targets, targets, targets], [out_tokens]
    shares, others, grad_in_norm = [], [], None
    near, near_last, ins, small, smalls, expert_grads = [], [], [], [None], [], []
    for i in range(jobs + 2):
        outs, parts, more = [], [], [None, None]
        if here.square:
            ahead = here.rows_first(width) if i <= jobs else 0
            if i > 1:
                line = ahead + near_last[0].shape[0] if i > 1 else 0
            columns = small[0].shape[1] // 2 if small[0] is not None else 0
            if i in (3, 4):
                came = ins[i == 4][line:].reshape(small[0].shape)
                small = [small[0] + came.astype(jnp.float32)]
            if i in (2, 3):
                more[i == 3] = small[0][:, columns:].astype(bfloat).reshape(-1, width // 2)
                small = [small[0][:, :columns]]
            if i > 1:
                pieces_small = []
                if i == 4:
                    pieces_small = [
                        piece.reshape(-1, width).astype(jnp.float32 if p == 0 else bfloat)
                        for p, piece in enumerate(jnp.split(small[0], here.nz, axis=1))
                    ]
                parts = list(line_fold(ins, ahead, near_last, here.nz, pieces_small))
            if i == 0:
                outs = far
            elif i <= jobs:
                *outs, keep_x, keep_y = fold(ins, near, far if i < jobs else [], more)
                near_last = [keep_x, keep_y]
        else:
            outs = far if i < jobs else []
        if not here.square and 0 < i <= jobs:
            parts = here.line_parts(ins)
        sending_y = []
        if adds_y:
            collect_y.land(moving)
            sending_y = collect_y.add(adds_y[0], parts_y[adds_y.pop(0)])
        (
            outs, parts, sending_y, near_last, small, rights, smalls, grads, back_y, rows_in, grad_in_norm
        ) = tie(
            outs, parts, sending_y, near_last, small, rights, smalls, grads, back_y, rows_in, grad_in_norm
        )
        ins = arrive(outs) if outs else []
        if parts:
            parts = here.along_whole_line(parts)
        moving = collect_y.send(sending_y) if sending_y else []
        if here.square and i == 5:
            smalls = here.to_cores(smalls)
        if i < jobs:
            near = here.scatter_near(*lefts[i], rights[i])
        if i == 0:
            others = [here.other_core(grads, step) for step in range(1, here.cores)]
        if i + 1 < jobs:
            rights.append(jnp.concatenate([v[i] for v in [grads, *others]], axis=0))
        if i + 1 < jobs:
            far = here.scatter_far(*lefts[i + 1], rights[i + 1])
        if i == 0:
            grads, others = tie(grads, others)
            grad_in_norm = times_transposed(grads, pieces, 0, 3)
        if i == 1:
            grad_tokens, grad_gain_in = input_gradient(
                grad_in_norm, sources, tokens, inverse_one, gains_f[:1], grad_residual
            )
            small_rows = 4 + experts
            smalls = jnp.concatenate(
                [
                    grad_gain_in[:1],
                    grad_gain_heads[:2],
                    grad_gain_mid[None],
                    grad_router.T,
                    jnp.zeros((-small_rows % 32, width), jnp.float32),
                ],
                axis=0,
            )
            if here.square:
                smalls = jnp.concatenate(here.core_columns(smalls), axis=0)
                small = [product(smalls.astype(bfloat), order_x)]
            grad_tokens, small, smalls, ins = tie(grad_tokens, small, smalls, ins)
        if i == 0 and len(late) > 2:
            add_up_y(late[2])
        if 2 <= i <= 3:
            grad = rows_product(rows_in, [kept[i] for kept in backward])
            expert_grads.append(grad)
            ins, expert_grads = tie(ins, expert_grads)
        if i == 3:
            mixed = (residual + collect_y.total).astype(bfloat)
            mixed, ins = tie(mixed, ins)
        ins, parts, moving, far, near, rights, smalls, parts_y, grad_in_norm, others = tie(
            ins, parts, moving, far, near, rights, smalls, parts_y, grad_in_norm, others
        )
        if parts:
            share = sum(part.astype(jnp.float32) for part in parts)
            if here.square and i == 4:
                smalls = jnp.split(share[shard:].reshape(-1, shard), here.cores, axis=0)
            shares.append(share[:shard])
    if here.square:
        smalls = sum(smalls)
    else:
        smalls = lax.psum(smalls, ("dp", "expert"))
        smalls = lax.dynamic_slice(
            smalls, (0, (here.core * here.count + here.me) * shard), (smalls.shape[0], shard)
        )
    grad_wo, grad_wv, grad_wk, grad_wq = shares
    grad_gate_w, grad_up_w = expert_grads
    return (
        mixed,
        grad_tokens,
        smalls[:4],
        grad_wq,
        grad_wk,
        grad_wv,
        grad_wo,
        smalls[4:small_rows].T,
        grad_gate_w[None, None],
        grad_up_w[None, None],
        grad_down[None, None],
    )


def solution(mesh):
    return jax.shard_map(
        on_device,
        mesh=mesh,
        in_specs=(
            P(("dp", "expert"), None),
            P(("dp", "expert"), None),
            P(("dp", "expert"), None),
            P(None, ("dp", "expert")),
            P(("dp", "expert"), None),
            P(("dp", "expert"), None),
            P(("dp", "expert"), None),
            P(("dp", "expert"), None),
            P(("dp", "expert"), None),
            P("expert", None, None),
            P("expert", None, None),
            P("expert", None, None),
            P(("dp", "expert"), None),
        ),
        out_specs=(
            P(("dp", "expert"), None),
            P(("dp", "expert"), None),
            P(None, ("dp", "expert")),
            P(("dp", "expert"), None),
            P(("dp", "expert"), None),
            P(("dp", "expert"), None),
            P(("dp", "expert"), None),
            P(("dp", "expert"), None),
            P("dp", "expert", None, None),
            P("dp", "expert", None, None),
            P("dp", "expert", None, None),
        ),
        check_vma=False,
    )
```
